32 devices in a mesh: cheb: 4 (over y, core), wear: 4 (over z), age: 2 (over x).
Axes of the slice: x: 2, y: 2, z: 4, core: 2. Of those that a mesh axis runs over, the one named last changes fastest.
Arguments:
- adjoint_value: float32 [256, 128, 1024], P('wear', 'age', 'cheb'), may hold values from -6 to 6
- load_diffusion: float32 [1024], replicated, may hold values from 0.2 to 1
- load_drift: float32 [1024], replicated, may hold values from -1 to 1
- wear_speed: float32 [1024], P('cheb'), may hold values from 0.05 to 0.3
- hazard: float32 [256, 128], P('wear', 'age'), may hold values from 0.05 to 0.5
Outputs:
- next_value: float32 [256, 128, 1024], P('wear', 'age', 'cheb')
The draws below stay inside these ranges and needn't reach their ends.
All inputs are finite; a program needn't handle non-finite values.
Results may differ from the reference program's by a relative error of at most 0.0037.
Values may be sent and summed in bfloat16 or wider, within the bound.
No kernel may reach another device: no remote copies, remote signals or barrier semaphores. Data moves between devices by JAX's collectives and lax.ppermute only.
A program may use at most 128 MiB of HBM per device.

```python
import math
import jax
import jax.numpy as jnp
from jax import lax

L = 1024
SUBSTEPS = 4
W = 256
A = 128


def block_levels(stream_key, dims, cuts, low, largest):
    loudness = 1.0
    for axis_at, parts in cuts:
        draws = jax.random.uniform(jax.random.fold_in(jax.random.fold_in(stream_key, 6), axis_at), (parts,), jnp.float32, low / len(cuts), largest / len(cuts))
        loudness = loudness * jnp.repeat(jnp.exp(draws), dims[axis_at] // parts).reshape((-1,) + (1,) * (len(dims) - 1 - axis_at))
    return loudness


def bell_draw(key, shape, scale, limit, pieces=(), kind=jnp.bfloat16):
    values = jax.random.normal(key, shape, jnp.float32) * scale
    if len(pieces) > 0:
        values = block_levels(key, shape, pieces, -0.22, 0.18) * values
    return jnp.clip(values, min=-limit, max=limit).astype(kind)


def setup_inputs(seed: int = 0) -> dict:
    key_list = jax.random.split(jax.random.key(seed), 6)
    adjoint_value = bell_draw(key_list[0], (W, A, L), 1.0, 6.0, ((0, 4), (1, 2), (2, 4)), jnp.float32)
    load_diffusion = jnp.clip(jnp.exp(jax.random.uniform(key_list[1], (L,), jnp.float32, math.log(0.2), math.log(1.0))), 0.2, 1.0)
    load_drift = jnp.clip(jax.random.uniform(key_list[2], (L,), jnp.float32, -1.0, 1.0), -1.0, 1.0)
    wear_speed = jnp.clip(0.05 + 0.25 * jax.random.uniform(key_list[3], (L,), jnp.float32) ** block_levels(key_list[3], (L,), ((0, 4),), -0.2, 0.2), 0.05, 0.3)
    hazard = jnp.clip(jnp.exp(math.log(0.5) - 2.3025851 * jax.random.uniform(key_list[4], (W, A), jnp.float32) ** block_levels(key_list[4], (W, A), ((0, 4), (1, 2)), -0.2, 0.2)), 0.05, 0.5)
    return dict(adjoint_value=adjoint_value, load_diffusion=load_diffusion, load_drift=load_drift, wear_speed=wear_speed, hazard=hazard)


age_courant = 0.4
wear_spread = 0.1
coupling = 0.05


def chebyshev_tables(points):
    modes = jnp.arange(points, dtype=jnp.int32)[:, None]
    nodes = jnp.arange(points, dtype=jnp.int32)[None, :]
    phase_index = (modes * (2 * nodes + 1)) % (4 * points)
    angles = phase_index.astype(jnp.float32) * (math.pi / (2 * points))
    cosine = jnp.cos(angles)
    sine_part = jnp.sin(angles)
    weights = jnp.where(modes == 0, 1.0, 2.0).astype(jnp.float32) / points
    wavenumber = modes.astype(jnp.float32) / points
    analysis = (weights * cosine).astype(jnp.bfloat16)
    second_table = (-(wavenumber * wavenumber) * cosine).T.astype(jnp.bfloat16)
    first_table = (wavenumber * sine_part).T.astype(jnp.bfloat16)
    return analysis, second_table, first_table


def advance(padded, wear_speed):
    centre = padded[1:-1, 1:-1]
    older = padded[1:-1, 2:]
    more_worn = padded[2:, 1:-1]
    less_worn = padded[:-2, 1:-1]
    mixed = padded[2:, 2:] - padded[2:, :-2] - padded[:-2, 2:] + padded[:-2, :-2]
    return (centre + age_courant * (older - centre) + wear_speed * (more_worn - centre)
            + wear_spread * (more_worn - 2.0 * centre + less_worn) + coupling * mixed)


def reference(adjoint_value, load_diffusion, load_drift, wear_speed, hazard):
    analysis, second_table, first_table = chebyshev_tables(L)

    def section_row(pair):
        plane, hazard_row = pair
        rounded = plane.astype(jnp.bfloat16)
        coefficients = jnp.dot(rounded, analysis.T, preferred_element_type=jnp.float32).astype(jnp.bfloat16)
        second = jnp.dot(coefficients, second_table.T, preferred_element_type=jnp.float32)
        gradient = jnp.dot(coefficients, first_table.T, preferred_element_type=jnp.float32)
        load_rate = load_diffusion * second + load_drift * gradient
        return plane + load_rate - hazard_row[:, None] * plane

    field = lax.map(section_row, (adjoint_value, hazard))
    for substep in range(SUBSTEPS):
        field = advance(jnp.pad(field, ((1, 1), (1, 1), (0, 0))), wear_speed)
    return field
```

```python
import functools

import jax
import jax.numpy as jnp
import numpy as np
from jax import lax
from jax.experimental import pallas as pl
from jax.experimental.pallas import tpu as pltpu
from jax.sharding import PartitionSpec as P

SUBSTEPS = 4
HALO = SUBSTEPS

age_courant = 0.4
wear_spread = 0.1
coupling = 0.05
GAIN = 1.0 / coupling
START = coupling**SUBSTEPS

f32 = jnp.float32
bf16 = jnp.bfloat16
VMEM_LIMIT = 48 * 2**20


def operators(points):
    modes = np.arange(points)[:, None]
    nodes = np.arange(points)[None, :]
    angles = (modes * (2 * nodes + 1)) % (4 * points) * (np.pi / (2 * points))
    cosine, sine = np.cos(angles), np.sin(angles)
    analysis = np.where(modes == 0, 1.0, 2.0) / points * cosine
    wavenumber = modes / points
    return (-(wavenumber**2) * cosine).T @ analysis, (wavenumber * sine).T @ analysis


@functools.lru_cache(maxsize=None)
def factors(points, devices):
    second, first = operators(points)
    size = points // devices
    parts = [slice(b * size, (b + 1) * size) for b in range(devices)]
    slots, found = [], {}
    for shift in range(1, devices):
        groups = {}
        for c in range(devices):
            b = c ^ shift if devices & (devices - 1) == 0 else (c + shift) % devices
            joint = np.concatenate([second[parts[b], parts[c]], first[parts[b], parts[c]]])
            _, sizes, rows = np.linalg.svd(joint, full_matrices=False)
            rank = int((sizes > joint.shape[0] * np.finfo(np.float64).eps).sum())
            rank = -(-rank // 8) * 8
            basis = rows[:rank]
            found[c, b] = (basis, second[parts[b], parts[c]] @ basis.T, first[parts[b], parts[c]] @ basis.T)
            groups.setdefault(rank, []).append((c, b))
        slots += [(tuple(pairs), rank) for rank, pairs in sorted(groups.items())]
    total = sum(rank for _, rank in slots)
    send = np.zeros((devices, total, size))
    take_second = np.zeros((devices, total, size))
    take_first = np.zeros((devices, total, size))
    at = 0
    for pairs, rank in slots:
        for c, b in pairs:
            basis, left_second, left_first = found[c, b]
            send[c, at : at + rank] = basis
            take_second[b, at : at + rank] = left_second.T
            take_first[b, at : at + rank] = left_first.T
        at += rank
    own_second = np.stack([second[p, p].T for p in parts])
    own_first = np.stack([first[p, p].T for p in parts])
    return slots, send, take_second, take_first, own_second, own_first


def pack_kernel(ranks, at_ref, u_ref, send_ref, *out_refs):
    halves = []
    for half in range(2):
        cells = u_ref[half].reshape(-1, u_ref.shape[-1]).astype(bf16)
        halves.append(
            lax.dot_general(send_ref[0], cells, (((1,), (1,)), ((), ())), preferred_element_type=f32)
        )
    row = 0
    for rank, out_ref in zip(ranks, out_refs):
        both = jnp.concatenate([h[row : row + rank] for h in halves], axis=0)
        out_ref[...] = both.astype(bf16)
        row += rank


def pack(at, u4, send, ranks, chunk):
    _, wears, ages, size = u4.shape
    cells = wears * ages
    return pl.pallas_call(
        functools.partial(pack_kernel, ranks),
        grid_spec=pltpu.PrefetchScalarGridSpec(
            num_scalar_prefetch=1,
            grid=(wears // chunk,),
            in_specs=[
                pl.BlockSpec((2, chunk, ages, size), lambda g, at: (0, g, 0, 0)),
                pl.BlockSpec((1, sum(ranks), size), lambda g, at: (at[0], 0, 0)),
            ],
            out_specs=[pl.BlockSpec((2 * r, chunk * ages), lambda g, at: (0, g)) for r in ranks],
        ),
        out_shape=[jax.ShapeDtypeStruct((2 * r, cells), bf16) for r in ranks],
        compiler_params=pltpu.CompilerParams(vmem_limit_bytes=VMEM_LIMIT),
        cost_estimate=pl.CostEstimate(
            flops=4 * cells * sum(ranks) * size, bytes_accessed=8 * cells * size, transcendentals=0
        ),
        name="pack_coefficients",
    )(at, u4, send)


def section_kernel(ranks, sides, at_ref, side_ref, u_ref, keep_ref, second_ref, first_ref, take_second_ref,
                   take_first_ref, diffusion_ref, drift_ref, *refs):
    q_refs, refs = refs[: len(ranks)], refs[len(ranks) :]
    s_ref, top_ref, bottom_ref = refs[:3]
    edge_refs = refs[3 : 3 + sides]
    own, take = refs[3 + sides :]
    g = pl.program_id(0)
    chunk, ages, size = u_ref.shape[1:]

    @pl.when(g == 0)
    def _():
        diffusion, drift = diffusion_ref[0] * START, drift_ref[0] * START
        own[...] = (second_ref[0] * diffusion + first_ref[0] * drift).astype(bf16)
        take[...] = (take_second_ref[0] * diffusion + take_first_ref[0] * drift).astype(bf16)

    for half in range(2):
        u = u_ref[half].reshape(chunk * ages, size)
        rate = jnp.dot(u.astype(bf16), own[...], preferred_element_type=f32)
        q = jnp.concatenate([r[...].astype(f32)[half * n : half * n + n] for r, n in zip(q_refs, ranks)], axis=0)
        rate += lax.dot_general(
            q.astype(bf16), take[...], (((0,), (0,)), ((), ())), preferred_element_type=f32
        )
        keep = keep_ref[half].reshape(chunk * ages, 128)
        sectioned = rate + jnp.concatenate(
            [keep * u[:, i : i + 128] for i in range(0, size, 128)], axis=1
        )
        sectioned = sectioned.reshape(chunk, ages, size)
        s_ref[half] = sectioned
        last = [sectioned[w, ages - HALO :] for w in range(chunk)]
        first = [sectioned[w, :HALO] for w in range(chunk)]
        last, first = jnp.concatenate(last, axis=0), jnp.concatenate(first, axis=0)
        if sides == 1:
            edge_refs[0][half] = jnp.where(side_ref[0] == 0, last, first).astype(bf16)
        else:
            edge_refs[0][half] = last.astype(bf16)
            edge_refs[1][half] = first.astype(bf16)
        if half == 0:
            @pl.when(g == 0)
            def _():
                top_ref[...] = sectioned[:HALO].reshape(HALO * ages, size).astype(bf16)
        else:
            @pl.when(g == pl.num_programs(0) - 1)
            def _():
                bottom_ref[...] = sectioned[chunk - HALO :].reshape(HALO * ages, size).astype(bf16)


def section(at, side, u4, keep, tables, diffusion, drift, q, ranks, sides, chunk):
    _, wears, ages, size = u4.shape
    cells = wears * ages
    own_second, own_first, take_second, take_first = tables
    total = sum(ranks)
    mine = lambda g, at, side: (at[0], 0, 0)
    whole = lambda g, at, side: (0, 0)
    return pl.pallas_call(
        functools.partial(section_kernel, ranks, sides),
        grid_spec=pltpu.PrefetchScalarGridSpec(
            num_scalar_prefetch=2,
            grid=(wears // chunk,),
            in_specs=[
                pl.BlockSpec((2, chunk, ages, size), lambda g, at, side: (0, g, 0, 0)),
                pl.BlockSpec((2, chunk, ages, 128), lambda g, at, side: (0, g, 0, 0)),
                pl.BlockSpec((1, size, size), mine),
                pl.BlockSpec((1, size, size), mine),
                pl.BlockSpec((1, total, size), mine),
                pl.BlockSpec((1, total, size), mine),
                pl.BlockSpec((1, 1, size), mine),
                pl.BlockSpec((1, 1, size), mine),
            ]
            + [pl.BlockSpec((2 * r, chunk * ages), lambda g, at, side: (0, g)) for r in ranks],
            out_specs=[
                pl.BlockSpec((2, chunk, ages, size), lambda g, at, side: (0, g, 0, 0)),
                pl.BlockSpec((HALO * ages, size), whole),
                pl.BlockSpec((HALO * ages, size), whole),
            ]
            + [pl.BlockSpec((2, chunk * HALO, size), lambda g, at, side: (0, g, 0))] * sides,
            scratch_shapes=[pltpu.VMEM((size, size), bf16), pltpu.VMEM((total, size), bf16)],
        ),
        out_shape=[
            jax.ShapeDtypeStruct((2, wears, ages, size), f32),
            jax.ShapeDtypeStruct((HALO * ages, size), bf16),
            jax.ShapeDtypeStruct((HALO * ages, size), bf16),
        ]
        + [jax.ShapeDtypeStruct((2, wears * HALO, size), bf16)] * sides,
        compiler_params=pltpu.CompilerParams(vmem_limit_bytes=VMEM_LIMIT),
        cost_estimate=pl.CostEstimate(
            flops=4 * cells * (total + size) * size, bytes_accessed=24 * cells * size, transcendentals=0
        ),
        name="section",
    )(at, side, u4, keep, own_second, own_first, take_second, take_first, diffusion, drift, *q)


ROW0 = 16


def substeps_kernel(flag_ref, s_ref, speed_ref, up_ref, down_ref, left_ref, right_ref, ul_ref, ur_ref, dl_ref,
                    dr_ref, o_ref, za, zb, stage, in_sem, out_sem):
    halves, rows, _, _ = za.shape
    wears, ages = rows - 2 * HALO, stage.shape[1]
    first_w, last_w, first_a, last_a = (flag_ref[i] == 1 for i in range(4))
    low, high = ROW0 - 8, ROW0 + ages + 8
    loads = []
    for l in range(halves):
        copy = pltpu.make_async_copy(
            s_ref.at[:, :, pl.ds(l * 128, 128)],
            za.at[l, pl.ds(HALO, wears), pl.ds(ROW0, ages), :],
            in_sem.at[l],
        )
        copy.start()
        loads.append(copy)
    has_left = jnp.where(first_a, 0.0, 1.0).astype(f32)
    has_right = jnp.where(last_a, 0.0, 1.0).astype(f32)
    for l in range(halves):
        lanes = pl.ds(l * 128, 128)
        zero = jnp.zeros((rows, 8, 128), f32)
        za[l, :, low:ROW0, :] = zero
        za[l, :, ROW0 + ages : high, :] = zero
        for z in (za, zb):
            z[l, :, low - 8 : low, :] = zero
            z[l, :, high : high + 8, :] = zero
        for ref, at, wide in ((up_ref, 0, None), (down_ref, HALO + wears, None)):
            za[l, at : at + HALO, ROW0 : ROW0 + ages, :] = ref[:, lanes].astype(f32).reshape(HALO, ages, 128)
        for ref, at, count, col, has in (
            (left_ref, HALO, wears, ROW0 - HALO, has_left),
            (right_ref, HALO, wears, ROW0 + ages, has_right),
            (ul_ref, 0, HALO, ROW0 - HALO, has_left),
            (ur_ref, 0, HALO, ROW0 + ages, has_right),
            (dl_ref, HALO + wears, HALO, ROW0 - HALO, has_left),
            (dr_ref, HALO + wears, HALO, ROW0 + ages, has_right),
        ):
            strip = ref[:, lanes].astype(f32) * has
            za[l, at : at + count, col : col + HALO, :] = strip.reshape(count, HALO, 128)
    sublane = lax.broadcasted_iota(jnp.int32, (8, 128), 0)
    for copy in loads:
        copy.wait()

    keep_low = jnp.zeros((8, 128), f32) + has_left
    keep_high = jnp.zeros((8, 128), f32) + has_right
    stores = []
    for k in range(1, SUBSTEPS + 1):
        src, dst = (za, zb) if k % 2 == 1 else (zb, za)
        final = k == SUBSTEPS
        lo, hi = (ROW0, ROW0 + ages) if final else (low, high)
        pieces = 4 if final else 1
        bounds = [k + (rows - 2 * k) * p // pieces for p in range(pieces + 1)]
        for p in range(pieces):
            for l in range(halves):
                speed = speed_ref[0:1, l * 128 : (l + 1) * 128]
                stay = GAIN * (1.0 - age_courant - 2.0 * wear_spread - speed)
                worn = GAIN * (speed + wear_spread)

                def terms(w, src=src, l=l, lo=lo, hi=hi, stay=stay, worn=worn):
                    t = src[l, w, lo:hi, :]
                    older = src[l, w, lo + 1 : hi + 1, :]
                    slope = older - src[l, w, lo - 1 : hi - 1, :]
                    centre = stay * t + (GAIN * age_courant) * older
                    less = (t - slope) + t
                    return centre, worn * t + slope, less

                def body(w, carry, dst=dst, l=l, lo=lo, hi=hi, final=final, terms=terms):
                    partial, less = carry
                    centre, more, new_less = terms(w + 1)
                    out = partial + more
                    if final:
                        stage[w - HALO, :, l * 128 : (l + 1) * 128] = out
                    else:
                        dst[l, w, lo : lo + 8, :] = out[:8] * keep_low
                        dst[l, w, lo + 8 : hi - 8, :] = out[8:-8]
                        dst[l, w, hi - 8 : hi, :] = out[-8:] * keep_high
                    return centre + less, new_less

                start, stop = bounds[p], bounds[p + 1]
                _, _, less0 = terms(start - 1)
                centre1, _, less1 = terms(start)
                count = stop - start
                lax.fori_loop(start, stop, body, (centre1 + less0, less1), unroll=4 if count % 4 == 0 else 2)
            if final:
                a, b = bounds[p] - HALO, bounds[p + 1] - HALO
                copy = pltpu.make_async_copy(
                    stage.at[pl.ds(a, b - a)], o_ref.at[pl.ds(a, b - a)], out_sem.at[p]
                )
                copy.start()
                stores.append(copy)
        if not final:
            for at, flag in ((HALO - 1, first_w), (HALO + wears, last_w)):
                @pl.when(flag)
                def _(dst=dst, at=at):
                    for l in range(halves):
                        dst[l, at, low:high, :] = jnp.zeros((high - low, 128), f32)
    for copy in stores:
        copy.wait()


def run_substeps(flags, s, speed, halos):
    wears, ages, size = s.shape
    halves = size // 128
    rows = wears + 2 * HALO
    vmem = pl.BlockSpec(memory_space=pltpu.VMEM)
    buffer = pltpu.VMEM((halves, rows, ages + 32, 128), f32)
    return pl.pallas_call(
        substeps_kernel,
        out_shape=jax.ShapeDtypeStruct(s.shape, f32),
        in_specs=[pl.BlockSpec(memory_space=pltpu.SMEM), pl.BlockSpec(memory_space=pl.ANY)] + [vmem] * 9,
        out_specs=pl.BlockSpec(memory_space=pl.ANY),
        scratch_shapes=[
            buffer,
            buffer,
            pltpu.VMEM(s.shape, f32),
            pltpu.SemaphoreType.DMA((halves,)),
            pltpu.SemaphoreType.DMA((4,)),
        ],
        compiler_params=pltpu.CompilerParams(vmem_limit_bytes=VMEM_LIMIT),
        cost_estimate=pl.CostEstimate(
            flops=10 * SUBSTEPS * wears * ages * size, bytes_accessed=8 * wears * ages * size, transcendentals=0
        ),
        name="substeps",
    )(flags, s, speed, *halos)


def body(adjoint_value, load_diffusion, load_drift, wear_speed, hazard):
    wears, ages, size = adjoint_value.shape
    points = load_diffusion.shape[0]
    devices = points // size
    slots, send, take_second, take_first, own_second, own_first = factors(points, devices)
    ranks = tuple(rank for _, rank in slots)
    cheb = lax.axis_index("cheb")
    wear, age = lax.axis_index("wear"), lax.axis_index("age")
    n_wear, n_age = lax.axis_size("wear"), lax.axis_size("age")
    at = cheb.astype(jnp.int32).reshape(1)
    side = age.astype(jnp.int32).reshape(1)
    u4 = adjoint_value.reshape(2, wears // 2, ages, size)
    chunk = 4

    q = pack(at, u4, jnp.asarray(send, bf16), ranks, chunk)
    arrived = [lax.ppermute(x, "cheb", list(pairs)) for x, (pairs, _) in zip(q, slots)]

    keep = jnp.broadcast_to((START * (1.0 - hazard))[:, :, None], (wears, ages, 128))
    keep = keep.reshape(2, wears // 2, ages, 128)
    tables = [jnp.asarray(t, f32) for t in (own_second, own_first, take_second, take_first)]
    sides = 1 if n_age == 2 else 2
    out = section(
        at, side, u4, keep, tables, load_diffusion.reshape(devices, 1, size), load_drift.reshape(devices, 1, size),
        arrived, ranks, sides, chunk,
    )
    s, top, bottom = out[:3]
    edges = out[3:]
    s = s.reshape(wears, ages, size)
    corner = HALO * HALO

    def shift(x, dw, da):
        pairs = []
        for w in range(n_wear):
            for a in range(n_age):
                to_w, to_a = w + dw, (1 - a if da is None else a + da)
                if 0 <= to_w < n_wear and 0 <= to_a < n_age:
                    pairs.append((w * n_age + a, to_w * n_age + to_a))
        return lax.ppermute(x, ("wear", "age"), pairs)

    up, down = shift(bottom, 1, 0), shift(top, -1, 0)
    if sides == 1:
        x = edges[0]
        left = right = shift(x, 0, None).reshape(-1, size)
        ul = ur = shift(x[1, -corner:], 1, None)
        dl = dr = shift(x[0, :corner], -1, None)
    else:
        last, first = edges
        left, right = shift(last, 0, 1).reshape(-1, size), shift(first, 0, -1).reshape(-1, size)
        ul, ur = shift(last[1, -corner:], 1, 1), shift(first[1, -corner:], 1, -1)
        dl, dr = shift(last[0, :corner], -1, 1), shift(first[0, :corner], -1, -1)
    flags = jnp.stack([wear == 0, wear == n_wear - 1, age == 0, age == n_age - 1]).astype(jnp.int32)
    halos = [up, down, left, right, ul, ur, dl, dr]
    return run_substeps(flags, s, wear_speed.reshape(1, size), halos)


def solution(mesh):
    placed = (P("wear", "age", "cheb"), P(), P(), P("cheb"), P("wear", "age"))
    return jax.shard_map(
        body, mesh=mesh, in_specs=placed, out_specs=P("wear", "age", "cheb"), check_vma=False
    )
```

```python
import functools

import jax
import jax.numpy as jnp
import numpy as np
from jax import lax
from jax.experimental import pallas as pl
from jax.experimental.pallas import tpu as pltpu
from jax.sharding import PartitionSpec as P

SUBSTEPS = 4
HALO = SUBSTEPS

age_courant = 0.4
wear_spread = 0.1
coupling = 0.05
GAIN = 1.0 / coupling
START = coupling**SUBSTEPS

f32 = jnp.float32
bf16 = jnp.bfloat16
VMEM_LIMIT = 48 * 2**20


def operators(points):
    modes = np.arange(points)[:, None]
    nodes = np.arange(points)[None, :]
    angles = (modes * (2 * nodes + 1)) % (4 * points) * (np.pi / (2 * points))
    cosine, sine = np.cos(angles), np.sin(angles)
    analysis = np.where(modes == 0, 1.0, 2.0) / points * cosine
    wavenumber = modes / points
    return (-(wavenumber**2) * cosine).T @ analysis, (wavenumber * sine).T @ analysis


def arrived_rows(rank):
    return -(-rank // 16) * 16


@functools.lru_cache(maxsize=None)
def factors(points, devices):
    second, first = operators(points)
    size = points // devices
    parts = [slice(b * size, (b + 1) * size) for b in range(devices)]
    slots, found = [], {}
    for shift in range(1, devices):
        groups = {}
        for c in range(devices):
            b = c ^ shift if devices & (devices - 1) == 0 else (c + shift) % devices
            joint = np.concatenate([second[parts[b], parts[c]], first[parts[b], parts[c]]])
            _, sizes, rows = np.linalg.svd(joint, full_matrices=False)
            rank = int((sizes > joint.shape[0] * np.finfo(np.float64).eps).sum())
            rank = -(-rank // 8) * 8
            basis = rows[:rank]
            found[c, b] = (basis, second[parts[b], parts[c]] @ basis.T, first[parts[b], parts[c]] @ basis.T)
            groups.setdefault(rank, []).append((c, b))
        slots += [(tuple(pairs), rank) for rank, pairs in sorted(groups.items())]
    send = np.zeros((devices, sum(rank for _, rank in slots), size))
    wide = sum(arrived_rows(rank) for _, rank in slots)
    take_second = np.zeros((devices, 2, wide, size))
    take_first = np.zeros((devices, 2, wide, size))
    at = row = 0
    for pairs, rank in slots:
        whole = rank // 16 * 16
        for c, b in pairs:
            basis, left_second, left_first = found[c, b]
            send[c, at : at + rank] = basis
            for half in range(2):
                for take, left in ((take_second, left_second.T), (take_first, left_first.T)):
                    take[b, half, row : row + whole] = left[:whole]
                    place = row + whole + half * (rank - whole)
                    take[b, half, place : place + rank - whole] = left[whole:]
        at += rank
        row += arrived_rows(rank)
    own_second = np.stack([second[p, p].T for p in parts])
    own_first = np.stack([first[p, p].T for p in parts])
    return slots, send, take_second, take_first, own_second, own_first


def pack_kernel(ranks, at_ref, u_hbm, send_hbm, *refs):
    q_refs, (u_ref, send, send_sem, u_sem) = refs[: len(ranks)], refs[len(ranks) :]
    _, wears, ages, size = u_ref.shape
    chunk = 4
    table = pltpu.make_async_copy(send_hbm.at[at_ref[0]], send, send_sem)
    table.start()
    loads = []
    for g in range(wears // chunk):
        rows = pl.ds(g * chunk, chunk)
        loads.append(pltpu.make_async_copy(u_hbm.at[:, rows], u_ref.at[:, rows], u_sem.at[g]))
        loads[-1].start()
    table.wait()
    for g in range(wears // chunk):
        loads[g].wait()
        halves = []
        for half in range(2):
            cells = u_ref[half, g * chunk : (g + 1) * chunk].reshape(chunk * ages, size).astype(bf16)
            halves.append(
                lax.dot_general(send[...], cells, (((1,), (1,)), ((), ())), preferred_element_type=f32)
            )
        row = 0
        for rank, q_ref in zip(ranks, q_refs):
            cut = row + rank // 16 * 16
            pieces = [h[row:cut] for h in halves if cut > row] + [h[cut : row + rank] for h in halves if cut < row + rank]
            q_ref[:, g * chunk * ages : (g + 1) * chunk * ages] = jnp.concatenate(pieces, axis=0).astype(bf16)
            row += rank


ANY = pl.BlockSpec(memory_space=pl.ANY)
VMEM = pl.BlockSpec(memory_space=pltpu.VMEM)
SMEM = pl.BlockSpec(memory_space=pltpu.SMEM)


def in_hbm(x):
    return pltpu.with_memory_space_constraint(x, pltpu.HBM)


def pack(at, u4, send, ranks):
    _, wears, ages, size = u4.shape
    cells = wears * ages
    return pl.pallas_call(
        functools.partial(pack_kernel, ranks),
        in_specs=[SMEM, ANY, ANY],
        out_specs=[VMEM] * (len(ranks) + 1),
        out_shape=[jax.ShapeDtypeStruct((2 * r, cells), bf16) for r in ranks] + [pltpu.VMEM(u4.shape, f32)],
        scratch_shapes=[
            pltpu.VMEM(send.shape[1:], bf16),
            pltpu.SemaphoreType.DMA,
            pltpu.SemaphoreType.DMA((wears // 4,)),
        ],
        compiler_params=pltpu.CompilerParams(vmem_limit_bytes=16 * 2**20),
        cost_estimate=pl.CostEstimate(
            flops=4 * cells * sum(ranks) * size, bytes_accessed=8 * cells * size, transcendentals=0
        ),
        name="pack_coefficients",
    )(at, in_hbm(u4), in_hbm(send))


ROW0 = 16


def local_kernel(at_ref, u_ref, hazard_ref, diffusion_ref, drift_ref, second_hbm, first_hbm, z, second, first, own, sem):
    halves, rows, _, _ = z.shape
    _, wears, ages, size = u_ref.shape
    at = at_ref[0]
    copies = [
        pltpu.make_async_copy(second_hbm.at[at], second, sem.at[0]),
        pltpu.make_async_copy(first_hbm.at[at], first, sem.at[1]),
    ]
    for copy in copies:
        copy.start()
    for l in range(halves):
        zero = jnp.zeros((rows, 16, 128), f32)
        z[l, :, :ROW0, :] = zero
        z[l, :, ROW0 + ages :, :] = zero
    keep = jnp.transpose(START - START * hazard_ref[...])
    for copy in copies:
        copy.wait()
    own[...] = (second[...] * (START * diffusion_ref[at]) + first[...] * (START * drift_ref[at])).astype(bf16)
    chunk = 4
    for w in range(0, 2 * wears, chunk):
        half, v = divmod(w, wears)
        u = u_ref[half, v : v + chunk].reshape(chunk * ages, size)
        rate = jnp.dot(u.astype(bf16), own[...], preferred_element_type=f32)
        for i in range(chunk):
            cells = slice(i * ages, (i + 1) * ages)
            value = rate[cells] + keep[:, w + i : w + i + 1] * u[cells]
            for l in range(halves):
                z[l, HALO + w + i, ROW0 : ROW0 + ages, :] = value[:, l * 128 : (l + 1) * 128]


def local(at, u4, hazard, diffusion, drift, second, first):
    _, wears, ages, size = u4.shape
    cells = 2 * wears * ages
    return pl.pallas_call(
        local_kernel,
        in_specs=[SMEM] + [VMEM] * 4 + [ANY, ANY],
        out_specs=VMEM,
        out_shape=pltpu.VMEM((size // 128, 2 * wears + 2 * HALO, ages + 32, 128), f32),
        scratch_shapes=[
            pltpu.VMEM((size, size), f32),
            pltpu.VMEM((size, size), f32),
            pltpu.VMEM((size, size), bf16),
            pltpu.SemaphoreType.DMA((2,)),
        ],
        compiler_params=pltpu.CompilerParams(vmem_limit_bytes=24 * 2**20),
        cost_estimate=pl.CostEstimate(
            flops=2 * cells * size * size, bytes_accessed=8 * cells * size, transcendentals=0
        ),
        name="local_rate",
    )(at, u4, hazard, diffusion, drift, in_hbm(second), in_hbm(first))


def section_kernel(ranks, sides, wears, ages, at_ref, side_ref, z_in, diffusion_ref, drift_ref, second_hbm, first_hbm,
                   *refs):
    q_refs, refs = refs[: len(ranks)], refs[len(ranks) :]
    z, top_ref, bottom_ref = refs[:3]
    edge_refs = refs[3 : 3 + sides]
    second, first, take, sem = refs[3 + sides :]
    halves, size = z.shape[0], z.shape[0] * 128
    at = at_ref[0]
    copies = [
        pltpu.make_async_copy(second_hbm.at[at], second, sem.at[0]),
        pltpu.make_async_copy(first_hbm.at[at], first, sem.at[1]),
    ]
    for copy in copies:
        copy.start()
    for copy in copies:
        copy.wait()
    take[...] = (second[...] * (START * diffusion_ref[at]) + first[...] * (START * drift_ref[at])).astype(bf16)
    chunk = 4
    for w in range(0, wears, chunk):
        half, v = divmod(w, wears // 2)
        columns = slice(v * ages, (v + chunk) * ages)
        tiles = []
        for rank, q in zip(ranks, q_refs):
            cut = rank // 16 * 16
            if cut:
                tiles.append(q[half * cut : (half + 1) * cut, columns])
            if rank > cut:
                tiles.append(q[2 * cut : 2 * rank, columns])
        rate = lax.dot_general(
            jnp.concatenate(tiles, axis=0), take[half], (((0,), (0,)), ((), ())), preferred_element_type=f32
        )
        values = []
        for i in range(chunk):
            value = [
                z_in[l, HALO + w + i, ROW0 : ROW0 + ages, :]
                + rate[i * ages : (i + 1) * ages, l * 128 : (l + 1) * 128]
                for l in range(halves)
            ]
            for l in range(halves):
                z[l, HALO + w + i, ROW0 : ROW0 + ages, :] = value[l]
            values.append(jnp.concatenate(value, axis=1))
        last = jnp.concatenate([x[ages - HALO :] for x in values], axis=0)
        early = jnp.concatenate([x[:HALO] for x in values], axis=0)
        place = slice(v * HALO, (v + chunk) * HALO)
        if sides == 1:
            edge_refs[0][half, place] = jnp.where(side_ref[0] == 0, last, early).astype(bf16)
        else:
            edge_refs[0][half, place] = last.astype(bf16)
            edge_refs[1][half, place] = early.astype(bf16)
        for start, ref in ((0, top_ref), (wears - HALO, bottom_ref)):
            if w == start:
                ref[...] = jnp.concatenate(values, axis=0).astype(bf16)


def section(at, side, z, diffusion, drift, second, first, q, ranks, sides, wears, ages):
    size = z.shape[0] * 128
    cells = wears * ages
    wide = second.shape[2]
    return pl.pallas_call(
        functools.partial(section_kernel, ranks, sides, wears, ages),
        in_specs=[SMEM, SMEM, VMEM, VMEM, VMEM, ANY, ANY] + [VMEM] * len(ranks),
        out_specs=[VMEM] * (3 + sides),
        out_shape=[
            pltpu.VMEM(z.shape, f32),
            jax.ShapeDtypeStruct((HALO * ages, size), bf16),
            jax.ShapeDtypeStruct((HALO * ages, size), bf16),
        ]
        + [jax.ShapeDtypeStruct((2, wears // 2 * HALO, size), bf16)] * sides,
        scratch_shapes=[
            pltpu.VMEM((2, wide, size), f32),
            pltpu.VMEM((2, wide, size), f32),
            pltpu.VMEM((2, wide, size), bf16),
            pltpu.SemaphoreType.DMA((2,)),
        ],
        input_output_aliases={2: 0},
        compiler_params=pltpu.CompilerParams(vmem_limit_bytes=24 * 2**20),
        cost_estimate=pl.CostEstimate(
            flops=2 * cells * wide * size, bytes_accessed=8 * cells * size, transcendentals=0
        ),
        name="section",
    )(at, side, z, diffusion, drift, in_hbm(second), in_hbm(first), *q)


def substeps_kernel(flag_ref, z_in, speed_ref, up_ref, down_ref, left_ref, right_ref, ul_ref, ur_ref, dl_ref,
                    dr_ref, o_ref, za, zb, stage, out_sem):
    halves, rows, _, _ = za.shape
    wears, ages = rows - 2 * HALO, stage.shape[1]
    first_w, last_w, first_a, last_a = (flag_ref[i] == 1 for i in range(4))
    low, high = ROW0 - 8, ROW0 + ages + 8
    has_left = jnp.where(first_a, 0.0, 1.0).astype(f32)
    has_right = jnp.where(last_a, 0.0, 1.0).astype(f32)
    for l in range(halves):
        lanes = pl.ds(l * 128, 128)
        zero = jnp.zeros((rows, 8, 128), f32)
        zb[l, :, low - 8 : low, :] = zero
        zb[l, :, high : high + 8, :] = zero
        for ref, at in ((up_ref, 0), (down_ref, HALO + wears)):
            za[l, at : at + HALO, ROW0 : ROW0 + ages, :] = ref[:, lanes].astype(f32).reshape(HALO, ages, 128)
        for ref, at, count, col, has in (
            (left_ref, HALO, wears, ROW0 - HALO, has_left),
            (right_ref, HALO, wears, ROW0 + ages, has_right),
            (ul_ref, 0, HALO, ROW0 - HALO, has_left),
            (ur_ref, 0, HALO, ROW0 + ages, has_right),
            (dl_ref, HALO + wears, HALO, ROW0 - HALO, has_left),
            (dr_ref, HALO + wears, HALO, ROW0 + ages, has_right),
        ):
            strip = ref[:, lanes].astype(f32) * has
            za[l, at : at + count, col : col + HALO, :] = strip.reshape(count, HALO, 128)

    keep_low = jnp.zeros((8, 128), f32) + has_left
    keep_high = jnp.zeros((8, 128), f32) + has_right
    stores = []
    for k in range(1, SUBSTEPS + 1):
        src, dst = (za, zb) if k % 2 == 1 else (zb, za)
        final = k == SUBSTEPS
        lo, hi = (ROW0, ROW0 + ages) if final else (low, high)
        pieces = 4 if final else 1
        bounds = [k + (rows - 2 * k) * p // pieces for p in range(pieces + 1)]
        for p in range(pieces):
            for l in range(halves):
                speed = speed_ref[0:1, l * 128 : (l + 1) * 128]
                stay = GAIN * (1.0 - age_courant - 2.0 * wear_spread - speed)
                worn = GAIN * (speed + wear_spread)

                def terms(w, src=src, l=l, lo=lo, hi=hi, stay=stay, worn=worn):
                    t = src[l, w, lo:hi, :]
                    older = src[l, w, lo + 1 : hi + 1, :]
                    slope = older - src[l, w, lo - 1 : hi - 1, :]
                    centre = stay * t + (GAIN * age_courant) * older
                    less = (t - slope) + t
                    return centre, worn * t + slope, less

                def body(w, carry, dst=dst, l=l, lo=lo, hi=hi, final=final, terms=terms):
                    partial, less = carry
                    centre, more, new_less = terms(w + 1)
                    out = partial + more
                    if final:
                        stage[w - HALO, :, l * 128 : (l + 1) * 128] = out
                    else:
                        dst[l, w, lo : lo + 8, :] = out[:8] * keep_low
                        dst[l, w, lo + 8 : hi - 8, :] = out[8:-8]
                        dst[l, w, hi - 8 : hi, :] = out[-8:] * keep_high
                    return centre + less, new_less

                start, stop = bounds[p], bounds[p + 1]
                _, _, less0 = terms(start - 1)
                centre1, _, less1 = terms(start)
                count = stop - start
                lax.fori_loop(start, stop, body, (centre1 + less0, less1), unroll=4 if count % 4 == 0 else 2)
            if final:
                a, b = bounds[p] - HALO, bounds[p + 1] - HALO
                copy = pltpu.make_async_copy(
                    stage.at[pl.ds(a, b - a)], o_ref.at[pl.ds(a, b - a)], out_sem.at[p]
                )
                copy.start()
                stores.append(copy)
        if not final:
            for at, flag in ((HALO - 1, first_w), (HALO + wears, last_w)):
                @pl.when(flag)
                def _(dst=dst, at=at):
                    for l in range(halves):
                        dst[l, at, low:high, :] = jnp.zeros((high - low, 128), f32)
    for copy in stores:
        copy.wait()


def run_substeps(flags, z, speed, halos, wears, ages):
    size = z.shape[0] * 128
    shape = (wears, ages, size)
    return pl.pallas_call(
        substeps_kernel,
        out_shape=[jax.ShapeDtypeStruct(shape, f32), pltpu.VMEM(z.shape, f32)],
        in_specs=[SMEM] + [VMEM] * 10,
        out_specs=[ANY, VMEM],
        scratch_shapes=[
            pltpu.VMEM(z.shape, f32),
            pltpu.VMEM(shape, f32),
            pltpu.SemaphoreType.DMA((4,)),
        ],
        input_output_aliases={1: 1},
        compiler_params=pltpu.CompilerParams(vmem_limit_bytes=32 * 2**20),
        cost_estimate=pl.CostEstimate(
            flops=10 * SUBSTEPS * wears * ages * size, bytes_accessed=8 * wears * ages * size, transcendentals=0
        ),
        name="substeps",
    )(flags, z, speed, *halos)[0]


def body(adjoint_value, load_diffusion, load_drift, wear_speed, hazard):
    wears, ages, size = adjoint_value.shape
    points = load_diffusion.shape[0]
    devices = points // size
    slots, send, take_second, take_first, own_second, own_first = factors(points, devices)
    ranks = tuple(rank for _, rank in slots)
    cheb = lax.axis_index("cheb")
    wear, age = lax.axis_index("wear"), lax.axis_index("age")
    n_wear, n_age = lax.axis_size("wear"), lax.axis_size("age")
    at = cheb.astype(jnp.int32).reshape(1)
    side = age.astype(jnp.int32).reshape(1)
    u4 = adjoint_value.reshape(2, wears // 2, ages, size)
    diffusion = load_diffusion.reshape(devices, 1, size)
    drift = load_drift.reshape(devices, 1, size)

    *q, u4 = pack(at, u4, jnp.asarray(send, bf16), ranks)
    arrived = [lax.ppermute(x, "cheb", list(pairs)) for x, (pairs, _) in zip(q, slots)]
    z = local(at, u4, hazard, diffusion, drift, jnp.asarray(own_second, f32), jnp.asarray(own_first, f32))
    sides = 1 if n_age == 2 else 2
    z, top, bottom, *edges = section(
        at, side, z, diffusion, drift, jnp.asarray(take_second, f32), jnp.asarray(take_first, f32), arrived, ranks,
        sides, wears, ages,
    )
    corner = HALO * HALO

    def shift(x, dw, da):
        pairs = []
        for w in range(n_wear):
            for a in range(n_age):
                to_w, to_a = w + dw, (1 - a if da is None else a + da)
                if 0 <= to_w < n_wear and 0 <= to_a < n_age:
                    pairs.append((w * n_age + a, to_w * n_age + to_a))
        return lax.ppermute(x, ("wear", "age"), pairs)

    if sides == 1:
        x = edges[0]
        ul = ur = shift(x[1, -corner:], 1, None)
        dl = dr = shift(x[0, :corner], -1, None)
        left = right = shift(x, 0, None).reshape(-1, size)
    else:
        last, first = edges
        ul, ur = shift(last[1, -corner:], 1, 1), shift(first[1, -corner:], 1, -1)
        dl, dr = shift(last[0, :corner], -1, 1), shift(first[0, :corner], -1, -1)
        left, right = shift(last, 0, 1).reshape(-1, size), shift(first, 0, -1).reshape(-1, size)
    up, down = shift(bottom, 1, 0), shift(top, -1, 0)
    flags = jnp.stack([wear == 0, wear == n_wear - 1, age == 0, age == n_age - 1]).astype(jnp.int32)
    halos = [up, down, left, right, ul, ur, dl, dr]
    return run_substeps(flags, z, wear_speed.reshape(1, size), halos, wears, ages)


def solution(mesh):
    placed = (P("wear", "age", "cheb"), P(), P(), P("cheb"), P("wear", "age"))
    return jax.shard_map(
        body, mesh=mesh, in_specs=placed, out_specs=P("wear", "age", "cheb"), check_vma=False
    )
```

```python
import functools

import jax
import jax.numpy as jnp
import numpy as np
from jax import lax
from jax.experimental import pallas as pl
from jax.experimental.pallas import tpu as pltpu
from jax.sharding import PartitionSpec as P

SUBSTEPS = 4
HALO = SUBSTEPS

age_courant = 0.4
wear_spread = 0.1
coupling = 0.05
GAIN = 1.0 / coupling
START = coupling**SUBSTEPS

f32 = jnp.float32
bf16 = jnp.bfloat16


def operators(points):
    modes = np.arange(points)[:, None]
    nodes = np.arange(points)[None, :]
    angles = (modes * (2 * nodes + 1)) % (4 * points) * (np.pi / (2 * points))
    cosine, sine = np.cos(angles), np.sin(angles)
    analysis = np.where(modes == 0, 1.0, 2.0) / points * cosine
    wavenumber = modes / points
    return (-(wavenumber**2) * cosine).T @ analysis, (wavenumber * sine).T @ analysis


def arrived_rows(rank):
    return -(-rank // 16) * 16


@functools.lru_cache(maxsize=None)
def factors(points, devices):
    second, first = operators(points)
    size = points // devices
    parts = [slice(b * size, (b + 1) * size) for b in range(devices)]
    slots, found = [], {}
    for shift in range(1, devices):
        groups = {}
        for c in range(devices):
            b = c ^ shift if devices & (devices - 1) == 0 else (c + shift) % devices
            joint = np.concatenate([second[parts[b], parts[c]], first[parts[b], parts[c]]])
            _, sizes, rows = np.linalg.svd(joint, full_matrices=False)
            rank = int((sizes > joint.shape[0] * np.finfo(np.float64).eps).sum())
            rank = -(-rank // 8) * 8
            basis = rows[:rank]
            found[c, b] = (basis, second[parts[b], parts[c]] @ basis.T, first[parts[b], parts[c]] @ basis.T)
            groups.setdefault(rank, []).append((c, b))
        slots += [(tuple(pairs), rank) for rank, pairs in sorted(groups.items())]
    send = np.zeros((devices, sum(rank for _, rank in slots), size))
    wide = sum(arrived_rows(rank) for _, rank in slots)
    take_second = np.zeros((devices, 2, wide, size))
    take_first = np.zeros((devices, 2, wide, size))
    at = row = 0
    for pairs, rank in slots:
        whole = rank // 16 * 16
        for c, b in pairs:
            basis, left_second, left_first = found[c, b]
            send[c, at : at + rank] = basis
            for half in range(2):
                for take, left in ((take_second, left_second.T), (take_first, left_first.T)):
                    take[b, half, row : row + whole] = left[:whole]
                    place = row + whole + half * (rank - whole)
                    take[b, half, place : place + rank - whole] = left[whole:]
        at += rank
        row += arrived_rows(rank)
    own_second = np.stack([second[p, p].T for p in parts])
    own_first = np.stack([first[p, p].T for p in parts])
    return slots, send, take_second, take_first, own_second, own_first


ANY = pl.BlockSpec(memory_space=pl.ANY)
VMEM = pl.BlockSpec(memory_space=pltpu.VMEM)
SMEM = pl.BlockSpec(memory_space=pltpu.SMEM)
ROW0 = 16
HAZARD_ROWS = 16


def in_hbm(x):
    return pltpu.with_memory_space_constraint(x, pltpu.HBM)


def in_vmem(x):
    return pltpu.with_memory_space_constraint(x, pltpu.VMEM)


def params(mebibytes):
    return pltpu.CompilerParams(vmem_limit_bytes=mebibytes * 2**20)


def cost(flops, bytes_accessed):
    return pl.CostEstimate(flops=flops, bytes_accessed=bytes_accessed, transcendentals=0)


def edge_kernel(sides, side_ref, u_hbm, hazard_hbm, *refs):
    out_refs, (tiles, hazard, sem) = refs[:sides], refs[sides:]
    wears, ages, size = u_hbm.shape
    copies = [pltpu.make_async_copy(hazard_hbm, hazard, sem.at[sides])]
    for i in range(sides):
        if sides == 1:
            start = pl.multiple_of(jnp.where(side_ref[0] == 0, ages - 8, 0), 8)
        else:
            start = (ages - 8, 0)[i]
        copies.append(pltpu.make_async_copy(u_hbm.at[:, pl.ds(start, 8)], tiles.at[i], sem.at[i]))
    for copy in copies:
        copy.start()
    for copy in copies:
        copy.wait()
    by_age = jnp.transpose(hazard[...])
    last, early = by_age[ages - HALO :], by_age[:HALO]
    for i, out_ref in enumerate(out_refs):
        for w in range(0, wears, 4):
            late = [tiles[i, w + j, 8 - HALO :] for j in range(4)]
            soon = [tiles[i, w + j, :HALO] for j in range(4)]
            late, soon = jnp.concatenate(late, axis=0), jnp.concatenate(soon, axis=0)
            if sides == 1:
                cells = jnp.where(side_ref[0] == 0, late, soon)
            else:
                cells = (late, soon)[i]
            out_ref[w * HALO : (w + 4) * HALO] = cells.astype(bf16)
        if sides == 1:
            exact = jnp.where(side_ref[0] == 0, last, early)
        else:
            exact = (last, early)[i]
        high = exact.astype(bf16).astype(f32)
        rows = jnp.concatenate([high, exact - high, jnp.zeros((HAZARD_ROWS - 2 * HALO, wears), f32)], axis=0)
        rows = jnp.concatenate([rows, jnp.zeros((HAZARD_ROWS, size - wears), f32)], axis=1)
        out_ref[wears * HALO :] = rows.astype(bf16)


def edges(side, u, hazard, sides):
    wears, ages, size = u.shape
    return pl.pallas_call(
        functools.partial(edge_kernel, sides),
        in_specs=[SMEM, ANY, ANY],
        out_specs=[VMEM] * sides,
        out_shape=[jax.ShapeDtypeStruct((wears * HALO + HAZARD_ROWS, size), bf16)] * sides,
        scratch_shapes=[
            pltpu.VMEM((sides, wears, 8, size), f32),
            pltpu.VMEM((wears, ages), f32),
            pltpu.SemaphoreType.DMA((sides + 1,)),
        ],
        compiler_params=params(8),
        cost_estimate=cost(0, 8 * wears * 8 * size),
        name="age_edges",
    )(side, in_hbm(u), in_hbm(hazard))


def pack_rows(ranks, halves):
    packed, row = [], 0
    for rank in ranks:
        cut = row + rank // 16 * 16
        pieces = [h[row:cut] for h in halves if cut > row]
        pieces += [h[cut : row + rank] for h in halves if cut < row + rank]
        packed.append(jnp.concatenate(pieces, axis=0).astype(bf16))
        row += rank
    return packed


def analyse(table, cells):
    return lax.dot_general(table, cells, (((1,), (1,)), ((), ())), preferred_element_type=f32)


def pack_kernel(ranks, at_ref, u_hbm, send_hbm, *refs):
    q_refs, (u_ref, send, send_sem, u_sem) = refs[: len(ranks)], refs[len(ranks) :]
    _, wears, ages, size = u_ref.shape
    chunk = 4
    table = pltpu.make_async_copy(send_hbm.at[at_ref[0]], send, send_sem)
    table.start()
    loads = []
    for g in range(wears // chunk):
        rows = pl.ds(g * chunk, chunk)
        loads.append(pltpu.make_async_copy(u_hbm.at[:, rows], u_ref.at[:, rows], u_sem.at[g]))
        loads[-1].start()
    table.wait()
    for g in range(wears // chunk):
        loads[g].wait()
        halves = [
            analyse(send[...], u_ref[half, g * chunk : (g + 1) * chunk].reshape(chunk * ages, size).astype(bf16))
            for half in range(2)
        ]
        for q_ref, rows in zip(q_refs, pack_rows(ranks, halves)):
            q_ref[:, g * chunk * ages : (g + 1) * chunk * ages] = rows


def pack(at, u4, send, ranks, extra):
    _, wears, ages, size = u4.shape
    cells = wears * ages
    return pl.pallas_call(
        functools.partial(pack_kernel, ranks),
        in_specs=[SMEM, ANY, ANY],
        out_specs=[VMEM] * (len(ranks) + 2),
        out_shape=[jax.ShapeDtypeStruct((2 * r, cells + extra), bf16) for r in ranks]
        + [pltpu.VMEM(u4.shape, f32), pltpu.VMEM(send.shape[1:], bf16)],
        scratch_shapes=[pltpu.SemaphoreType.DMA, pltpu.SemaphoreType.DMA((wears // 4,))],
        compiler_params=params(16),
        cost_estimate=cost(4 * cells * sum(ranks) * size, 8 * cells * size),
        name="pack_coefficients",
    )(at, in_hbm(u4), in_hbm(send))


def pack_edges_kernel(ranks, sides, send_ref, *refs):
    edge_refs, q_refs = refs[:sides], refs[sides + len(ranks) :]
    count = edge_refs[0].shape[0] - HAZARD_ROWS
    halves = []
    for half in range(2):
        cells = [r[half * count // 2 : (half + 1) * count // 2] for r in edge_refs]
        halves.append(analyse(send_ref[...], jnp.concatenate(cells, axis=0)))
    for q_ref, rows in zip(q_refs, pack_rows(ranks, halves)):
        q_ref[:, q_ref.shape[1] - rows.shape[1] :] = rows


def pack_edges(send, near, q, ranks, sides):
    return pl.pallas_call(
        functools.partial(pack_edges_kernel, ranks, sides),
        in_specs=[VMEM] * (1 + sides + len(ranks)),
        out_specs=[VMEM] * len(ranks),
        out_shape=[jax.ShapeDtypeStruct(x.shape, x.dtype) for x in q],
        input_output_aliases={1 + sides + i: i for i in range(len(ranks))},
        compiler_params=params(8),
        cost_estimate=cost(0, 2**18),
        name="pack_edges",
    )(in_vmem(send), *near, *q)


def local_kernel(sides, at_ref, u_ref, hazard_hbm, diffusion_hbm, drift_hbm, second_hbm, first_hbm, take_second_hbm,
                 take_first_hbm, *refs):
    edge_refs, refs = refs[:sides], refs[sides:]
    z, beside, take, hazard, diffusion, drift, second, first, own, take_second, take_first, sem = refs
    halves, rows, _, _ = z.shape
    _, wears, ages, size = u_ref.shape
    at = at_ref[0]
    moves = (
        (second_hbm.at[at], second), (first_hbm.at[at], first), (diffusion_hbm.at[at], diffusion),
        (drift_hbm.at[at], drift), (hazard_hbm, hazard), (take_second_hbm.at[at], take_second),
        (take_first_hbm.at[at], take_first),
    )
    copies = [pltpu.make_async_copy(src, dst, sem.at[i]) for i, (src, dst) in enumerate(moves)]
    for copy in copies:
        copy.start()
    for l in range(halves):
        zero = jnp.zeros((rows, 16, 128), f32)
        z[l, :, :ROW0, :] = zero
        z[l, :, ROW0 + ages :, :] = zero
    for copy in copies:
        copy.wait()
    scaled, moved = START * diffusion[...], START * drift[...]
    own[...] = (second[...] * scaled + first[...] * moved).astype(bf16)
    take[...] = (take_second[...] * scaled + take_first[...] * moved).astype(bf16)
    keep = jnp.transpose(START - START * hazard[...])
    chunk = 4
    for w in range(0, 2 * wears, chunk):
        half, v = divmod(w, wears)
        u = u_ref[half, v : v + chunk].reshape(chunk * ages, size)
        rate = jnp.dot(u.astype(bf16), own[...], preferred_element_type=f32)
        for i in range(chunk):
            cells = slice(i * ages, (i + 1) * ages)
            value = rate[cells] + keep[:, w + i : w + i + 1] * u[cells]
            for l in range(halves):
                z[l, HALO + w + i, ROW0 : ROW0 + ages, :] = value[:, l * 128 : (l + 1) * 128]
    for s, ref in enumerate(edge_refs):
        count = 2 * wears * HALO
        parts = ref[count:].astype(f32)
        near = START - START * (parts[:HALO, : 2 * wears] + parts[HALO : 2 * HALO, : 2 * wears])
        near = jnp.concatenate([near, near], axis=0)
        for w in range(0, 2 * wears, 4):
            place = slice(w * HALO, (w + 4) * HALO)
            u = ref[place]
            rate = jnp.dot(u, own[...], preferred_element_type=f32)
            columns = [
                jnp.broadcast_to(near[:HALO, w + j : w + j + 1], (HALO, size)) for j in range(4)
            ]
            beside[s, place] = rate + jnp.concatenate(columns, axis=0) * u.astype(f32)


def local(at, u4, hazard, diffusion, drift, tables, near, sides):
    _, wears, ages, size = u4.shape
    cells = 2 * wears * ages
    wide = tables[2].shape[2]
    return pl.pallas_call(
        functools.partial(local_kernel, sides),
        in_specs=[SMEM, VMEM] + [ANY] * 7 + [VMEM] * sides,
        out_specs=[VMEM] * 3,
        out_shape=[
            pltpu.VMEM((size // 128, 2 * wears + 2 * HALO, ages + 32, 128), f32),
            pltpu.VMEM((sides, 2 * wears * HALO, size), f32),
            pltpu.VMEM((2, wide, size), bf16),
        ],
        scratch_shapes=[
            pltpu.VMEM(hazard.shape, f32),
            pltpu.VMEM((1, size), f32),
            pltpu.VMEM((1, size), f32),
            pltpu.VMEM((size, size), f32),
            pltpu.VMEM((size, size), f32),
            pltpu.VMEM((size, size), bf16),
            pltpu.VMEM((2, wide, size), f32),
            pltpu.VMEM((2, wide, size), f32),
            pltpu.SemaphoreType.DMA((7,)),
        ],
        compiler_params=params(24),
        cost_estimate=cost(2 * cells * size * size, 8 * cells * size),
        name="local_rate",
    )(at, in_vmem(u4), *[in_hbm(x) for x in (hazard, diffusion, drift, *tables)], *near)


def arrived_tiles(ranks, q_refs, half, columns):
    tiles = []
    for rank, q in zip(ranks, q_refs):
        cut = rank // 16 * 16
        if cut:
            tiles.append(q[half * cut : (half + 1) * cut, columns])
        if rank > cut:
            tiles.append(q[2 * cut : 2 * rank, columns])
    return jnp.concatenate(tiles, axis=0)


def distant(ranks, q_refs, take_ref, half, columns):
    return lax.dot_general(
        arrived_tiles(ranks, q_refs, half, columns), take_ref[half], (((0,), (0,)), ((), ())),
        preferred_element_type=f32,
    )


def edge_columns(sides, main, each):
    return [slice(main + s * each, main + (s + 1) * each) for s in range(sides)]


def rows_kernel(ranks, sides, wears, ages, z_in, beside_ref, take_ref, *refs):
    q_refs, (z, top_ref, bottom_ref) = refs[: len(ranks)], refs[len(ranks) :]
    del z
    halves = z_in.shape[0]
    main, each = wears // 2 * ages, wears // 2 * HALO
    for half, start, ref in ((0, 0, top_ref), (1, wears - HALO, bottom_ref)):
        v = (start - half * wears // 2) * ages
        rate = distant(ranks, q_refs, take_ref, half, slice(v, v + HALO * ages))
        for i in range(HALO):
            near = [z_in[l, HALO + start + i, ROW0 : ROW0 + ages, :] for l in range(halves)]
            cells = slice(i * ages, (i + 1) * ages)
            ref[cells] = (rate[cells] + jnp.concatenate(near, axis=1)).astype(bf16)
        for s, columns in enumerate(edge_columns(sides, main, each)):
            corner = HALO * HALO
            first = 0 if half == 0 else each - corner
            rate = distant(ranks, q_refs, take_ref, half, columns)[first : first + corner]
            place = slice(start * HALO, start * HALO + corner)
            row = HALO * ages + s * corner
            ref[row : row + corner] = (rate + beside_ref[s, place]).astype(bf16)


def outer_rows(z, beside, take, q, ranks, sides, wears, ages):
    size = z.shape[0] * 128
    message = jax.ShapeDtypeStruct((HALO * ages + sides * HALO * HALO, size), bf16)
    return pl.pallas_call(
        functools.partial(rows_kernel, ranks, sides, wears, ages),
        in_specs=[VMEM] * (3 + len(ranks)),
        out_specs=[VMEM] * 3,
        out_shape=[pltpu.VMEM(z.shape, f32), message, message],
        input_output_aliases={0: 0},
        compiler_params=params(8),
        cost_estimate=cost(2 * 8 * ages * take.shape[1] * size, 2**20),
        name="outer_rows",
    )(z, in_vmem(beside), in_vmem(take), *q)


def section_kernel(ranks, sides, wears, ages, flag_ref, z_in, beside_ref, take_ref, *refs):
    q_refs, (z,) = refs[: len(ranks)], refs[len(ranks) :]
    halves = z.shape[0]
    main, each = wears // 2 * ages, wears // 2 * HALO
    chunk = 4
    for w in range(0, wears, chunk):
        half, v = divmod(w, wears // 2)
        rate = distant(ranks, q_refs, take_ref, half, slice(v * ages, (v + chunk) * ages))
        for i in range(chunk):
            for l in range(halves):
                z[l, HALO + w + i, ROW0 : ROW0 + ages, :] = (
                    z_in[l, HALO + w + i, ROW0 : ROW0 + ages, :]
                    + rate[i * ages : (i + 1) * ages, l * 128 : (l + 1) * 128]
                )
    has = [jnp.where(flag_ref[2 + i] == 1, 0.0, 1.0).astype(f32) for i in range(2)]
    for s in range(sides):
        for half in range(2):
            columns = edge_columns(sides, main, each)[s]
            place = slice(half * each, (half + 1) * each)
            cells = distant(ranks, q_refs, take_ref, half, columns) + beside_ref[s, place]
            for i, column in ((0, ROW0 - HALO), (1, ROW0 + ages)):
                if sides == 1 or s == i:
                    part = cells * has[i]
                    for w in range(wears // 2):
                        for l in range(halves):
                            z[l, HALO + half * wears // 2 + w, column : column + HALO, :] = part[
                                w * HALO : (w + 1) * HALO, l * 128 : (l + 1) * 128
                            ]


def section(flags, z, beside, take, q, ranks, sides, wears, ages):
    size = z.shape[0] * 128
    cells = wears * ages
    return pl.pallas_call(
        functools.partial(section_kernel, ranks, sides, wears, ages),
        in_specs=[SMEM] + [VMEM] * (3 + len(ranks)),
        out_specs=VMEM,
        out_shape=pltpu.VMEM(z.shape, f32),
        input_output_aliases={1: 0},
        compiler_params=params(24),
        cost_estimate=cost(2 * cells * take.shape[1] * size, 8 * cells * size),
        name="section",
    )(flags, z, in_vmem(beside), in_vmem(take), *q)


def substeps_kernel(sides, flag_ref, z_in, speed_ref, up_ref, down_ref, o_ref, za, zb, stage, out_sem):
    del z_in
    halves, rows, _, _ = za.shape
    wears, ages = rows - 2 * HALO, stage.shape[1]
    first_w, last_w, first_a, last_a = (flag_ref[i] == 1 for i in range(4))
    has = [jnp.where(x, 0.0, 1.0).astype(f32) for x in (first_a, last_a)]
    for l in range(halves):
        lanes = pl.ds(l * 128, 128)
        zb[l, :, :ROW0, :] = jnp.zeros((rows, ROW0, 128), f32)
        zb[l, :, ROW0 + ages :, :] = jnp.zeros((rows, 16, 128), f32)
        for ref, at in ((up_ref, 0), (down_ref, HALO + wears)):
            values = ref[:, lanes].astype(f32)
            za[l, at : at + HALO, ROW0 : ROW0 + ages, :] = values[: HALO * ages].reshape(HALO, ages, 128)
            for s in range(sides):
                corner = values[HALO * (ages + s * HALO) : HALO * (ages + (s + 1) * HALO)]
                for i, column in ((0, ROW0 - HALO), (1, ROW0 + ages)):
                    if sides == 1 or s == i:
                        part = corner * has[i]
                        for w in range(HALO):
                            za[l, at + w, column : column + HALO, :] = part[w * HALO : (w + 1) * HALO]

    def run(low, high, masked):
        stores = []
        keep_low = jnp.zeros((8, 128), f32) + has[0]
        keep_high = jnp.zeros((8, 128), f32) + has[1]
        for k in range(1, SUBSTEPS + 1):
            src, dst = (za, zb) if k % 2 == 1 else (zb, za)
            final = k == SUBSTEPS
            lo, hi = (ROW0, ROW0 + ages) if final else (low, high)
            pieces = 4 if final else 1
            bounds = [k + (rows - 2 * k) * p // pieces for p in range(pieces + 1)]
            for p in range(pieces):
                for l in range(halves):
                    speed = speed_ref[0:1, l * 128 : (l + 1) * 128]
                    stay = GAIN * (1.0 - age_courant - 2.0 * wear_spread - speed)
                    worn = GAIN * (speed + wear_spread)

                    def terms(w, src=src, l=l, lo=lo, hi=hi, stay=stay, worn=worn):
                        t = src[l, w, lo:hi, :]
                        older = src[l, w, lo + 1 : hi + 1, :]
                        slope = older - src[l, w, lo - 1 : hi - 1, :]
                        centre = stay * t + (GAIN * age_courant) * older
                        less = (t - slope) + t
                        return centre, worn * t + slope, less

                    def body(w, carry, dst=dst, l=l, lo=lo, hi=hi, final=final, terms=terms):
                        partial, less = carry
                        centre, more, new_less = terms(w + 1)
                        out = partial + more
                        if final:
                            stage[w - HALO, :, l * 128 : (l + 1) * 128] = out
                        elif masked:
                            dst[l, w, lo : lo + 8, :] = out[:8] * keep_low
                            dst[l, w, lo + 8 : hi - 8, :] = out[8:-8]
                            dst[l, w, hi - 8 : hi, :] = out[-8:] * keep_high
                        else:
                            dst[l, w, lo:hi, :] = out
                        return centre + less, new_less

                    start, stop = bounds[p], bounds[p + 1]
                    _, _, less0 = terms(start - 1)
                    centre1, _, less1 = terms(start)
                    count = stop - start
                    lax.fori_loop(start, stop, body, (centre1 + less0, less1), unroll=4 if count % 4 == 0 else 2)
                if final:
                    a, b = bounds[p] - HALO, bounds[p + 1] - HALO
                    copy = pltpu.make_async_copy(
                        stage.at[pl.ds(a, b - a)], o_ref.at[pl.ds(a, b - a)], out_sem.at[p]
                    )
                    copy.start()
                    stores.append(copy)
            if not final:
                for at, flag in ((HALO - 1, first_w), (HALO + wears, last_w)):
                    @pl.when(flag)
                    def _(dst=dst, at=at):
                        for l in range(halves):
                            dst[l, at, low:high, :] = jnp.zeros((high - low, 128), f32)
        for copy in stores:
            copy.wait()

    if sides == 1:
        pl.when(first_a)(lambda: run(ROW0, ROW0 + ages + 8, False))
        pl.when(last_a)(lambda: run(ROW0 - 8, ROW0 + ages, False))
    else:
        run(ROW0 - 8, ROW0 + ages + 8, True)


def run_substeps(flags, z, speed, up, down, sides, wears, ages):
    size = z.shape[0] * 128
    shape = (wears, ages, size)
    return pl.pallas_call(
        functools.partial(substeps_kernel, sides),
        out_shape=[jax.ShapeDtypeStruct(shape, f32), pltpu.VMEM(z.shape, f32)],
        in_specs=[SMEM] + [VMEM] * 4,
        out_specs=[ANY, VMEM],
        scratch_shapes=[
            pltpu.VMEM(z.shape, f32),
            pltpu.VMEM(shape, f32),
            pltpu.SemaphoreType.DMA((4,)),
        ],
        input_output_aliases={1: 1},
        compiler_params=params(32),
        cost_estimate=cost(10 * SUBSTEPS * wears * ages * size, 8 * wears * ages * size),
        name="substeps",
    )(flags, z, speed, up, down)[0]


def body(adjoint_value, load_diffusion, load_drift, wear_speed, hazard):
    wears, ages, size = adjoint_value.shape
    points = load_diffusion.shape[0]
    devices = points // size
    slots, send, take_second, take_first, own_second, own_first = factors(points, devices)
    ranks = tuple(rank for _, rank in slots)
    cheb = lax.axis_index("cheb")
    wear, age = lax.axis_index("wear"), lax.axis_index("age")
    n_wear, n_age = lax.axis_size("wear"), lax.axis_size("age")
    at = cheb.astype(jnp.int32).reshape(1)
    side = age.astype(jnp.int32).reshape(1)
    flags = jnp.stack([wear == 0, wear == n_wear - 1, age == 0, age == n_age - 1]).astype(jnp.int32)
    sides = 1 if n_age == 2 else 2
    extra = sides * wears // 2 * HALO
    u4 = adjoint_value.reshape(2, wears // 2, ages, size)
    diffusion = load_diffusion.reshape(devices, 1, size)
    drift = load_drift.reshape(devices, 1, size)
    tables = [jnp.asarray(t, f32) for t in (own_second, own_first, take_second, take_first)]

    edge = edges(side, adjoint_value, hazard, sides)
    after = [(i, i + 1) for i in range(n_age - 1)]
    before = [(i + 1, i) for i in range(n_age - 1)]
    if sides == 1:
        near = [lax.ppermute(edge[0], "age", after + before)]
    else:
        near = [lax.ppermute(x, "age", pairs) for x, pairs in zip(edge, (after, before))]
    *q, u4, send = pack(at, u4, jnp.asarray(send, bf16), ranks, extra)
    q = pack_edges(send, near, q, ranks, sides)
    arrived = [lax.ppermute(x, "cheb", list(pairs)) for x, (pairs, _) in zip(q, slots)]
    z, beside, take = local(at, u4, hazard, diffusion, drift, tables, near, sides)
    z, top, bottom = outer_rows(z, beside, take, arrived, ranks, sides, wears, ages)
    up = lax.ppermute(bottom, "wear", [(i, i + 1) for i in range(n_wear - 1)])
    down = lax.ppermute(top, "wear", [(i + 1, i) for i in range(n_wear - 1)])
    z = section(flags, z, beside, take, arrived, ranks, sides, wears, ages)
    return run_substeps(flags, z, wear_speed.reshape(1, size), up, down, sides, wears, ages)


def solution(mesh):
    placed = (P("wear", "age", "cheb"), P(), P(), P("cheb"), P("wear", "age"))
    return jax.shard_map(
        body, mesh=mesh, in_specs=placed, out_specs=P("wear", "age", "cheb"), check_vma=False
    )
```

```python
import functools

import jax
import jax.numpy as jnp
import numpy as np
from jax import lax
from jax.experimental import pallas as pl
from jax.experimental.pallas import tpu as pltpu
from jax.sharding import PartitionSpec as P

SUBSTEPS = 4
HALO = SUBSTEPS

age_courant = 0.4
wear_spread = 0.1
coupling = 0.05
GAIN = 1.0 / coupling
START = coupling**SUBSTEPS

f32 = jnp.float32
bf16 = jnp.bfloat16


def operators(points):
    modes = np.arange(points)[:, None]
    nodes = np.arange(points)[None, :]
    angles = (modes * (2 * nodes + 1)) % (4 * points) * (np.pi / (2 * points))
    cosine, sine = np.cos(angles), np.sin(angles)
    analysis = np.where(modes == 0, 1.0, 2.0) / points * cosine
    wavenumber = modes / points
    return (-(wavenumber**2) * cosine).T @ analysis, (wavenumber * sine).T @ analysis


def arrived_rows(rank):
    return -(-rank // 16) * 16


@functools.lru_cache(maxsize=None)
def factors(points, devices):
    second, first = operators(points)
    size = points // devices
    parts = [slice(b * size, (b + 1) * size) for b in range(devices)]
    slots, found = [], {}
    for shift in range(1, devices):
        pairs, most = [], 0
        for c in range(devices):
            b = c ^ shift if devices & (devices - 1) == 0 else (c + shift) % devices
            joint = np.concatenate([second[parts[b], parts[c]], first[parts[b], parts[c]]])
            _, sizes, rows = np.linalg.svd(joint, full_matrices=False)
            rank = int((sizes > joint.shape[0] * np.finfo(np.float64).eps).sum())
            rank = -(-rank // 8) * 8
            basis = rows[:rank]
            found[c, b] = (basis, second[parts[b], parts[c]] @ basis.T, first[parts[b], parts[c]] @ basis.T)
            pairs.append((c, b))
            most = max(most, rank)
        slots.append((tuple(pairs), most))
    send = np.zeros((devices, sum(rank for _, rank in slots), size))
    wide = sum(arrived_rows(rank) for _, rank in slots)
    take_second = np.zeros((devices, 2, wide, size))
    take_first = np.zeros((devices, 2, wide, size))
    at = row = 0
    for pairs, rank in slots:
        whole = rank // 16 * 16
        for c, b in pairs:
            basis, left_second, left_first = (
                np.pad(x, ((0, rank - len(found[c, b][0])), (0, 0))) for x in (found[c, b][0], found[c, b][1].T, found[c, b][2].T)
            )
            send[c, at : at + rank] = basis
            for half in range(2):
                for take, left in ((take_second, left_second), (take_first, left_first)):
                    take[b, half, row : row + whole] = left[:whole]
                    place = row + whole + half * (rank - whole)
                    take[b, half, place : place + rank - whole] = left[whole:]
        at += rank
        row += arrived_rows(rank)
    own_second = np.stack([second[p, p].T for p in parts])
    own_first = np.stack([first[p, p].T for p in parts])
    return slots, send, take_second, take_first, own_second, own_first


ANY = pl.BlockSpec(memory_space=pl.ANY)
VMEM = pl.BlockSpec(memory_space=pltpu.VMEM)
SMEM = pl.BlockSpec(memory_space=pltpu.SMEM)
FIRST_WEAR, LAST_WEAR, FIRST_AGE, LAST_AGE, CHEB = range(5)
ROW0 = 16
HAZARD_ROWS = 16


def in_hbm(x):
    return pltpu.with_memory_space_constraint(x, pltpu.HBM)


def in_vmem(x):
    return pltpu.with_memory_space_constraint(x, pltpu.VMEM)


def params(mebibytes):
    return pltpu.CompilerParams(vmem_limit_bytes=mebibytes * 2**20)


def cost(flops, bytes_accessed):
    return pl.CostEstimate(flops=flops, bytes_accessed=bytes_accessed, transcendentals=0)


def edge_kernel(sides, flag_ref, u_hbm, hazard_hbm, *refs):
    out_refs, (tiles, hazard, sem) = refs[:sides], refs[sides:]
    wears, ages, size = u_hbm.shape
    copies = [pltpu.make_async_copy(hazard_hbm, hazard, sem.at[sides])]
    for i in range(sides):
        if sides == 1:
            start = pl.multiple_of(jnp.where(flag_ref[FIRST_AGE] == 1, ages - 8, 0), 8)
        else:
            start = (ages - 8, 0)[i]
        copies.append(pltpu.make_async_copy(u_hbm.at[:, pl.ds(start, 8)], tiles.at[i], sem.at[i]))
    for copy in copies:
        copy.start()
    for copy in copies:
        copy.wait()
    by_age = jnp.transpose(hazard[...])
    last, early = by_age[ages - HALO :], by_age[:HALO]
    for i, out_ref in enumerate(out_refs):
        for w in range(0, wears, 4):
            late = [tiles[i, w + j, 8 - HALO :] for j in range(4)]
            soon = [tiles[i, w + j, :HALO] for j in range(4)]
            late, soon = jnp.concatenate(late, axis=0), jnp.concatenate(soon, axis=0)
            if sides == 1:
                cells = jnp.where(flag_ref[FIRST_AGE] == 1, late, soon)
            else:
                cells = (late, soon)[i]
            out_ref[w * HALO : (w + 4) * HALO] = cells.astype(bf16)
        if sides == 1:
            exact = jnp.where(flag_ref[FIRST_AGE] == 1, last, early)
        else:
            exact = (last, early)[i]
        high = exact.astype(bf16).astype(f32)
        rows = jnp.concatenate([high, exact - high, jnp.zeros((HAZARD_ROWS - 2 * HALO, wears), f32)], axis=0)
        rows = jnp.concatenate([rows, jnp.zeros((HAZARD_ROWS, size - wears), f32)], axis=1)
        out_ref[wears * HALO :] = rows.astype(bf16)


def edges(flags, u, hazard, sides):
    wears, ages, size = u.shape
    return pl.pallas_call(
        functools.partial(edge_kernel, sides),
        in_specs=[SMEM, ANY, ANY],
        out_specs=[VMEM] * sides,
        out_shape=[jax.ShapeDtypeStruct((wears * HALO + HAZARD_ROWS, size), bf16)] * sides,
        scratch_shapes=[
            pltpu.VMEM((sides, wears, 8, size), f32),
            pltpu.VMEM((wears, ages), f32),
            pltpu.SemaphoreType.DMA((sides + 1,)),
        ],
        compiler_params=params(16),
        cost_estimate=cost(0, 8 * wears * 8 * size),
        name="age_edges",
    )(flags, in_hbm(u), in_hbm(hazard))


def pack_rows(ranks, halves):
    packed, row = [], 0
    for rank in ranks:
        cut = row + rank // 16 * 16
        pieces = [h[row:cut] for h in halves if cut > row]
        pieces += [h[cut : row + rank] for h in halves if cut < row + rank]
        packed.append(jnp.concatenate(pieces, axis=0).astype(bf16))
        row += rank
    return packed


def analyse(table, cells):
    return lax.dot_general(table, cells, (((1,), (1,)), ((), ())), preferred_element_type=f32)


def pack_kernel(ranks, flag_ref, u_hbm, send_hbm, *refs):
    q_refs, (u_ref, send, send_sem, u_sem) = refs[: len(ranks)], refs[len(ranks) :]
    _, wears, ages, size = u_ref.shape
    chunk = 4
    table = pltpu.make_async_copy(send_hbm.at[flag_ref[CHEB]], send, send_sem)
    table.start()
    loads = []
    for g in range(wears // chunk):
        rows = pl.ds(g * chunk, chunk)
        loads.append(pltpu.make_async_copy(u_hbm.at[:, rows], u_ref.at[:, rows], u_sem.at[g]))
        loads[-1].start()
    table.wait()
    for g in range(wears // chunk):
        loads[g].wait()
        halves = [
            analyse(send[...], u_ref[half, g * chunk : (g + 1) * chunk].reshape(chunk * ages, size).astype(bf16))
            for half in range(2)
        ]
        for q_ref, rows in zip(q_refs, pack_rows(ranks, halves)):
            q_ref[:, g * chunk * ages : (g + 1) * chunk * ages] = rows


def pack(flags, u4, send, ranks, extra):
    _, wears, ages, size = u4.shape
    cells = wears * ages
    return pl.pallas_call(
        functools.partial(pack_kernel, ranks),
        in_specs=[SMEM, ANY, ANY],
        out_specs=[VMEM] * (len(ranks) + 2),
        out_shape=[jax.ShapeDtypeStruct((2 * r, cells + extra), bf16) for r in ranks]
        + [pltpu.VMEM(u4.shape, f32), pltpu.VMEM(send.shape[1:], bf16)],
        scratch_shapes=[pltpu.SemaphoreType.DMA, pltpu.SemaphoreType.DMA((wears // 4,))],
        compiler_params=params(16),
        cost_estimate=cost(4 * cells * sum(ranks) * size, 8 * cells * size),
        name="pack_coefficients",
    )(flags, in_hbm(u4), in_hbm(send))


def pack_edges_kernel(ranks, sides, send_ref, *refs):
    edge_refs, q_refs = refs[:sides], refs[sides + len(ranks) :]
    count = edge_refs[0].shape[0] - HAZARD_ROWS
    halves = []
    for half in range(2):
        cells = [r[half * count // 2 : (half + 1) * count // 2] for r in edge_refs]
        halves.append(analyse(send_ref[...], jnp.concatenate(cells, axis=0)))
    for q_ref, rows in zip(q_refs, pack_rows(ranks, halves)):
        q_ref[:, q_ref.shape[1] - rows.shape[1] :] = rows


def pack_edges(send, near, q, ranks, sides):
    return pl.pallas_call(
        functools.partial(pack_edges_kernel, ranks, sides),
        in_specs=[VMEM] * (1 + sides + len(ranks)),
        out_specs=[VMEM] * len(ranks),
        out_shape=[jax.ShapeDtypeStruct(x.shape, x.dtype) for x in q],
        input_output_aliases={1 + sides + i: i for i in range(len(ranks))},
        compiler_params=params(16),
        cost_estimate=cost(0, 2**18),
        name="pack_edges",
    )(in_vmem(send), *near, *q)


def local_kernel(sides, flag_ref, u_ref, hazard_hbm, diffusion_hbm, drift_hbm, second_hbm, first_hbm, take_second_hbm,
                 take_first_hbm, *refs):
    edge_refs, refs = refs[:sides], refs[sides:]
    z, beside, ends, take, hazard, diffusion, drift, second, first, own, take_second, take_first, sem = refs
    halves, rows, _, _ = z.shape
    _, wears, ages, size = u_ref.shape
    at = flag_ref[CHEB]
    moves = (
        (second_hbm.at[at], second), (first_hbm.at[at], first), (diffusion_hbm.at[at], diffusion),
        (drift_hbm.at[at], drift), (hazard_hbm, hazard), (take_second_hbm.at[at], take_second),
        (take_first_hbm.at[at], take_first),
    )
    copies = [pltpu.make_async_copy(src, dst, sem.at[i]) for i, (src, dst) in enumerate(moves)]
    for copy in copies:
        copy.start()
    for l in range(halves):
        zero = jnp.zeros((rows, 16, 128), f32)
        z[l, :, :ROW0, :] = zero
        z[l, :, ROW0 + ages :, :] = zero
    for copy in copies:
        copy.wait()
    scaled, moved = START * diffusion[...], START * drift[...]
    own[...] = (second[...] * scaled + first[...] * moved).astype(bf16)
    take[...] = (take_second[...] * scaled + take_first[...] * moved).astype(bf16)
    keep = jnp.transpose(START - START * hazard[...])
    chunk = 4
    for w in range(0, 2 * wears, chunk):
        half, v = divmod(w, wears)
        u = u_ref[half, v : v + chunk].reshape(chunk * ages, size)
        rate = jnp.dot(u.astype(bf16), own[...], preferred_element_type=f32)
        for i in range(chunk):
            cells = slice(i * ages, (i + 1) * ages)
            value = rate[cells] + keep[:, w + i : w + i + 1] * u[cells]
            for l in range(halves):
                z[l, HALO + w + i, ROW0 : ROW0 + ages, :] = value[:, l * 128 : (l + 1) * 128]
            for e, start in enumerate((0, 2 * wears - HALO)):
                if start <= w + i < start + HALO:
                    ends[e, (w + i - start) * ages : (w + i - start + 1) * ages] = value
    for s, ref in enumerate(edge_refs):
        count = 2 * wears * HALO
        parts = ref[count:].astype(f32)
        near = START - START * (parts[:HALO, : 2 * wears] + parts[HALO : 2 * HALO, : 2 * wears])
        near = jnp.concatenate([near, near], axis=0)
        for w in range(0, 2 * wears, 4):
            place = slice(w * HALO, (w + 4) * HALO)
            u = ref[place]
            rate = jnp.dot(u, own[...], preferred_element_type=f32)
            columns = [
                jnp.broadcast_to(near[:HALO, w + j : w + j + 1], (HALO, size)) for j in range(4)
            ]
            beside[s, place] = rate + jnp.concatenate(columns, axis=0) * u.astype(f32)


def local(flags, u4, hazard, diffusion, drift, tables, near, sides):
    _, wears, ages, size = u4.shape
    cells = 2 * wears * ages
    wide = tables[2].shape[2]
    return pl.pallas_call(
        functools.partial(local_kernel, sides),
        in_specs=[SMEM, VMEM] + [ANY] * 7 + [VMEM] * sides,
        out_specs=[VMEM] * 4,
        out_shape=[
            pltpu.VMEM((size // 128, 2 * wears + 2 * HALO, ages + 32, 128), f32),
            pltpu.VMEM((sides, 2 * wears * HALO, size), f32),
            pltpu.VMEM((2, HALO * ages, size), f32),
            pltpu.VMEM((2, wide, size), bf16),
        ],
        scratch_shapes=[
            pltpu.VMEM(hazard.shape, f32),
            pltpu.VMEM((1, size), f32),
            pltpu.VMEM((1, size), f32),
            pltpu.VMEM((size, size), f32),
            pltpu.VMEM((size, size), f32),
            pltpu.VMEM((size, size), bf16),
            pltpu.VMEM((2, wide, size), f32),
            pltpu.VMEM((2, wide, size), f32),
            pltpu.SemaphoreType.DMA((7,)),
        ],
        compiler_params=params(16),
        cost_estimate=cost(2 * cells * size * size, 8 * cells * size),
        name="local_rate",
    )(flags, in_vmem(u4), *[in_hbm(x) for x in (hazard, diffusion, drift, *tables)], *near)


def arrived_tiles(ranks, q_refs, half, columns):
    tiles = []
    for rank, q in zip(ranks, q_refs):
        cut = rank // 16 * 16
        if cut:
            tiles.append(q[half * cut : (half + 1) * cut, columns])
        if rank > cut:
            tiles.append(q[2 * cut : 2 * rank, columns])
    return jnp.concatenate(tiles, axis=0)


def distant(ranks, q_refs, take_ref, half, columns):
    return lax.dot_general(
        arrived_tiles(ranks, q_refs, half, columns), take_ref[half], (((0,), (0,)), ((), ())),
        preferred_element_type=f32,
    )


def edge_columns(sides, main, each):
    return [slice(main + s * each, main + (s + 1) * each) for s in range(sides)]


def rows_kernel(ranks, sides, wears, ages, ends_ref, beside_ref, take_ref, *refs):
    q_refs, out_refs = refs[: len(ranks)], refs[len(ranks) :]
    main, each = wears // 2 * ages, wears // 2 * HALO
    corner = HALO * HALO
    for half, (start, out_ref) in enumerate(zip((0, wears - HALO), out_refs)):
        v = (start - half * wears // 2) * ages
        rate = distant(ranks, q_refs, take_ref, half, slice(v, v + HALO * ages))
        out_ref[: HALO * ages] = (rate + ends_ref[half]).astype(bf16)
        for s, columns in enumerate(edge_columns(sides, main, each)):
            first = 0 if half == 0 else each - corner
            rate = distant(ranks, q_refs, take_ref, half, columns)[first : first + corner]
            place = slice(start * HALO, start * HALO + corner)
            row = HALO * ages + s * corner
            out_ref[row : row + corner] = (rate + beside_ref[s, place]).astype(bf16)


def outer_rows(ends, beside, take, q, ranks, sides, wears, ages):
    size = ends.shape[-1]
    message = jax.ShapeDtypeStruct((HALO * ages + sides * HALO * HALO, size), bf16)
    return pl.pallas_call(
        functools.partial(rows_kernel, ranks, sides, wears, ages),
        in_specs=[VMEM] * (3 + len(ranks)),
        out_specs=[VMEM] * 2,
        out_shape=[message, message],
        compiler_params=params(16),
        cost_estimate=cost(2 * 8 * ages * take.shape[1] * size, 2**20),
        name="outer_rows",
    )(in_vmem(ends), in_vmem(beside), in_vmem(take), *q)


def section_kernel(ranks, sides, wears, ages, flag_ref, z_in, beside_ref, take_ref, *refs):
    q_refs, (z,) = refs[: len(ranks)], refs[len(ranks) :]
    halves = z.shape[0]
    main, each = wears // 2 * ages, wears // 2 * HALO
    chunk = 4
    for w in range(0, wears, chunk):
        half, v = divmod(w, wears // 2)
        rate = distant(ranks, q_refs, take_ref, half, slice(v * ages, (v + chunk) * ages))
        for i in range(chunk):
            for l in range(halves):
                z[l, HALO + w + i, ROW0 : ROW0 + ages, :] = (
                    z_in[l, HALO + w + i, ROW0 : ROW0 + ages, :]
                    + rate[i * ages : (i + 1) * ages, l * 128 : (l + 1) * 128]
                )
    has = [jnp.where(flag_ref[FIRST_AGE + i] == 1, 0.0, 1.0).astype(f32) for i in range(2)]
    for s in range(sides):
        for half in range(2):
            columns = edge_columns(sides, main, each)[s]
            place = slice(half * each, (half + 1) * each)
            cells = distant(ranks, q_refs, take_ref, half, columns) + beside_ref[s, place]
            for i, column in ((0, ROW0 - HALO), (1, ROW0 + ages)):
                if sides == 1 or s == i:
                    part = cells * has[i]
                    for w in range(wears // 2):
                        for l in range(halves):
                            z[l, HALO + half * wears // 2 + w, column : column + HALO, :] = part[
                                w * HALO : (w + 1) * HALO, l * 128 : (l + 1) * 128
                            ]


def section(flags, z, beside, take, q, ranks, sides, wears, ages):
    size = z.shape[0] * 128
    cells = wears * ages
    return pl.pallas_call(
        functools.partial(section_kernel, ranks, sides, wears, ages),
        in_specs=[SMEM] + [VMEM] * (3 + len(ranks)),
        out_specs=VMEM,
        out_shape=pltpu.VMEM(z.shape, f32),
        input_output_aliases={1: 0},
        compiler_params=params(16),
        cost_estimate=cost(2 * cells * take.shape[1] * size, 8 * cells * size),
        name="section",
    )(flags, z, in_vmem(beside), in_vmem(take), *q)


def lane_terms(speed_ref, l):
    speed = speed_ref[0:1, l * 128 : (l + 1) * 128]
    stay = GAIN * (1.0 - age_courant - 2.0 * wear_spread - speed)
    worn = GAIN * (speed + wear_spread)
    return stay, worn


def row_terms(src, l, w, lo, hi, stay, worn):
    t = src[l, w, lo:hi, :]
    older = src[l, w, lo + 1 : hi + 1, :]
    slope = older - src[l, w, lo - 1 : hi - 1, :]
    centre = stay * t + (GAIN * age_courant) * older
    less = (t - slope) + t
    return centre, worn * t + slope, less


def rows_step(src, l, start, stop, lo, hi, factors, put, unroll):
    def step(w, carry):
        partial, less = carry
        centre, more, new_less = row_terms(src, l, w + 1, lo, hi, *factors)
        put(w, partial + more)
        return centre + less, new_less

    _, _, less0 = row_terms(src, l, start - 1, lo, hi, *factors)
    centre1, _, less1 = row_terms(src, l, start, lo, hi, *factors)
    lax.fori_loop(start, stop, step, (centre1 + less0, less1), unroll=unroll)


def put_in(dst, l, lo, hi, keeps, factor=None):
    def put(w, out):
        if factor is not None:
            out = out * factor(w)
        if keeps is None:
            dst[l, w, lo:hi, :] = out
        else:
            dst[l, w, lo : lo + 8, :] = out[:8] * keeps[0]
            dst[l, w, lo + 8 : hi - 8, :] = out[8:-8]
            dst[l, w, hi - 8 : hi, :] = out[-8:] * keeps[1]

    return put


def by_sides(sides, flag_ref, ages, run):
    if sides == 1:
        pl.when(flag_ref[FIRST_AGE] == 1)(lambda: run(ROW0, ROW0 + ages + 8, None))
        pl.when(flag_ref[FIRST_AGE] == 0)(lambda: run(ROW0 - 8, ROW0 + ages, None))
    else:
        has = [jnp.where(flag_ref[FIRST_AGE + i] == 1, 0.0, 1.0).astype(f32) for i in range(2)]
        run(ROW0 - 8, ROW0 + ages + 8, [jnp.zeros((8, 128), f32) + h for h in has])


def inner_kernel(sides, flag_ref, z0, speed_ref, o_ref, z1, z2, z3, stage, out_sem):
    halves, rows, _, _ = z0.shape
    count, ages = stage.shape[:2]
    fields = (z0, z1, z2, z3)

    def run(low, high, keeps):
        for z in fields[1:]:
            for l in range(halves):
                if low == ROW0:
                    z[l, :, ROW0 - 8 : ROW0, :] = jnp.zeros((rows, 8, 128), f32)
                if high == ROW0 + ages:
                    z[l, :, high : high + 8, :] = jnp.zeros((rows, 8, 128), f32)
        for k in range(1, SUBSTEPS):
            for l in range(halves):
                rows_step(
                    fields[k - 1], l, HALO + k, rows - HALO - k, low, high, lane_terms(speed_ref, l),
                    put_in(fields[k], l, low, high, keeps), 2,
                )
        stores = []
        first = HALO + SUBSTEPS
        bounds = [0, count * 3 // 7, count * 5 // 7, count * 6 // 7, count]
        for a, b in zip(bounds, bounds[1:]):
            for l in range(halves):
                def put(w, out, l=l):
                    stage[w - first, :, l * 128 : (l + 1) * 128] = out

                rows_step(
                    fields[-1], l, first + a, first + b, ROW0, ROW0 + ages, lane_terms(speed_ref, l), put, 4,
                )
            copy = pltpu.make_async_copy(
                stage.at[pl.ds(a, b - a)], o_ref.at[pl.ds(SUBSTEPS + a, b - a)], out_sem.at[len(stores)]
            )
            copy.start()
            stores.append(copy)
        for copy in stores:
            copy.wait()

    by_sides(sides, flag_ref, ages, run)


def inner_substeps(flags, z, speed, sides, wears, ages):
    size = z.shape[0] * 128
    shape = (wears, ages, size)
    return pl.pallas_call(
        functools.partial(inner_kernel, sides),
        out_shape=[jax.ShapeDtypeStruct(shape, f32)] + [pltpu.VMEM(z.shape, f32)] * 3,
        in_specs=[SMEM] + [VMEM] * 2,
        out_specs=[ANY] + [VMEM] * 3,
        scratch_shapes=[pltpu.VMEM((wears - 2 * SUBSTEPS, ages, size), f32), pltpu.SemaphoreType.DMA((4,))],
        compiler_params=params(16),
        cost_estimate=cost(10 * SUBSTEPS * wears * ages * size, 8 * wears * ages * size),
        name="inner_substeps",
    )(flags, in_vmem(z), speed)


def outer_kernel(sides, flag_ref, o_in, z0_in, z1_in, z2_in, z3_in, speed_ref, up_ref, down_ref, o_ref, z0, z1, z2, z3,
                 stage, out_sem):
    del o_in, z0_in, z1_in, z2_in, z3_in
    halves, rows, _, _ = z0.shape
    wears, ages = rows - 2 * HALO, stage.shape[2]
    fields = (z0, z1, z2, z3)
    has = [jnp.where(flag_ref[FIRST_AGE + i] == 1, 0.0, 1.0).astype(f32) for i in range(2)]
    near = [jnp.where(flag_ref[FIRST_WEAR + i] == 1, 0.0, 1.0).astype(f32) for i in range(2)]
    for l in range(halves):
        lanes = pl.ds(l * 128, 128)
        for e, (ref, at) in enumerate(((up_ref, 0), (down_ref, HALO + wears))):
            values = ref[:, lanes].astype(f32) * near[e]
            z0[l, at : at + HALO, ROW0 : ROW0 + ages, :] = values[: HALO * ages].reshape(HALO, ages, 128)
            for s in range(sides):
                corner = values[HALO * (ages + s * HALO) : HALO * (ages + (s + 1) * HALO)]
                for i, column in ((0, ROW0 - HALO), (1, ROW0 + ages)):
                    if sides == 1 or s == i:
                        part = corner * has[i]
                        for w in range(HALO):
                            z0[l, at + w, column : column + HALO, :] = part[w * HALO : (w + 1) * HALO]

    def run(low, high, keeps):
        for k in range(1, SUBSTEPS):
            for l in range(halves):
                for e, start in enumerate((k, rows - HALO - k)):
                    beyond = (lambda w: w < HALO, lambda w: w >= HALO + wears)[e]
                    rows_step(
                        fields[k - 1], l, start, start + HALO, low, high, lane_terms(speed_ref, l),
                        put_in(
                            fields[k], l, low, high, keeps,
                            lambda w, e=e, beyond=beyond: jnp.where(beyond(w), near[e], 1.0).astype(f32),
                        ), 4,
                    )
        stores = []
        for e, start in enumerate((HALO, rows - 2 * HALO)):
            for l in range(halves):
                def put(w, out, l=l, e=e, start=start):
                    stage[e, w - start, :, l * 128 : (l + 1) * 128] = out

                rows_step(fields[-1], l, start, start + HALO, ROW0, ROW0 + ages, lane_terms(speed_ref, l), put, 4)
            copy = pltpu.make_async_copy(stage.at[e], o_ref.at[pl.ds(start - HALO, HALO)], out_sem.at[e])
            copy.start()
            stores.append(copy)
        for copy in stores:
            copy.wait()

    by_sides(sides, flag_ref, ages, run)


def outer_substeps(flags, o, fields, speed, up, down, sides):
    wears, ages, size = o.shape
    return pl.pallas_call(
        functools.partial(outer_kernel, sides),
        out_shape=[jax.ShapeDtypeStruct(o.shape, f32)] + [pltpu.VMEM(z.shape, f32) for z in fields],
        in_specs=[SMEM, ANY] + [VMEM] * 7,
        out_specs=[ANY] + [VMEM] * 4,
        scratch_shapes=[pltpu.VMEM((2, HALO, ages, size), f32), pltpu.SemaphoreType.DMA((2,))],
        input_output_aliases={1 + i: i for i in range(5)},
        compiler_params=params(16),
        cost_estimate=cost(20 * SUBSTEPS * 2 * HALO * ages * size, 2**20),
        name="outer_substeps",
    )(flags, o, *fields, speed, up, down)[0]


def body(adjoint_value, load_diffusion, load_drift, wear_speed, hazard):
    wears, ages, size = adjoint_value.shape
    points = load_diffusion.shape[0]
    devices = points // size
    slots, send, take_second, take_first, own_second, own_first = factors(points, devices)
    ranks = tuple(rank for _, rank in slots)
    cheb = lax.axis_index("cheb")
    wear, age = lax.axis_index("wear"), lax.axis_index("age")
    n_wear, n_age = lax.axis_size("wear"), lax.axis_size("age")
    flags = jnp.stack([wear == 0, wear == n_wear - 1, age == 0, age == n_age - 1, cheb]).astype(jnp.int32)
    sides = 1 if n_age == 2 else 2
    extra = sides * wears // 2 * HALO
    u4 = adjoint_value.reshape(2, wears // 2, ages, size)
    diffusion = load_diffusion.reshape(devices, 1, size)
    drift = load_drift.reshape(devices, 1, size)
    tables = [jnp.asarray(t, f32) for t in (own_second, own_first, take_second, take_first)]

    def ring(n):
        after = [(i, (i + 1) % n) for i in range(n)]
        return after, [(j, i) for i, j in after]

    edge = edges(flags, adjoint_value, hazard, sides)
    near = [lax.ppermute(x, "age", pairs) for x, pairs in zip(edge, ring(n_age))]
    *q, u4, send = pack(flags, u4, jnp.asarray(send, bf16), ranks, extra)
    q = pack_edges(send, near, q, ranks, sides)
    arrived = [lax.ppermute(x, "cheb", list(pairs)) for x, (pairs, _) in zip(q, slots)]
    z, beside, ends, take = local(flags, u4, hazard, diffusion, drift, tables, near, sides)
    top, bottom = outer_rows(ends, beside, take, arrived, ranks, sides, wears, ages)
    after, before = ring(n_wear)
    up, down = lax.ppermute(bottom, "wear", after), lax.ppermute(top, "wear", before)
    z = section(flags, z, beside, take, arrived, ranks, sides, wears, ages)
    speed = wear_speed.reshape(1, size)
    o, *fields = inner_substeps(flags, z, speed, sides, wears, ages)
    return outer_substeps(flags, o, [z, *fields], speed, up, down, sides)


def solution(mesh):
    placed = (P("wear", "age", "cheb"), P(), P(), P("cheb"), P("wear", "age"))
    return jax.shard_map(
        body, mesh=mesh, in_specs=placed, out_specs=P("wear", "age", "cheb"), check_vma=False
    )
```

```python
import functools

import jax
import jax.numpy as jnp
import numpy as np
from jax import lax
from jax.experimental import pallas as pl
from jax.experimental.pallas import tpu as pltpu
from jax.sharding import PartitionSpec as P

SUBSTEPS = 4
HALO = SUBSTEPS

age_courant = 0.4
wear_spread = 0.1
coupling = 0.05
GAIN = 1.0 / coupling
START = coupling**SUBSTEPS

f32 = jnp.float32
bf16 = jnp.bfloat16


def operators(points):
    modes = np.arange(points)[:, None]
    nodes = np.arange(points)[None, :]
    angles = (modes * (2 * nodes + 1)) % (4 * points) * (np.pi / (2 * points))
    cosine, sine = np.cos(angles), np.sin(angles)
    analysis = np.where(modes == 0, 1.0, 2.0) / points * cosine
    wavenumber = modes / points
    return (-(wavenumber**2) * cosine).T @ analysis, (wavenumber * sine).T @ analysis


def arrived_rows(rank):
    return -(-rank // 16) * 16


@functools.lru_cache(maxsize=None)
def factors(points, devices):
    second, first = operators(points)
    size = points // devices
    parts = [slice(b * size, (b + 1) * size) for b in range(devices)]
    slots, found = [], {}
    for shift in range(1, devices):
        pairs, most = [], 0
        for c in range(devices):
            b = c ^ shift if devices & (devices - 1) == 0 else (c + shift) % devices
            joint = np.concatenate([second[parts[b], parts[c]], first[parts[b], parts[c]]])
            _, sizes, rows = np.linalg.svd(joint, full_matrices=False)
            rank = int((sizes > joint.shape[0] * np.finfo(np.float64).eps).sum())
            rank = -(-rank // 8) * 8
            basis = rows[:rank]
            found[c, b] = (basis, second[parts[b], parts[c]] @ basis.T, first[parts[b], parts[c]] @ basis.T)
            pairs.append((c, b))
            most = max(most, rank)
        slots.append((tuple(pairs), most))
    send = np.zeros((devices, sum(rank for _, rank in slots), size))
    wide = sum(arrived_rows(rank) for _, rank in slots)
    take_second = np.zeros((devices, 2, wide, size))
    take_first = np.zeros((devices, 2, wide, size))
    at = row = 0
    for pairs, rank in slots:
        whole = rank // 16 * 16
        for c, b in pairs:
            basis, left_second, left_first = (
                np.pad(x, ((0, rank - len(found[c, b][0])), (0, 0))) for x in (found[c, b][0], found[c, b][1].T, found[c, b][2].T)
            )
            send[c, at : at + rank] = basis
            for half in range(2):
                for take, left in ((take_second, left_second), (take_first, left_first)):
                    take[b, half, row : row + whole] = left[:whole]
                    place = row + whole + half * (rank - whole)
                    take[b, half, place : place + rank - whole] = left[whole:]
        at += rank
        row += arrived_rows(rank)
    own_second = np.stack([second[p, p].T for p in parts])
    own_first = np.stack([first[p, p].T for p in parts])
    return slots, send, take_second, take_first, own_second, own_first


ANY = pl.BlockSpec(memory_space=pl.ANY)
VMEM = pl.BlockSpec(memory_space=pltpu.VMEM)
SMEM = pl.BlockSpec(memory_space=pltpu.SMEM)
ROW0 = 16
HAZARD_ROWS = 16


def at_end(axis, last):
    return lax.axis_index(axis) == (lax.axis_size(axis) - 1 if last else 0)


def in_hbm(x):
    return pltpu.with_memory_space_constraint(x, pltpu.HBM)


def in_vmem(x):
    return pltpu.with_memory_space_constraint(x, pltpu.VMEM)


def params(mebibytes):
    return pltpu.CompilerParams(vmem_limit_bytes=mebibytes * 2**20)


def cost(flops, bytes_accessed):
    return pl.CostEstimate(flops=flops, bytes_accessed=bytes_accessed, transcendentals=0)


def edge_kernel(sides, u_hbm, hazard_hbm, *refs):
    out_refs, (tiles, hazard, sem) = refs[:sides], refs[sides:]
    wears, ages, size = u_hbm.shape
    copies = [pltpu.make_async_copy(hazard_hbm, hazard, sem.at[sides])]
    for i in range(sides):
        if sides == 1:
            start = pl.multiple_of(jnp.where(at_end("age", False), ages - 8, 0), 8)
        else:
            start = (ages - 8, 0)[i]
        copies.append(pltpu.make_async_copy(u_hbm.at[:, pl.ds(start, 8)], tiles.at[i], sem.at[i]))
    for copy in copies:
        copy.start()
    for copy in copies:
        copy.wait()
    by_age = jnp.transpose(hazard[...])
    last, early = by_age[ages - HALO :], by_age[:HALO]
    for i, out_ref in enumerate(out_refs):
        for w in range(0, wears, 4):
            late = [tiles[i, w + j, 8 - HALO :] for j in range(4)]
            soon = [tiles[i, w + j, :HALO] for j in range(4)]
            late, soon = jnp.concatenate(late, axis=0), jnp.concatenate(soon, axis=0)
            if sides == 1:
                cells = jnp.where(at_end("age", False), late, soon)
            else:
                cells = (late, soon)[i]
            out_ref[w * HALO : (w + 4) * HALO] = cells.astype(bf16)
        if sides == 1:
            exact = jnp.where(at_end("age", False), last, early)
        else:
            exact = (last, early)[i]
        high = exact.astype(bf16).astype(f32)
        rows = jnp.concatenate([high, exact - high, jnp.zeros((HAZARD_ROWS - 2 * HALO, wears), f32)], axis=0)
        rows = jnp.concatenate([rows, jnp.zeros((HAZARD_ROWS, size - wears), f32)], axis=1)
        out_ref[wears * HALO :] = rows.astype(bf16)


def edges(u, hazard, sides):
    wears, ages, size = u.shape
    return pl.pallas_call(
        functools.partial(edge_kernel, sides),
        in_specs=[ANY, ANY],
        out_specs=[VMEM] * sides,
        out_shape=[jax.ShapeDtypeStruct((wears * HALO + HAZARD_ROWS, size), bf16)] * sides,
        scratch_shapes=[
            pltpu.VMEM((sides, wears, 8, size), f32),
            pltpu.VMEM((wears, ages), f32),
            pltpu.SemaphoreType.DMA((sides + 1,)),
        ],
        compiler_params=params(16),
        cost_estimate=cost(0, 8 * wears * 8 * size),
        name="age_edges",
    )(in_hbm(u), in_hbm(hazard))


def pack_rows(ranks, halves):
    packed, row = [], 0
    for rank in ranks:
        cut = row + rank // 16 * 16
        pieces = [h[row:cut] for h in halves if cut > row]
        pieces += [h[cut : row + rank] for h in halves if cut < row + rank]
        packed.append(jnp.concatenate(pieces, axis=0).astype(bf16))
        row += rank
    return packed


def analyse(table, cells):
    return lax.dot_general(table, cells, (((1,), (1,)), ((), ())), preferred_element_type=f32)


def pack_kernel(ranks, u_hbm, send_hbm, *refs):
    q_refs, (u_ref, send, send_sem, u_sem) = refs[: len(ranks)], refs[len(ranks) :]
    _, wears, ages, size = u_ref.shape
    chunk = 4
    table = pltpu.make_async_copy(send_hbm.at[lax.axis_index("cheb")], send, send_sem)
    table.start()
    loads = []
    for g in range(wears // chunk):
        rows = pl.ds(g * chunk, chunk)
        loads.append(pltpu.make_async_copy(u_hbm.at[:, rows], u_ref.at[:, rows], u_sem.at[g]))
        loads[-1].start()
    table.wait()
    for g in range(wears // chunk):
        loads[g].wait()
        halves = [
            analyse(send[...], u_ref[half, g * chunk : (g + 1) * chunk].reshape(chunk * ages, size).astype(bf16))
            for half in range(2)
        ]
        for q_ref, rows in zip(q_refs, pack_rows(ranks, halves)):
            q_ref[:, g * chunk * ages : (g + 1) * chunk * ages] = rows


def pack(u4, send, ranks, extra):
    _, wears, ages, size = u4.shape
    cells = wears * ages
    return pl.pallas_call(
        functools.partial(pack_kernel, ranks),
        in_specs=[ANY, ANY],
        out_specs=[VMEM] * (len(ranks) + 2),
        out_shape=[jax.ShapeDtypeStruct((2 * r, cells + extra), bf16) for r in ranks]
        + [pltpu.VMEM(u4.shape, f32), pltpu.VMEM(send.shape[1:], bf16)],
        scratch_shapes=[pltpu.SemaphoreType.DMA, pltpu.SemaphoreType.DMA((wears // 4,))],
        compiler_params=params(16),
        cost_estimate=cost(4 * cells * sum(ranks) * size, 8 * cells * size),
        name="pack_coefficients",
    )(in_hbm(u4), in_hbm(send))


def pack_edges_kernel(ranks, sides, send_ref, *refs):
    edge_refs, q_refs = refs[:sides], refs[sides + len(ranks) :]
    count = edge_refs[0].shape[0] - HAZARD_ROWS
    halves = []
    for half in range(2):
        cells = [r[half * count // 2 : (half + 1) * count // 2] for r in edge_refs]
        halves.append(analyse(send_ref[...], jnp.concatenate(cells, axis=0)))
    for q_ref, rows in zip(q_refs, pack_rows(ranks, halves)):
        q_ref[:, q_ref.shape[1] - rows.shape[1] :] = rows


def pack_edges(send, near, q, ranks, sides):
    return pl.pallas_call(
        functools.partial(pack_edges_kernel, ranks, sides),
        in_specs=[VMEM] * (1 + sides + len(ranks)),
        out_specs=[VMEM] * len(ranks),
        out_shape=[jax.ShapeDtypeStruct(x.shape, x.dtype) for x in q],
        input_output_aliases={1 + sides + i: i for i in range(len(ranks))},
        compiler_params=params(16),
        cost_estimate=cost(0, 2**18),
        name="pack_edges",
    )(in_vmem(send), *near, *q)


def local_kernel(sides, u_ref, hazard_hbm, diffusion_hbm, drift_hbm, second_hbm, first_hbm, take_second_hbm,
                 take_first_hbm, *refs):
    edge_refs, refs = refs[:sides], refs[sides:]
    z, beside, ends, take, hazard, diffusion, drift, second, first, own, take_second, take_first, sem = refs
    halves, rows, _, _ = z.shape
    _, wears, ages, size = u_ref.shape
    at = lax.axis_index("cheb")
    moves = (
        (second_hbm.at[at], second), (first_hbm.at[at], first), (diffusion_hbm.at[at], diffusion),
        (drift_hbm.at[at], drift), (hazard_hbm, hazard), (take_second_hbm.at[at], take_second),
        (take_first_hbm.at[at], take_first),
    )
    copies = [pltpu.make_async_copy(src, dst, sem.at[i]) for i, (src, dst) in enumerate(moves)]
    for copy in copies:
        copy.start()
    for l in range(halves):
        zero = jnp.zeros((rows, 16, 128), f32)
        z[l, :, :ROW0, :] = zero
        z[l, :, ROW0 + ages :, :] = zero
    for copy in copies:
        copy.wait()
    scaled, moved = START * diffusion[...], START * drift[...]
    own[...] = (second[...] * scaled + first[...] * moved).astype(bf16)
    take[...] = (take_second[...] * scaled + take_first[...] * moved).astype(bf16)
    keep = jnp.transpose(START - START * hazard[...])
    chunk = 4
    for w in range(0, 2 * wears, chunk):
        half, v = divmod(w, wears)
        u = u_ref[half, v : v + chunk].reshape(chunk * ages, size)
        rate = jnp.dot(u.astype(bf16), own[...], preferred_element_type=f32)
        for i in range(chunk):
            cells = slice(i * ages, (i + 1) * ages)
            value = rate[cells] + keep[:, w + i : w + i + 1] * u[cells]
            for l in range(halves):
                z[l, HALO + w + i, ROW0 : ROW0 + ages, :] = value[:, l * 128 : (l + 1) * 128]
            for e, start in enumerate((0, 2 * wears - HALO)):
                if start <= w + i < start + HALO:
                    ends[e, (w + i - start) * ages : (w + i - start + 1) * ages] = value
    for s, ref in enumerate(edge_refs):
        count = 2 * wears * HALO
        parts = ref[count:].astype(f32)
        near = START - START * (parts[:HALO, : 2 * wears] + parts[HALO : 2 * HALO, : 2 * wears])
        near = jnp.concatenate([near, near], axis=0)
        for w in range(0, 2 * wears, 4):
            place = slice(w * HALO, (w + 4) * HALO)
            u = ref[place]
            rate = jnp.dot(u, own[...], preferred_element_type=f32)
            columns = [
                jnp.broadcast_to(near[:HALO, w + j : w + j + 1], (HALO, size)) for j in range(4)
            ]
            beside[s, place] = rate + jnp.concatenate(columns, axis=0) * u.astype(f32)


def local(u4, hazard, diffusion, drift, tables, near, sides):
    _, wears, ages, size = u4.shape
    cells = 2 * wears * ages
    wide = tables[2].shape[2]
    return pl.pallas_call(
        functools.partial(local_kernel, sides),
        in_specs=[VMEM] + [ANY] * 7 + [VMEM] * sides,
        out_specs=[VMEM] * 4,
        out_shape=[
            pltpu.VMEM((size // 128, 2 * wears + 2 * HALO, ages + 32, 128), f32),
            pltpu.VMEM((sides, 2 * wears * HALO, size), f32),
            pltpu.VMEM((2, HALO * ages, size), f32),
            pltpu.VMEM((2, wide, size), bf16),
        ],
        scratch_shapes=[
            pltpu.VMEM(hazard.shape, f32),
            pltpu.VMEM((1, size), f32),
            pltpu.VMEM((1, size), f32),
            pltpu.VMEM((size, size), f32),
            pltpu.VMEM((size, size), f32),
            pltpu.VMEM((size, size), bf16),
            pltpu.VMEM((2, wide, size), f32),
            pltpu.VMEM((2, wide, size), f32),
            pltpu.SemaphoreType.DMA((7,)),
        ],
        compiler_params=params(16),
        cost_estimate=cost(2 * cells * size * size, 8 * cells * size),
        name="local_rate",
    )(in_vmem(u4), *[in_hbm(x) for x in (hazard, diffusion, drift, *tables)], *near)


def arrived_tiles(ranks, q_refs, half, columns):
    tiles = []
    for rank, q in zip(ranks, q_refs):
        cut = rank // 16 * 16
        if cut:
            tiles.append(q[half * cut : (half + 1) * cut, columns])
        if rank > cut:
            tiles.append(q[2 * cut : 2 * rank, columns])
    return jnp.concatenate(tiles, axis=0)


def distant(ranks, q_refs, take_ref, half, columns):
    return lax.dot_general(
        arrived_tiles(ranks, q_refs, half, columns), take_ref[half], (((0,), (0,)), ((), ())),
        preferred_element_type=f32,
    )


def edge_columns(sides, main, each):
    return [slice(main + s * each, main + (s + 1) * each) for s in range(sides)]


def rows_kernel(ranks, sides, wears, ages, ends_ref, beside_ref, take_ref, *refs):
    q_refs, out_refs = refs[: len(ranks)], refs[len(ranks) :]
    main, each = wears // 2 * ages, wears // 2 * HALO
    corner = HALO * HALO
    for half, (start, out_ref) in enumerate(zip((0, wears - HALO), out_refs)):
        v = (start - half * wears // 2) * ages
        rate = distant(ranks, q_refs, take_ref, half, slice(v, v + HALO * ages))
        out_ref[: HALO * ages] = (rate + ends_ref[half]).astype(bf16)
        for s, columns in enumerate(edge_columns(sides, main, each)):
            first = 0 if half == 0 else each - corner
            rate = distant(ranks, q_refs, take_ref, half, columns)[first : first + corner]
            place = slice(start * HALO, start * HALO + corner)
            row = HALO * ages + s * corner
            out_ref[row : row + corner] = (rate + beside_ref[s, place]).astype(bf16)


def outer_rows(ends, beside, take, q, ranks, sides, wears, ages):
    size = ends.shape[-1]
    message = jax.ShapeDtypeStruct((HALO * ages + sides * HALO * HALO, size), bf16)
    return pl.pallas_call(
        functools.partial(rows_kernel, ranks, sides, wears, ages),
        in_specs=[VMEM] * (3 + len(ranks)),
        out_specs=[VMEM] * 2,
        out_shape=[message, message],
        compiler_params=params(16),
        cost_estimate=cost(2 * 8 * ages * take.shape[1] * size, 2**20),
        name="outer_rows",
    )(in_vmem(ends), in_vmem(beside), in_vmem(take), *q)


def section_kernel(ranks, sides, wears, ages, z_in, beside_ref, take_ref, *refs):
    q_refs, (z,) = refs[: len(ranks)], refs[len(ranks) :]
    halves = z.shape[0]
    main, each = wears // 2 * ages, wears // 2 * HALO
    chunk = 4
    for w in range(0, wears, chunk):
        half, v = divmod(w, wears // 2)
        rate = distant(ranks, q_refs, take_ref, half, slice(v * ages, (v + chunk) * ages))
        for i in range(chunk):
            for l in range(halves):
                z[l, HALO + w + i, ROW0 : ROW0 + ages, :] = (
                    z_in[l, HALO + w + i, ROW0 : ROW0 + ages, :]
                    + rate[i * ages : (i + 1) * ages, l * 128 : (l + 1) * 128]
                )
    has = [jnp.where(at_end("age", i == 1), 0.0, 1.0).astype(f32) for i in range(2)]
    for s in range(sides):
        for half in range(2):
            columns = edge_columns(sides, main, each)[s]
            place = slice(half * each, (half + 1) * each)
            cells = distant(ranks, q_refs, take_ref, half, columns) + beside_ref[s, place]
            for i, column in ((0, ROW0 - HALO), (1, ROW0 + ages)):
                if sides == 1 or s == i:
                    part = cells * has[i]
                    for w in range(wears // 2):
                        for l in range(halves):
                            z[l, HALO + half * wears // 2 + w, column : column + HALO, :] = part[
                                w * HALO : (w + 1) * HALO, l * 128 : (l + 1) * 128
                            ]


def section(z, beside, take, q, ranks, sides, wears, ages):
    size = z.shape[0] * 128
    cells = wears * ages
    return pl.pallas_call(
        functools.partial(section_kernel, ranks, sides, wears, ages),
        in_specs=[VMEM] * (3 + len(ranks)),
        out_specs=VMEM,
        out_shape=pltpu.VMEM(z.shape, f32),
        input_output_aliases={0: 0},
        compiler_params=params(16),
        cost_estimate=cost(2 * cells * take.shape[1] * size, 8 * cells * size),
        name="section",
    )(z, in_vmem(beside), in_vmem(take), *q)


def lane_terms(speed_ref, l):
    speed = speed_ref[0:1, l * 128 : (l + 1) * 128]
    stay = GAIN * (1.0 - age_courant - 2.0 * wear_spread - speed)
    worn = GAIN * (speed + wear_spread)
    return stay, worn


def row_terms(src, l, w, lo, hi, stay, worn):
    t = src[l, w, lo:hi, :]
    older = src[l, w, lo + 1 : hi + 1, :]
    slope = older - src[l, w, lo - 1 : hi - 1, :]
    centre = stay * t + (GAIN * age_courant) * older
    less = (t - slope) + t
    return centre, worn * t + slope, less


def rows_step(src, l, start, stop, lo, hi, factors, put, unroll):
    def step(w, carry):
        partial, less = carry
        centre, more, new_less = row_terms(src, l, w + 1, lo, hi, *factors)
        put(w, partial + more)
        return centre + less, new_less

    _, _, less0 = row_terms(src, l, start - 1, lo, hi, *factors)
    centre1, _, less1 = row_terms(src, l, start, lo, hi, *factors)
    lax.fori_loop(start, stop, step, (centre1 + less0, less1), unroll=unroll)


def put_in(dst, l, lo, hi, keeps, factor=None):
    def put(w, out):
        if factor is not None:
            out = out * factor(w)
        if keeps is None:
            dst[l, w, lo:hi, :] = out
        else:
            dst[l, w, lo : lo + 8, :] = out[:8] * keeps[0]
            dst[l, w, lo + 8 : hi - 8, :] = out[8:-8]
            dst[l, w, hi - 8 : hi, :] = out[-8:] * keeps[1]

    return put


def by_sides(sides, ages, run):
    if sides == 1:
        pl.when(at_end("age", False))(lambda: run(ROW0, ROW0 + ages + 8, None))
        pl.when(at_end("age", True))(lambda: run(ROW0 - 8, ROW0 + ages, None))
    else:
        has = [jnp.where(at_end("age", i == 1), 0.0, 1.0).astype(f32) for i in range(2)]
        run(ROW0 - 8, ROW0 + ages + 8, [jnp.zeros((8, 128), f32) + h for h in has])


def inner_kernel(sides, z0, speed_ref, o_ref, z1, z2, z3, stage, out_sem):
    halves, rows, _, _ = z0.shape
    count, ages = stage.shape[:2]
    fields = (z0, z1, z2, z3)

    def run(low, high, keeps):
        for z in fields[1:]:
            for l in range(halves):
                if low == ROW0:
                    z[l, :, ROW0 - 8 : ROW0, :] = jnp.zeros((rows, 8, 128), f32)
                if high == ROW0 + ages:
                    z[l, :, high : high + 8, :] = jnp.zeros((rows, 8, 128), f32)
        for k in range(1, SUBSTEPS):
            for l in range(halves):
                rows_step(
                    fields[k - 1], l, HALO + k, rows - HALO - k, low, high, lane_terms(speed_ref, l),
                    put_in(fields[k], l, low, high, keeps), 2,
                )
        stores = []
        first = HALO + SUBSTEPS
        bounds = [0, count * 3 // 7, count * 5 // 7, count * 6 // 7, count]
        for a, b in zip(bounds, bounds[1:]):
            for l in range(halves):
                def put(w, out, l=l):
                    stage[w - first, :, l * 128 : (l + 1) * 128] = out

                rows_step(
                    fields[-1], l, first + a, first + b, ROW0, ROW0 + ages, lane_terms(speed_ref, l), put, 4,
                )
            copy = pltpu.make_async_copy(
                stage.at[pl.ds(a, b - a)], o_ref.at[pl.ds(SUBSTEPS + a, b - a)], out_sem.at[len(stores)]
            )
            copy.start()
            stores.append(copy)
        for copy in stores:
            copy.wait()

    by_sides(sides, ages, run)


def inner_substeps(z, speed, sides, wears, ages):
    size = z.shape[0] * 128
    shape = (wears, ages, size)
    return pl.pallas_call(
        functools.partial(inner_kernel, sides),
        out_shape=[jax.ShapeDtypeStruct(shape, f32)] + [pltpu.VMEM(z.shape, f32)] * 3,
        in_specs=[VMEM] * 2,
        out_specs=[ANY] + [VMEM] * 3,
        scratch_shapes=[pltpu.VMEM((wears - 2 * SUBSTEPS, ages, size), f32), pltpu.SemaphoreType.DMA((4,))],
        compiler_params=params(16),
        cost_estimate=cost(10 * SUBSTEPS * wears * ages * size, 8 * wears * ages * size),
        name="inner_substeps",
    )(in_vmem(z), speed)


def outer_kernel(sides, o_in, z0_in, z1_in, z2_in, z3_in, speed_ref, up_ref, down_ref, o_ref, z0, z1, z2, z3,
                 stage, out_sem):
    del o_in, z0_in, z1_in, z2_in, z3_in
    halves, rows, _, _ = z0.shape
    wears, ages = rows - 2 * HALO, stage.shape[2]
    fields = (z0, z1, z2, z3)
    has = [jnp.where(at_end("age", i == 1), 0.0, 1.0).astype(f32) for i in range(2)]
    near = [jnp.where(at_end("wear", i == 1), 0.0, 1.0).astype(f32) for i in range(2)]
    for l in range(halves):
        lanes = pl.ds(l * 128, 128)
        for e, (ref, at) in enumerate(((up_ref, 0), (down_ref, HALO + wears))):
            values = ref[:, lanes].astype(f32) * near[e]
            z0[l, at : at + HALO, ROW0 : ROW0 + ages, :] = values[: HALO * ages].reshape(HALO, ages, 128)
            for s in range(sides):
                corner = values[HALO * (ages + s * HALO) : HALO * (ages + (s + 1) * HALO)]
                for i, column in ((0, ROW0 - HALO), (1, ROW0 + ages)):
                    if sides == 1 or s == i:
                        part = corner * has[i]
                        for w in range(HALO):
                            z0[l, at + w, column : column + HALO, :] = part[w * HALO : (w + 1) * HALO]

    def run(low, high, keeps):
        for k in range(1, SUBSTEPS):
            for l in range(halves):
                for e, start in enumerate((k, rows - HALO - k)):
                    beyond = (lambda w: w < HALO, lambda w: w >= HALO + wears)[e]
                    rows_step(
                        fields[k - 1], l, start, start + HALO, low, high, lane_terms(speed_ref, l),
                        put_in(
                            fields[k], l, low, high, keeps,
                            lambda w, e=e, beyond=beyond: jnp.where(beyond(w), near[e], 1.0).astype(f32),
                        ), 4,
                    )
        stores = []
        for e, start in enumerate((HALO, rows - 2 * HALO)):
            for l in range(halves):
                def put(w, out, l=l, e=e, start=start):
                    stage[e, w - start, :, l * 128 : (l + 1) * 128] = out

                rows_step(fields[-1], l, start, start + HALO, ROW0, ROW0 + ages, lane_terms(speed_ref, l), put, 4)
            copy = pltpu.make_async_copy(stage.at[e], o_ref.at[pl.ds(start - HALO, HALO)], out_sem.at[e])
            copy.start()
            stores.append(copy)
        for copy in stores:
            copy.wait()

    by_sides(sides, ages, run)


def outer_substeps(o, fields, speed, up, down, sides):
    wears, ages, size = o.shape
    return pl.pallas_call(
        functools.partial(outer_kernel, sides),
        out_shape=[jax.ShapeDtypeStruct(o.shape, f32)] + [pltpu.VMEM(z.shape, f32) for z in fields],
        in_specs=[ANY] + [VMEM] * 7,
        out_specs=[ANY] + [VMEM] * 4,
        scratch_shapes=[pltpu.VMEM((2, HALO, ages, size), f32), pltpu.SemaphoreType.DMA((2,))],
        input_output_aliases={i: i for i in range(5)},
        compiler_params=params(16),
        cost_estimate=cost(20 * SUBSTEPS * 2 * HALO * ages * size, 2**20),
        name="outer_substeps",
    )(o, *fields, speed, up, down)[0]


def body(adjoint_value, load_diffusion, load_drift, wear_speed, hazard):
    wears, ages, size = adjoint_value.shape
    points = load_diffusion.shape[0]
    devices = points // size
    slots, send, take_second, take_first, own_second, own_first = factors(points, devices)
    ranks = tuple(rank for _, rank in slots)
    n_wear, n_age = lax.axis_size("wear"), lax.axis_size("age")
    sides = 1 if n_age == 2 else 2
    extra = sides * wears // 2 * HALO
    u4 = adjoint_value.reshape(2, wears // 2, ages, size)
    diffusion = load_diffusion.reshape(devices, 1, size)
    drift = load_drift.reshape(devices, 1, size)
    tables = [jnp.asarray(t, f32) for t in (own_second, own_first, take_second, take_first)]

    def ring(n):
        after = [(i, (i + 1) % n) for i in range(n)]
        return after, [(j, i) for i, j in after]

    edge = edges(adjoint_value, hazard, sides)
    near = [lax.ppermute(x, "age", pairs) for x, pairs in zip(edge, ring(n_age))]
    *q, u4, send = pack(u4, jnp.asarray(send, bf16), ranks, extra)
    q = pack_edges(send, near, q, ranks, sides)
    arrived = [lax.ppermute(x, "cheb", list(pairs)) for x, (pairs, _) in zip(q, slots)]
    z, beside, ends, take = local(u4, hazard, diffusion, drift, tables, near, sides)
    top, bottom = outer_rows(ends, beside, take, arrived, ranks, sides, wears, ages)
    after, before = ring(n_wear)
    up, down = lax.ppermute(bottom, "wear", after), lax.ppermute(top, "wear", before)
    z = section(z, beside, take, arrived, ranks, sides, wears, ages)
    speed = wear_speed.reshape(1, size)
    o, *fields = inner_substeps(z, speed, sides, wears, ages)
    return outer_substeps(o, [z, *fields], speed, up, down, sides)


def solution(mesh):
    placed = (P("wear", "age", "cheb"), P(), P(), P("cheb"), P("wear", "age"))
    return jax.shard_map(
        body, mesh=mesh, in_specs=placed, out_specs=P("wear", "age", "cheb"), check_vma=False
    )
```

```python
import functools

import jax
import jax.numpy as jnp
import numpy as np
from jax import lax
from jax.experimental import pallas as pl
from jax.experimental.pallas import tpu as pltpu
from jax.sharding import PartitionSpec as P

SUBSTEPS = 4
HALO = SUBSTEPS

age_courant = 0.4
wear_spread = 0.1
coupling = 0.05
GAIN = 1.0 / coupling
START = coupling**SUBSTEPS

f32 = jnp.float32
bf16 = jnp.bfloat16


def operators(points):
    modes = np.arange(points)[:, None]
    nodes = np.arange(points)[None, :]
    angles = (modes * (2 * nodes + 1)) % (4 * points) * (np.pi / (2 * points))
    cosine, sine = np.cos(angles), np.sin(angles)
    analysis = np.where(modes == 0, 1.0, 2.0) / points * cosine
    wavenumber = modes / points
    return (-(wavenumber**2) * cosine).T @ analysis, (wavenumber * sine).T @ analysis


def arrived_rows(rank):
    return -(-rank // 16) * 16


@functools.lru_cache(maxsize=None)
def factors(points, devices):
    second, first = operators(points)
    size = points // devices
    parts = [slice(b * size, (b + 1) * size) for b in range(devices)]
    slots, found = [], {}
    for shift in range(1, devices):
        pairs, most = [], 0
        for c in range(devices):
            b = c ^ shift if devices & (devices - 1) == 0 else (c + shift) % devices
            joint = np.concatenate([second[parts[b], parts[c]], first[parts[b], parts[c]]])
            _, sizes, rows = np.linalg.svd(joint, full_matrices=False)
            rank = int((sizes > joint.shape[0] * np.finfo(np.float64).eps).sum())
            rank = -(-rank // 8) * 8
            basis = rows[:rank]
            found[c, b] = (basis, second[parts[b], parts[c]] @ basis.T, first[parts[b], parts[c]] @ basis.T)
            pairs.append((c, b))
            most = max(most, rank)
        slots.append((tuple(pairs), most))
    send = np.zeros((devices, sum(rank for _, rank in slots), size))
    wide = sum(arrived_rows(rank) for _, rank in slots)
    take_second = np.zeros((devices, 2, wide, size))
    take_first = np.zeros((devices, 2, wide, size))
    at = row = 0
    for pairs, rank in slots:
        whole = rank // 16 * 16
        for c, b in pairs:
            basis, left_second, left_first = (
                np.pad(x, ((0, rank - len(found[c, b][0])), (0, 0))) for x in (found[c, b][0], found[c, b][1].T, found[c, b][2].T)
            )
            send[c, at : at + rank] = basis
            for half in range(2):
                for take, left in ((take_second, left_second), (take_first, left_first)):
                    take[b, half, row : row + whole] = left[:whole]
                    place = row + whole + half * (rank - whole)
                    take[b, half, place : place + rank - whole] = left[whole:]
        at += rank
        row += arrived_rows(rank)
    own_second = np.stack([second[p, p].T for p in parts])
    own_first = np.stack([first[p, p].T for p in parts])
    return slots, send, take_second, take_first, own_second, own_first


ANY = pl.BlockSpec(memory_space=pl.ANY)
VMEM = pl.BlockSpec(memory_space=pltpu.VMEM)
PIN = pltpu.VMEM
ROW0 = 16
HAZARD_ROWS = 16


def at_end(axis, last):
    return lax.axis_index(axis) == (lax.axis_size(axis) - 1 if last else 0)


def in_hbm(x):
    return pltpu.with_memory_space_constraint(x, pltpu.HBM)


def in_vmem(x):
    return pltpu.with_memory_space_constraint(x, pltpu.VMEM)


def params(mebibytes):
    return pltpu.CompilerParams(vmem_limit_bytes=mebibytes * 2**20)


def cost(flops, bytes_accessed):
    return pl.CostEstimate(flops=flops, bytes_accessed=bytes_accessed, transcendentals=0)


def edge_kernel(sides, u_hbm, hazard_hbm, *refs):
    out_refs, (tiles, hazard, sem) = refs[:sides], refs[sides:]
    wears, ages, size = u_hbm.shape
    copies = [pltpu.make_async_copy(hazard_hbm, hazard, sem.at[sides])]
    for i in range(sides):
        if sides == 1:
            start = pl.multiple_of(jnp.where(at_end("age", False), ages - 8, 0), 8)
        else:
            start = (ages - 8, 0)[i]
        copies.append(pltpu.make_async_copy(u_hbm.at[:, pl.ds(start, 8)], tiles.at[i], sem.at[i]))
    for copy in copies:
        copy.start()
    for copy in copies:
        copy.wait()
    by_age = jnp.transpose(hazard[...])
    last, early = by_age[ages - HALO :], by_age[:HALO]
    for i, out_ref in enumerate(out_refs):
        for w in range(0, wears, 4):
            late = [tiles[i, w + j, 8 - HALO :] for j in range(4)]
            soon = [tiles[i, w + j, :HALO] for j in range(4)]
            late, soon = jnp.concatenate(late, axis=0), jnp.concatenate(soon, axis=0)
            if sides == 1:
                cells = jnp.where(at_end("age", False), late, soon)
            else:
                cells = (late, soon)[i]
            out_ref[w * HALO : (w + 4) * HALO] = cells.astype(bf16)
        if sides == 1:
            exact = jnp.where(at_end("age", False), last, early)
        else:
            exact = (last, early)[i]
        high = exact.astype(bf16).astype(f32)
        rows = jnp.concatenate([high, exact - high, jnp.zeros((HAZARD_ROWS - 2 * HALO, wears), f32)], axis=0)
        rows = jnp.concatenate([rows, jnp.zeros((HAZARD_ROWS, size - wears), f32)], axis=1)
        out_ref[wears * HALO : wears * HALO + HAZARD_ROWS] = rows.astype(bf16)
        out_ref[wears * HALO + HAZARD_ROWS :] = jnp.zeros_like(out_ref[wears * HALO + HAZARD_ROWS :])


def edges(u, hazard, sides, rows):
    wears, ages, size = u.shape
    return pl.pallas_call(
        functools.partial(edge_kernel, sides),
        in_specs=[ANY, ANY],
        out_specs=[VMEM] * sides,
        out_shape=[PIN((rows, size), bf16)] * sides,
        scratch_shapes=[
            pltpu.VMEM((sides, wears, 8, size), f32),
            pltpu.VMEM((wears, ages), f32),
            pltpu.SemaphoreType.DMA((sides + 1,)),
        ],
        compiler_params=params(16),
        cost_estimate=cost(0, 8 * wears * 8 * size),
        name="age_edges",
    )(in_hbm(u), in_hbm(hazard))


def pack_rows(ranks, halves):
    packed, row = [], 0
    for rank in ranks:
        cut = row + rank // 16 * 16
        pieces = [h[row:cut] for h in halves if cut > row]
        pieces += [h[cut : row + rank] for h in halves if cut < row + rank]
        packed.append(jnp.concatenate(pieces, axis=0).astype(bf16))
        row += rank
    return packed


def analyse(table, cells):
    return lax.dot_general(table, cells, (((1,), (1,)), ((), ())), preferred_element_type=f32)


def pack_kernel(ranks, sides, u_ref, send_hbm, *refs):
    q_refs, (send, send_sem) = refs[sides : sides + len(ranks)], refs[sides + len(ranks) :]
    _, wears, ages, size = u_ref.shape
    chunk = 4
    table = pltpu.make_async_copy(send_hbm.at[lax.axis_index("cheb")], send, send_sem)
    table.start()
    table.wait()
    for g in range(wears // chunk):
        halves = [
            analyse(send[...], u_ref[half, g * chunk : (g + 1) * chunk].reshape(chunk * ages, size).astype(bf16))
            for half in range(2)
        ]
        for q_ref, rows in zip(q_refs, pack_rows(ranks, halves)):
            q_ref[:, g * chunk * ages : (g + 1) * chunk * ages] = rows


def pack(u4, send, edge, ranks):
    _, wears, ages, size = u4.shape
    cells = wears * ages
    return pl.pallas_call(
        functools.partial(pack_kernel, ranks, len(edge)),
        in_specs=[VMEM, ANY] + [ANY] * len(edge),
        out_specs=[VMEM] * (len(ranks) + 1),
        out_shape=[PIN((2 * r, cells), bf16) for r in ranks] + [PIN(send.shape[1:], bf16)],
        scratch_shapes=[pltpu.SemaphoreType.DMA],
        compiler_params=params(16),
        cost_estimate=cost(4 * cells * sum(ranks) * size, 8 * cells * size),
        name="pack_coefficients",
    )(in_vmem(u4), in_hbm(send), *[in_vmem(x) for x in edge])


def pack_edges_kernel(ranks, sides, send_ref, *refs):
    edge_refs, q_refs = refs[:sides], refs[sides + 2 :]
    count = 2 * q_refs[0].shape[1] // sides
    halves = []
    for half in range(2):
        cells = [r[half * count // 2 : (half + 1) * count // 2] for r in edge_refs]
        halves.append(analyse(send_ref[...], jnp.concatenate(cells, axis=0)))
    for q_ref, rows in zip(q_refs, pack_rows(ranks, halves)):
        q_ref[...] = rows


def pack_edges(send, near, arrived, ranks, sides, extra):
    return pl.pallas_call(
        functools.partial(pack_edges_kernel, ranks, sides),
        in_specs=[VMEM] * (2 + sides),
        out_specs=[VMEM] * (1 + len(ranks)),
        out_shape=[PIN(arrived.shape, bf16)] + [PIN((2 * r, extra), bf16) for r in ranks],
        input_output_aliases={1 + sides: 0},
        compiler_params=params(16),
        cost_estimate=cost(0, 2**18),
        name="pack_edges",
    )(*[in_vmem(x) for x in (send, *near, arrived)])


def local_kernel(sides, u_ref, hazard_hbm, diffusion_hbm, drift_hbm, second_hbm, first_hbm, take_second_hbm,
                 take_first_hbm, *refs):
    edge_refs, refs = refs[:sides], refs[sides:]
    z, beside, ends, take, hazard, diffusion, drift, second, first, own, take_second, take_first, sem = refs
    halves, rows, _, _ = z.shape
    _, wears, ages, size = u_ref.shape
    at = lax.axis_index("cheb")
    moves = (
        (second_hbm.at[at], second), (first_hbm.at[at], first), (diffusion_hbm.at[at], diffusion),
        (drift_hbm.at[at], drift), (hazard_hbm, hazard), (take_second_hbm.at[at], take_second),
        (take_first_hbm.at[at], take_first),
    )
    copies = [pltpu.make_async_copy(src, dst, sem.at[i]) for i, (src, dst) in enumerate(moves)]
    for copy in copies:
        copy.start()
    for l in range(halves):
        zero = jnp.zeros((rows, 16, 128), f32)
        z[l, :, :ROW0, :] = zero
        z[l, :, ROW0 + ages :, :] = zero
    for copy in copies:
        copy.wait()
    scaled, moved = START * diffusion[...], START * drift[...]
    own[...] = (second[...] * scaled + first[...] * moved).astype(bf16)
    take[...] = (take_second[...] * scaled + take_first[...] * moved).astype(bf16)
    keep = jnp.transpose(START - START * hazard[...])
    chunk = 4
    for w in range(0, 2 * wears, chunk):
        half, v = divmod(w, wears)
        u = u_ref[half, v : v + chunk].reshape(chunk * ages, size)
        rate = jnp.dot(u.astype(bf16), own[...], preferred_element_type=f32)
        for i in range(chunk):
            cells = slice(i * ages, (i + 1) * ages)
            value = rate[cells] + keep[:, w + i : w + i + 1] * u[cells]
            for l in range(halves):
                z[l, HALO + w + i, ROW0 : ROW0 + ages, :] = value[:, l * 128 : (l + 1) * 128]
            for e, start in enumerate((0, 2 * wears - HALO)):
                if start <= w + i < start + HALO:
                    ends[e, (w + i - start) * ages : (w + i - start + 1) * ages] = value
    for s, ref in enumerate(edge_refs):
        count = 2 * wears * HALO
        parts = ref[count : count + HAZARD_ROWS].astype(f32)
        near = START - START * (parts[:HALO, : 2 * wears] + parts[HALO : 2 * HALO, : 2 * wears])
        near = jnp.concatenate([near, near], axis=0)
        for w in range(0, 2 * wears, 4):
            place = slice(w * HALO, (w + 4) * HALO)
            u = ref[place]
            rate = jnp.dot(u, own[...], preferred_element_type=f32)
            columns = [
                jnp.broadcast_to(near[:HALO, w + j : w + j + 1], (HALO, size)) for j in range(4)
            ]
            beside[s, place] = rate + jnp.concatenate(columns, axis=0) * u.astype(f32)


def local(u4, hazard, diffusion, drift, tables, near, sides):
    _, wears, ages, size = u4.shape
    cells = 2 * wears * ages
    wide = tables[2].shape[2]
    return pl.pallas_call(
        functools.partial(local_kernel, sides),
        in_specs=[VMEM] + [ANY] * 7 + [VMEM] * sides,
        out_specs=[VMEM] * 4,
        out_shape=[
            pltpu.VMEM((size // 128, 2 * wears + 2 * HALO, ages + 32, 128), f32),
            pltpu.VMEM((sides, 2 * wears * HALO, size), f32),
            pltpu.VMEM((2, HALO * ages, size), f32),
            pltpu.VMEM((2, wide, size), bf16),
        ],
        scratch_shapes=[
            pltpu.VMEM(hazard.shape, f32),
            pltpu.VMEM((1, size), f32),
            pltpu.VMEM((1, size), f32),
            pltpu.VMEM((size, size), f32),
            pltpu.VMEM((size, size), f32),
            pltpu.VMEM((size, size), bf16),
            pltpu.VMEM((2, wide, size), f32),
            pltpu.VMEM((2, wide, size), f32),
            pltpu.SemaphoreType.DMA((7,)),
        ],
        compiler_params=params(16),
        cost_estimate=cost(2 * cells * size * size, 8 * cells * size),
        name="local_rate",
    )(in_vmem(u4), *[in_hbm(x) for x in (hazard, diffusion, drift, *tables)], *[in_vmem(x) for x in near])


def distant(ranks, q_refs, take_ref, half, columns):
    tiles = []
    for rank, q, place in zip(ranks, q_refs, columns):
        cut = rank // 16 * 16
        if cut:
            tiles.append(q[half * cut : (half + 1) * cut, place])
        if rank > cut:
            tiles.append(q[2 * cut : 2 * rank, place])
    return lax.dot_general(
        jnp.concatenate(tiles, axis=0), take_ref[half], (((0,), (0,)), ((), ())), preferred_element_type=f32
    )


def rows_kernel(ranks, sides, wears, ages, ends_ref, beside_ref, take_ref, *refs):
    q_refs, edge_refs, out_refs = refs[: len(ranks)], refs[len(ranks) : -2], refs[-2:]
    each, corner = wears // 2 * HALO, HALO * HALO
    for half, (start, out_ref) in enumerate(zip((0, wears - HALO), out_refs)):
        v = (start - half * wears // 2) * ages
        rate = distant(ranks, q_refs, take_ref, half, [slice(v, v + HALO * ages)] * len(ranks))
        out_ref[: HALO * ages] = (rate + ends_ref[half]).astype(bf16)
        first = 0 if half == 0 else each - corner
        for s in range(sides):
            rate = distant(ranks, edge_refs, take_ref, half, [slice(s * each, (s + 1) * each)] * len(ranks))
            place = slice(start * HALO, start * HALO + corner)
            row = HALO * ages + s * corner
            out_ref[row : row + corner] = (rate[first : first + corner] + beside_ref[s, place]).astype(bf16)


def outer_rows(ends, beside, take, q, q_edges, ranks, sides, wears, ages):
    size = ends.shape[-1]
    message = PIN((HALO * ages + sides * HALO * HALO, size), bf16)
    return pl.pallas_call(
        functools.partial(rows_kernel, ranks, sides, wears, ages),
        in_specs=[VMEM] * (3 + 2 * len(ranks)),
        out_specs=[VMEM] * 2,
        out_shape=[message, message],
        compiler_params=params(16),
        cost_estimate=cost(2 * 8 * ages * take.shape[1] * size, 2**20),
        name="outer_rows",
    )(*[in_vmem(x) for x in (ends, beside, take, *q, *q_edges)])


def section_kernel(ranks, sides, wears, ages, z_in, beside_ref, take_ref, *refs):
    q_refs, edge_refs, z = refs[: len(ranks)], refs[len(ranks) : -1], refs[-1]
    halves = z.shape[0]
    each = wears // 2 * HALO
    chunk = 4
    for w in range(0, wears, chunk):
        half, v = divmod(w, wears // 2)
        rate = distant(ranks, q_refs, take_ref, half, [slice(v * ages, (v + chunk) * ages)] * len(ranks))
        for i in range(chunk):
            for l in range(halves):
                z[l, HALO + w + i, ROW0 : ROW0 + ages, :] = (
                    z_in[l, HALO + w + i, ROW0 : ROW0 + ages, :]
                    + rate[i * ages : (i + 1) * ages, l * 128 : (l + 1) * 128]
                )
    has = [jnp.where(at_end("age", i == 1), 0.0, 1.0).astype(f32) for i in range(2)]
    for s in range(sides):
        for half in range(2):
            place = slice(half * each, (half + 1) * each)
            cells = distant(ranks, edge_refs, take_ref, half, [slice(s * each, (s + 1) * each)] * len(ranks))
            cells += beside_ref[s, place]
            for i, column in ((0, ROW0 - HALO), (1, ROW0 + ages)):
                if sides == 1 or s == i:
                    part = cells * has[i]
                    for w in range(wears // 2):
                        for l in range(halves):
                            z[l, HALO + half * wears // 2 + w, column : column + HALO, :] = part[
                                w * HALO : (w + 1) * HALO, l * 128 : (l + 1) * 128
                            ]


def section(z, beside, take, q, q_edges, ranks, sides, wears, ages):
    size = z.shape[0] * 128
    cells = wears * ages
    return pl.pallas_call(
        functools.partial(section_kernel, ranks, sides, wears, ages),
        in_specs=[VMEM] * (3 + 2 * len(ranks)),
        out_specs=VMEM,
        out_shape=pltpu.VMEM(z.shape, f32),
        input_output_aliases={0: 0},
        compiler_params=params(16),
        cost_estimate=cost(2 * cells * take.shape[1] * size, 8 * cells * size),
        name="section",
    )(z, *[in_vmem(x) for x in (beside, take, *q, *q_edges)])


def lane_terms(speed_ref, l):
    speed = speed_ref[0:1, l * 128 : (l + 1) * 128]
    stay = GAIN * (1.0 - age_courant - 2.0 * wear_spread - speed)
    worn = GAIN * (speed + wear_spread)
    return stay, worn


def row_terms(src, l, w, lo, hi, stay, worn):
    t = src[l, w, lo:hi, :]
    older = src[l, w, lo + 1 : hi + 1, :]
    slope = older - src[l, w, lo - 1 : hi - 1, :]
    centre = stay * t + (GAIN * age_courant) * older
    less = (t - slope) + t
    return centre, worn * t + slope, less


def rows_step(src, l, start, stop, lo, hi, factors, put, unroll):
    def step(w, carry):
        partial, less = carry
        centre, more, new_less = row_terms(src, l, w + 1, lo, hi, *factors)
        put(w, partial + more)
        return centre + less, new_less

    _, _, less0 = row_terms(src, l, start - 1, lo, hi, *factors)
    centre1, _, less1 = row_terms(src, l, start, lo, hi, *factors)
    lax.fori_loop(start, stop, step, (centre1 + less0, less1), unroll=unroll)


def put_in(dst, l, lo, hi, keeps, factor=None):
    def put(w, out):
        if factor is not None:
            out = out * factor(w)
        if keeps is None:
            dst[l, w, lo:hi, :] = out
        else:
            dst[l, w, lo : lo + 8, :] = out[:8] * keeps[0]
            dst[l, w, lo + 8 : hi - 8, :] = out[8:-8]
            dst[l, w, hi - 8 : hi, :] = out[-8:] * keeps[1]

    return put


def by_sides(sides, ages, run):
    if sides == 1:
        pl.when(at_end("age", False))(lambda: run(ROW0, ROW0 + ages + 8, None))
        pl.when(at_end("age", True))(lambda: run(ROW0 - 8, ROW0 + ages, None))
    else:
        has = [jnp.where(at_end("age", i == 1), 0.0, 1.0).astype(f32) for i in range(2)]
        run(ROW0 - 8, ROW0 + ages + 8, [jnp.zeros((8, 128), f32) + h for h in has])


def inner_kernel(sides, z0, speed_ref, o_ref, z1, z2, z3, stage, out_sem):
    halves, rows, _, _ = z0.shape
    count, ages = stage.shape[:2]
    fields = (z0, z1, z2, z3)

    def run(low, high, keeps):
        for z in fields[1:]:
            for l in range(halves):
                if low == ROW0:
                    z[l, :, ROW0 - 8 : ROW0, :] = jnp.zeros((rows, 8, 128), f32)
                if high == ROW0 + ages:
                    z[l, :, high : high + 8, :] = jnp.zeros((rows, 8, 128), f32)
        for k in range(1, SUBSTEPS):
            for l in range(halves):
                rows_step(
                    fields[k - 1], l, HALO + k, rows - HALO - k, low, high, lane_terms(speed_ref, l),
                    put_in(fields[k], l, low, high, keeps), 2,
                )
        stores = []
        first = HALO + SUBSTEPS
        bounds = [0, count * 3 // 7, count * 5 // 7, count * 6 // 7, count]
        for a, b in zip(bounds, bounds[1:]):
            for l in range(halves):
                def put(w, out, l=l):
                    stage[w - first, :, l * 128 : (l + 1) * 128] = out

                rows_step(
                    fields[-1], l, first + a, first + b, ROW0, ROW0 + ages, lane_terms(speed_ref, l), put, 4,
                )
            copy = pltpu.make_async_copy(
                stage.at[pl.ds(a, b - a)], o_ref.at[pl.ds(SUBSTEPS + a, b - a)], out_sem.at[len(stores)]
            )
            copy.start()
            stores.append(copy)
        for copy in stores:
            copy.wait()

    by_sides(sides, ages, run)


def inner_substeps(z, speed, sides, wears, ages):
    size = z.shape[0] * 128
    shape = (wears, ages, size)
    return pl.pallas_call(
        functools.partial(inner_kernel, sides),
        out_shape=[jax.ShapeDtypeStruct(shape, f32)] + [pltpu.VMEM(z.shape, f32)] * 3,
        in_specs=[VMEM] * 2,
        out_specs=[ANY] + [VMEM] * 3,
        scratch_shapes=[pltpu.VMEM((wears - 2 * SUBSTEPS, ages, size), f32), pltpu.SemaphoreType.DMA((4,))],
        compiler_params=params(16),
        cost_estimate=cost(10 * SUBSTEPS * wears * ages * size, 8 * wears * ages * size),
        name="inner_substeps",
    )(in_vmem(z), speed)


def outer_kernel(sides, o_in, z0_in, z1_in, z2_in, z3_in, speed_ref, up_ref, down_ref, o_ref, z0, z1, z2, z3,
                 stage, out_sem):
    del o_in, z0_in, z1_in, z2_in, z3_in
    halves, rows, _, _ = z0.shape
    wears, ages = rows - 2 * HALO, stage.shape[2]
    fields = (z0, z1, z2, z3)
    has = [jnp.where(at_end("age", i == 1), 0.0, 1.0).astype(f32) for i in range(2)]
    near = [jnp.where(at_end("wear", i == 1), 0.0, 1.0).astype(f32) for i in range(2)]
    for l in range(halves):
        lanes = pl.ds(l * 128, 128)
        for e, (ref, at) in enumerate(((up_ref, 0), (down_ref, HALO + wears))):
            values = ref[:, lanes].astype(f32) * near[e]
            z0[l, at : at + HALO, ROW0 : ROW0 + ages, :] = values[: HALO * ages].reshape(HALO, ages, 128)
            for s in range(sides):
                corner = values[HALO * (ages + s * HALO) : HALO * (ages + (s + 1) * HALO)]
                for i, column in ((0, ROW0 - HALO), (1, ROW0 + ages)):
                    if sides == 1 or s == i:
                        part = corner * has[i]
                        for w in range(HALO):
                            z0[l, at + w, column : column + HALO, :] = part[w * HALO : (w + 1) * HALO]

    def run(low, high, keeps):
        for k in range(1, SUBSTEPS):
            for l in range(halves):
                for e, start in enumerate((k, rows - HALO - k)):
                    beyond = (lambda w: w < HALO, lambda w: w >= HALO + wears)[e]
                    rows_step(
                        fields[k - 1], l, start, start + HALO, low, high, lane_terms(speed_ref, l),
                        put_in(
                            fields[k], l, low, high, keeps,
                            lambda w, e=e, beyond=beyond: jnp.where(beyond(w), near[e], 1.0).astype(f32),
                        ), 4,
                    )
        stores = []
        for e, start in enumerate((HALO, rows - 2 * HALO)):
            for l in range(halves):
                def put(w, out, l=l, e=e, start=start):
                    stage[e, w - start, :, l * 128 : (l + 1) * 128] = out

                rows_step(fields[-1], l, start, start + HALO, ROW0, ROW0 + ages, lane_terms(speed_ref, l), put, 4)
            copy = pltpu.make_async_copy(stage.at[e], o_ref.at[pl.ds(start - HALO, HALO)], out_sem.at[e])
            copy.start()
            stores.append(copy)
        for copy in stores:
            copy.wait()

    by_sides(sides, ages, run)


def outer_substeps(o, fields, speed, up, down, sides):
    wears, ages, size = o.shape
    return pl.pallas_call(
        functools.partial(outer_kernel, sides),
        out_shape=[jax.ShapeDtypeStruct(o.shape, f32)] + [pltpu.VMEM(z.shape, f32) for z in fields],
        in_specs=[ANY] + [VMEM] * 7,
        out_specs=[ANY] + [VMEM] * 4,
        scratch_shapes=[pltpu.VMEM((2, HALO, ages, size), f32), pltpu.SemaphoreType.DMA((2,))],
        input_output_aliases={i: i for i in range(5)},
        compiler_params=params(16),
        cost_estimate=cost(20 * SUBSTEPS * 2 * HALO * ages * size, 2**20),
        name="outer_substeps",
    )(o, *fields, speed, in_vmem(up), in_vmem(down))[0]


def body(adjoint_value, load_diffusion, load_drift, wear_speed, hazard):
    wears, ages, size = adjoint_value.shape
    points = load_diffusion.shape[0]
    devices = points // size
    slots, send, take_second, take_first, own_second, own_first = factors(points, devices)
    ranks = tuple(rank for _, rank in slots)
    n_wear, n_age = lax.axis_size("wear"), lax.axis_size("age")
    sides = 1 if n_age == 2 else 2
    extra = sides * wears // 2 * HALO
    u4 = adjoint_value.reshape(2, wears // 2, ages, size)
    diffusion = load_diffusion.reshape(devices, 1, size)
    drift = load_drift.reshape(devices, 1, size)
    tables = [jnp.asarray(t, f32) for t in (own_second, own_first, take_second, take_first)]

    def ring(n):
        after = [(i, (i + 1) % n) for i in range(n)]
        return after, [(j, i) for i, j in after]

    most = 2 * max(ranks) * (wears // 2 * ages) // size
    edge = edges(adjoint_value, hazard, sides, max(wears * HALO + HAZARD_ROWS, -(-most // 16) * 16))
    near = [lax.ppermute(x, "age", pairs) for x, pairs in zip(edge, ring(n_age))]
    *q, send = pack(u4, jnp.asarray(send, bf16), edge, ranks)
    moves = [list(pairs) for pairs, _ in slots]
    arrived = [lax.ppermute(x, "cheb", pairs) for x, pairs in zip(q, moves)]
    arrived[0], *q_edges = pack_edges(send, near, arrived[0], ranks, sides, extra)
    arrived_edges = [lax.ppermute(x, "cheb", pairs) for x, pairs in zip(q_edges, moves)]
    z, beside, ends, take = local(u4, hazard, diffusion, drift, tables, near, sides)
    top, bottom = outer_rows(ends, beside, take, arrived, arrived_edges, ranks, sides, wears, ages)
    after, before = ring(n_wear)
    up, down = lax.ppermute(bottom, "wear", after), lax.ppermute(top, "wear", before)
    z = section(z, beside, take, arrived, arrived_edges, ranks, sides, wears, ages)
    speed = wear_speed.reshape(1, size)
    o, *fields = inner_substeps(z, speed, sides, wears, ages)
    return outer_substeps(o, [z, *fields], speed, up, down, sides)


def solution(mesh):
    placed = (P("wear", "age", "cheb"), P(), P(), P("cheb"), P("wear", "age"))
    return jax.shard_map(
        body, mesh=mesh, in_specs=placed, out_specs=P("wear", "age", "cheb"), check_vma=False
    )
```

```python
import functools

import jax
import jax.numpy as jnp
import numpy as np
from jax import lax
from jax.experimental import pallas as pl
from jax.experimental.pallas import tpu as pltpu
from jax.sharding import PartitionSpec as P

SUBSTEPS = 4
HALO = SUBSTEPS

age_courant = 0.4
wear_spread = 0.1
coupling = 0.05
GAIN = 1.0 / coupling
START = coupling**SUBSTEPS

NEGLIGIBLE = 2.0**-32

f32 = jnp.float32
bf16 = jnp.bfloat16


def operators(points):
    modes = np.arange(points)[:, None]
    nodes = np.arange(points)[None, :]
    angles = (modes * (2 * nodes + 1)) % (4 * points) * (np.pi / (2 * points))
    cosine, sine = np.cos(angles), np.sin(angles)
    analysis = np.where(modes == 0, 1.0, 2.0) / points * cosine
    wavenumber = modes / points
    return (-(wavenumber**2) * cosine).T @ analysis, (wavenumber * sine).T @ analysis


def arrived_rows(rank):
    return -(-rank // 16) * 16


@functools.lru_cache(maxsize=None)
def factors(points, devices):
    second, first = operators(points)
    size = points // devices
    parts = [slice(b * size, (b + 1) * size) for b in range(devices)]
    slots, found = [], {}
    for shift in range(1, devices):
        pairs, most = [], 0
        for c in range(devices):
            b = c ^ shift if devices & (devices - 1) == 0 else (c + shift) % devices
            joint = np.concatenate([second[parts[b], parts[c]], first[parts[b], parts[c]]])
            _, sizes, rows = np.linalg.svd(joint, full_matrices=False)
            rank = int((sizes > NEGLIGIBLE).sum())
            rank = -(-rank // 8) * 8
            basis = rows[:rank]
            found[c, b] = (basis, second[parts[b], parts[c]] @ basis.T, first[parts[b], parts[c]] @ basis.T)
            pairs.append((c, b))
            most = max(most, rank)
        slots.append((tuple(pairs), most))
    send = np.zeros((devices, sum(rank for _, rank in slots), size))
    wide = sum(arrived_rows(rank) for _, rank in slots)
    take_second = np.zeros((devices, 2, wide, size))
    take_first = np.zeros((devices, 2, wide, size))
    at = row = 0
    for pairs, rank in slots:
        whole = rank // 16 * 16
        for c, b in pairs:
            basis, left_second, left_first = (
                np.pad(x, ((0, rank - len(found[c, b][0])), (0, 0))) for x in (found[c, b][0], found[c, b][1].T, found[c, b][2].T)
            )
            send[c, at : at + rank] = basis
            for half in range(2):
                for take, left in ((take_second, left_second), (take_first, left_first)):
                    take[b, half, row : row + whole] = left[:whole]
                    place = row + whole + half * (rank - whole)
                    take[b, half, place : place + rank - whole] = left[whole:]
        at += rank
        row += arrived_rows(rank)
    own_second = np.stack([second[p, p].T for p in parts])
    own_first = np.stack([first[p, p].T for p in parts])
    return slots, send, take_second, take_first, own_second, own_first


ANY = pl.BlockSpec(memory_space=pl.ANY)
VMEM = pl.BlockSpec(memory_space=pltpu.VMEM)
PIN = pltpu.VMEM
ROW0 = 16
HAZARD_ROWS = 16


def at_end(axis, last):
    return lax.axis_index(axis) == (lax.axis_size(axis) - 1 if last else 0)


def in_hbm(x):
    return pltpu.with_memory_space_constraint(x, pltpu.HBM)


def in_vmem(x):
    return pltpu.with_memory_space_constraint(x, pltpu.VMEM)


def params(mebibytes):
    return pltpu.CompilerParams(vmem_limit_bytes=mebibytes * 2**20)


def cost(flops, bytes_accessed):
    return pl.CostEstimate(flops=flops, bytes_accessed=bytes_accessed, transcendentals=0)


def edge_kernel(sides, u_hbm, hazard_hbm, *refs):
    out_refs, (tiles, hazard, sem) = refs[:sides], refs[sides:]
    wears, ages, size = u_hbm.shape
    copies = [pltpu.make_async_copy(hazard_hbm, hazard, sem.at[sides])]
    for i in range(sides):
        if sides == 1:
            start = pl.multiple_of(jnp.where(at_end("age", False), ages - 8, 0), 8)
        else:
            start = (ages - 8, 0)[i]
        copies.append(pltpu.make_async_copy(u_hbm.at[:, pl.ds(start, 8)], tiles.at[i], sem.at[i]))
    for copy in copies:
        copy.start()
    for copy in copies:
        copy.wait()
    by_age = jnp.transpose(hazard[...])
    last, early = by_age[ages - HALO :], by_age[:HALO]
    for i, out_ref in enumerate(out_refs):
        for w in range(0, wears, 4):
            late = [tiles[i, w + j, 8 - HALO :] for j in range(4)]
            soon = [tiles[i, w + j, :HALO] for j in range(4)]
            late, soon = jnp.concatenate(late, axis=0), jnp.concatenate(soon, axis=0)
            if sides == 1:
                cells = jnp.where(at_end("age", False), late, soon)
            else:
                cells = (late, soon)[i]
            out_ref[w * HALO : (w + 4) * HALO] = cells.astype(bf16)
        if sides == 1:
            exact = jnp.where(at_end("age", False), last, early)
        else:
            exact = (last, early)[i]
        high = exact.astype(bf16).astype(f32)
        rows = jnp.concatenate([high, exact - high, jnp.zeros((HAZARD_ROWS - 2 * HALO, wears), f32)], axis=0)
        rows = jnp.concatenate([rows, jnp.zeros((HAZARD_ROWS, size - wears), f32)], axis=1)
        out_ref[wears * HALO : wears * HALO + HAZARD_ROWS] = rows.astype(bf16)
        used = wears * HALO + HAZARD_ROWS
        if out_ref.shape[0] > used:
            out_ref[used:] = jnp.zeros((out_ref.shape[0] - used, size), bf16)


def edges(u, hazard, sides, rows):
    wears, ages, size = u.shape
    return pl.pallas_call(
        functools.partial(edge_kernel, sides),
        in_specs=[ANY, ANY],
        out_specs=[VMEM] * sides,
        out_shape=[PIN((rows, size), bf16)] * sides,
        scratch_shapes=[
            pltpu.VMEM((sides, wears, 8, size), f32),
            pltpu.VMEM((wears, ages), f32),
            pltpu.SemaphoreType.DMA((sides + 1,)),
        ],
        compiler_params=params(16),
        cost_estimate=cost(0, 8 * wears * 8 * size),
        name="age_edges",
    )(in_hbm(u), in_hbm(hazard))


def pack_rows(ranks, halves):
    packed, row = [], 0
    for rank in ranks:
        cut = row + rank // 16 * 16
        pieces = [h[row:cut] for h in halves if cut > row]
        pieces += [h[cut : row + rank] for h in halves if cut < row + rank]
        packed.append(jnp.concatenate(pieces, axis=0).astype(bf16))
        row += rank
    return packed


def analyse(table, cells):
    return lax.dot_general(table, cells, (((1,), (1,)), ((), ())), preferred_element_type=f32)


def pack_kernel(ranks, u_ref, *refs):
    shared, refs = refs[:SHARED], refs[SHARED:]
    tables, refs = refs[:TABLES], refs[-(len(ranks) + SHARED + TABLES + 1) :]
    q_refs, send = refs[: len(ranks)], refs[len(ranks)]
    copied, sem = refs[len(ranks) + 1 : -1], refs[-1]
    _, wears, ages, size = u_ref.shape
    at = lax.axis_index("cheb")
    sources = [t.at[at] for t in tables[:1]] + list(shared) + [t.at[at] for t in tables[1:]]
    copies = [pltpu.make_async_copy(a, b, sem.at[i]) for i, (a, b) in enumerate(zip(sources, (send, *copied)))]
    for copy in copies:
        copy.start()
    copies[0].wait()
    chunk = 4
    for g in range(wears // chunk):
        halves = [
            analyse(send[...], u_ref[half, g * chunk : (g + 1) * chunk].reshape(chunk * ages, size).astype(bf16))
            for half in range(2)
        ]
        for q_ref, rows in zip(q_refs, pack_rows(ranks, halves)):
            q_ref[:, g * chunk * ages : (g + 1) * chunk * ages] = rows
    for copy in copies[1:]:
        copy.wait()


SHARED, TABLES = 1, 7


def pack(u4, hazard, tables, edge, ranks):
    _, wears, ages, size = u4.shape
    cells = wears * ages
    copied = [PIN(hazard.shape, f32)] + [PIN(t.shape[1:], f32) for t in tables[1:]]
    out = pl.pallas_call(
        functools.partial(pack_kernel, ranks),
        in_specs=[VMEM] + [ANY] * (SHARED + TABLES + len(edge)),
        out_specs=[VMEM] * (len(ranks) + SHARED + TABLES),
        out_shape=[PIN((2 * r, cells), bf16) for r in ranks] + [PIN(tables[0].shape[1:], bf16)] + copied,
        scratch_shapes=[pltpu.SemaphoreType.DMA((SHARED + TABLES,))],
        compiler_params=params(16),
        cost_estimate=cost(4 * cells * sum(ranks) * size, 8 * cells * size),
        name="pack_coefficients",
    )(in_vmem(u4), *[in_hbm(x) for x in (hazard, *tables)], *[in_vmem(x) for x in edge])
    return out[: len(ranks)], out[len(ranks)], out[len(ranks) + 1 :]


def pack_edges_kernel(ranks, sides, send_ref, *refs):
    edge_refs, q_refs = refs[:sides], refs[sides + 2 :]
    count = 2 * q_refs[0].shape[1] // sides
    halves = []
    for half in range(2):
        cells = [r[half * count // 2 : (half + 1) * count // 2] for r in edge_refs]
        halves.append(analyse(send_ref[...], jnp.concatenate(cells, axis=0)))
    for q_ref, rows in zip(q_refs, pack_rows(ranks, halves)):
        q_ref[...] = rows


def pack_edges(send, near, arrived, ranks, sides, extra):
    return pl.pallas_call(
        functools.partial(pack_edges_kernel, ranks, sides),
        in_specs=[VMEM] * (2 + sides),
        out_specs=[VMEM] * (1 + len(ranks)),
        out_shape=[PIN(arrived.shape, bf16)] + [PIN((2 * r, extra), bf16) for r in ranks],
        input_output_aliases={1 + sides: 0},
        compiler_params=params(16),
        cost_estimate=cost(0, 2**18),
        name="pack_edges",
    )(*[in_vmem(x) for x in (send, *near, arrived)])


def local_kernel(sides, u_ref, hazard, diffusion, drift, second, first, take_second, take_first, *refs):
    edge_refs, fields, (beside, ends, take, own) = refs[:sides], refs[sides : sides + SUBSTEPS], refs[sides + SUBSTEPS :]
    z = fields[0]
    halves, rows, _, _ = z.shape
    _, wears, ages, size = u_ref.shape
    for l in range(halves):
        zero = jnp.zeros((rows, 16, 128), f32)
        z[l, :, :ROW0, :] = zero
        z[l, :, ROW0 + ages :, :] = zero
        for later in fields[1:]:
            later[l, :, ROW0 - 8 : ROW0, :] = zero[:, :8]
            later[l, :, ROW0 + ages : ROW0 + ages + 8, :] = zero[:, :8]
    scaled, moved = START * diffusion[...], START * drift[...]
    own[...] = (second[...] * scaled + first[...] * moved).astype(bf16)
    take[...] = (take_second[...] * scaled + take_first[...] * moved).astype(bf16)
    keep = jnp.transpose(START - START * hazard[...])
    chunk = 4
    for w in range(0, 2 * wears, chunk):
        half, v = divmod(w, wears)
        u = u_ref[half, v : v + chunk].reshape(chunk * ages, size)
        rate = jnp.dot(u.astype(bf16), own[...], preferred_element_type=f32)
        for i in range(chunk):
            cells = slice(i * ages, (i + 1) * ages)
            value = rate[cells] + keep[:, w + i : w + i + 1] * u[cells]
            for l in range(halves):
                z[l, HALO + w + i, ROW0 : ROW0 + ages, :] = value[:, l * 128 : (l + 1) * 128]
            for e, start in enumerate((0, 2 * wears - HALO)):
                if start <= w + i < start + HALO:
                    ends[e, (w + i - start) * ages : (w + i - start + 1) * ages] = value
    for s, ref in enumerate(edge_refs):
        count = 2 * wears * HALO
        parts = ref[count : count + HAZARD_ROWS].astype(f32)
        near = START - START * (parts[:HALO, : 2 * wears] + parts[HALO : 2 * HALO, : 2 * wears])
        rate = jnp.dot(ref[:count], own[...], preferred_element_type=f32)
        for w in range(0, 2 * wears, 4):
            place = slice(w * HALO, (w + 4) * HALO)
            columns = [jnp.broadcast_to(near[:, w + j : w + j + 1], (HALO, size)) for j in range(4)]
            beside[s, place] = rate[place] + jnp.concatenate(columns, axis=0) * ref[place].astype(f32)


def local(u4, tables, near, sides):
    _, wears, ages, size = u4.shape
    cells = 2 * wears * ages
    return pl.pallas_call(
        functools.partial(local_kernel, sides),
        in_specs=[VMEM] * (1 + len(tables) + sides),
        out_specs=[VMEM] * (SUBSTEPS + 3),
        out_shape=[pltpu.VMEM((size // 128, 2 * wears + 2 * HALO, ages + 32, 128), f32)] * SUBSTEPS
        + [
            pltpu.VMEM((sides, 2 * wears * HALO, size), f32),
            pltpu.VMEM((2, HALO * ages, size), f32),
            pltpu.VMEM(tables[-1].shape, bf16),
        ],
        scratch_shapes=[pltpu.VMEM((size, size), bf16)],
        compiler_params=params(16),
        cost_estimate=cost(2 * cells * size * size, 8 * cells * size),
        name="local_rate",
    )(*[in_vmem(x) for x in (u4, *tables, *near)])


def distant(ranks, q_refs, take_ref, half, columns):
    tiles = []
    for rank, q, place in zip(ranks, q_refs, columns):
        cut = rank // 16 * 16
        if cut:
            tiles.append(q[half * cut : (half + 1) * cut, place])
        if rank > cut:
            tiles.append(q[2 * cut : 2 * rank, place])
    return lax.dot_general(
        jnp.concatenate(tiles, axis=0), take_ref[half], (((0,), (0,)), ((), ())), preferred_element_type=f32
    )


def rows_kernel(ranks, sides, wears, ages, ends_ref, beside_ref, take_ref, *refs):
    q_refs, edge_refs, out_refs = refs[: len(ranks)], refs[len(ranks) : -2], refs[-2:]
    each, corner = wears // 2 * HALO, HALO * HALO
    for half, (start, out_ref) in enumerate(zip((0, wears - HALO), out_refs)):
        v = (start - half * wears // 2) * ages
        rate = distant(ranks, q_refs, take_ref, half, [slice(v, v + HALO * ages)] * len(ranks))
        out_ref[: HALO * ages] = (rate + ends_ref[half]).astype(bf16)
        first = 0 if half == 0 else each - corner
        for s in range(sides):
            rate = distant(ranks, edge_refs, take_ref, half, [slice(s * each, (s + 1) * each)] * len(ranks))
            place = slice(start * HALO, start * HALO + corner)
            row = HALO * ages + s * corner
            out_ref[row : row + corner] = (rate[first : first + corner] + beside_ref[s, place]).astype(bf16)


def outer_rows(ends, beside, take, q, q_edges, ranks, sides, wears, ages):
    size = ends.shape[-1]
    message = PIN((HALO * ages + sides * HALO * HALO, size), bf16)
    return pl.pallas_call(
        functools.partial(rows_kernel, ranks, sides, wears, ages),
        in_specs=[VMEM] * (3 + 2 * len(ranks)),
        out_specs=[VMEM] * 2,
        out_shape=[message, message],
        compiler_params=params(16),
        cost_estimate=cost(2 * 8 * ages * take.shape[1] * size, 2**20),
        name="outer_rows",
    )(*[in_vmem(x) for x in (ends, beside, take, *q, *q_edges)])


def section_kernel(ranks, sides, wears, ages, z_in, beside_ref, take_ref, *refs):
    q_refs, edge_refs, z = refs[: len(ranks)], refs[len(ranks) : -1], refs[-1]
    halves = z.shape[0]
    each = wears // 2 * HALO
    chunk = 4
    for w in range(0, wears, chunk):
        half, v = divmod(w, wears // 2)
        rate = distant(ranks, q_refs, take_ref, half, [slice(v * ages, (v + chunk) * ages)] * len(ranks))
        for i in range(chunk):
            for l in range(halves):
                z[l, HALO + w + i, ROW0 : ROW0 + ages, :] = (
                    z_in[l, HALO + w + i, ROW0 : ROW0 + ages, :]
                    + rate[i * ages : (i + 1) * ages, l * 128 : (l + 1) * 128]
                )
    has = [jnp.where(at_end("age", i == 1), 0.0, 1.0).astype(f32) for i in range(2)]
    for s in range(sides):
        for half in range(2):
            place = slice(half * each, (half + 1) * each)
            cells = distant(ranks, edge_refs, take_ref, half, [slice(s * each, (s + 1) * each)] * len(ranks))
            cells += beside_ref[s, place]
            for i, column in ((0, ROW0 - HALO), (1, ROW0 + ages)):
                if sides == 1 or s == i:
                    part = cells * has[i]
                    for w in range(wears // 2):
                        for l in range(halves):
                            z[l, HALO + half * wears // 2 + w, column : column + HALO, :] = part[
                                w * HALO : (w + 1) * HALO, l * 128 : (l + 1) * 128
                            ]


def section(z, beside, take, q, q_edges, ranks, sides, wears, ages):
    size = z.shape[0] * 128
    cells = wears * ages
    return pl.pallas_call(
        functools.partial(section_kernel, ranks, sides, wears, ages),
        in_specs=[VMEM] * (3 + 2 * len(ranks)),
        out_specs=VMEM,
        out_shape=pltpu.VMEM(z.shape, f32),
        input_output_aliases={0: 0},
        compiler_params=params(16),
        cost_estimate=cost(2 * cells * take.shape[1] * size, 8 * cells * size),
        name="section",
    )(z, *[in_vmem(x) for x in (beside, take, *q, *q_edges)])


def lane_terms(speed_ref, l):
    speed = speed_ref[0:1, l * 128 : (l + 1) * 128]
    stay = GAIN * (1.0 - age_courant - 2.0 * wear_spread - speed)
    worn = GAIN * (speed + wear_spread)
    return stay, worn


def row_terms(src, l, w, lo, hi, stay, worn):
    t = src[l, w, lo:hi, :]
    older = src[l, w, lo + 1 : hi + 1, :]
    slope = older - src[l, w, lo - 1 : hi - 1, :]
    centre = stay * t + (GAIN * age_courant) * older
    less = (t - slope) + t
    return centre, worn * t + slope, less


def rows_step(src, l, start, stop, lo, hi, factors, put, unroll):
    def step(w, carry):
        partial, less = carry
        centre, more, new_less = row_terms(src, l, w + 1, lo, hi, *factors)
        put(w, partial + more)
        return centre + less, new_less

    _, _, less0 = row_terms(src, l, start - 1, lo, hi, *factors)
    centre1, _, less1 = row_terms(src, l, start, lo, hi, *factors)
    if stop - start == unroll:
        carry = (centre1 + less0, less1)
        for w in range(start, stop):
            carry = step(w, carry)
        return
    lax.fori_loop(start, stop, step, (centre1 + less0, less1), unroll=unroll)


def put_in(dst, l, lo, hi, keeps, factor=None):
    def put(w, out):
        if factor is not None:
            out = out * factor(w)
        if keeps is None:
            dst[l, w, lo:hi, :] = out
        else:
            dst[l, w, lo : lo + 8, :] = out[:8] * keeps[0]
            dst[l, w, lo + 8 : hi - 8, :] = out[8:-8]
            dst[l, w, hi - 8 : hi, :] = out[-8:] * keeps[1]

    return put


def by_sides(sides, ages, run):
    if sides == 1:
        pl.when(at_end("age", False))(lambda: run(ROW0, ROW0 + ages + 8, None))
        pl.when(at_end("age", True))(lambda: run(ROW0 - 8, ROW0 + ages, None))
    else:
        has = [jnp.where(at_end("age", i == 1), 0.0, 1.0).astype(f32) for i in range(2)]
        run(ROW0 - 8, ROW0 + ages + 8, [jnp.zeros((8, 128), f32) + h for h in has])


def inner_kernel(sides, z0, z1_in, z2_in, z3_in, speed_ref, o_ref, rest, z1, z2, z3, stage, out_sem):
    del z1_in, z2_in, z3_in
    halves, rows, _, _ = z0.shape
    done, ages = stage.shape[:2]
    fields = (z0, z1, z2, z3)

    def run(low, high, keeps):
        for k in range(1, SUBSTEPS):
            for l in range(halves):
                rows_step(
                    fields[k - 1], l, HALO + k, rows - HALO - k, low, high, lane_terms(speed_ref, l),
                    put_in(fields[k], l, low, high, keeps), 4,
                )
        stores = []
        first = HALO + SUBSTEPS
        bounds = [0, done * 3 // 5 // 8 * 8, done, done + rest.shape[0]]
        for a, b in zip(bounds, bounds[1:]):
            for l in range(halves):
                def put(w, out, l=l, a=a):
                    if a < done:
                        stage[w - first, :, l * 128 : (l + 1) * 128] = out
                    else:
                        rest[w - first - done, :, l * 128 : (l + 1) * 128] = out

                rows_step(
                    fields[-1], l, first + a, first + b, ROW0, ROW0 + ages, lane_terms(speed_ref, l), put, 4,
                )
            if a < done:
                copy = pltpu.make_async_copy(
                    stage.at[pl.ds(a, b - a)], o_ref.at[pl.ds(SUBSTEPS + a, b - a)], out_sem.at[len(stores)]
                )
                copy.start()
                stores.append(copy)
        for copy in stores:
            copy.wait()

    by_sides(sides, ages, run)


def inner_substeps(fields, speed, sides, wears, ages):
    z = fields[0]
    size = z.shape[0] * 128
    shape = (wears, ages, size)
    kept = 16
    return pl.pallas_call(
        functools.partial(inner_kernel, sides),
        out_shape=[jax.ShapeDtypeStruct(shape, f32), pltpu.VMEM((kept, ages, size), f32)] + [pltpu.VMEM(z.shape, f32)] * 3,
        in_specs=[VMEM] * 5,
        out_specs=[ANY] + [VMEM] * 4,
        scratch_shapes=[
            pltpu.VMEM((wears - 2 * SUBSTEPS - kept, ages, size), f32),
            pltpu.SemaphoreType.DMA((2,)),
        ],
        input_output_aliases={1: 2, 2: 3, 3: 4},
        compiler_params=params(16),
        cost_estimate=cost(10 * SUBSTEPS * wears * ages * size, 8 * wears * ages * size),
        name="inner_substeps",
    )(*[in_vmem(x) for x in fields], speed)


def outer_kernel(sides, o_in, z0_in, z1_in, z2_in, z3_in, rest, speed_ref, up_ref, down_ref, o_ref, z0, z1, z2, z3,
                 stage, out_sem):
    del o_in, z0_in, z1_in, z2_in, z3_in
    halves, rows, _, _ = z0.shape
    wears, ages = rows - 2 * HALO, stage.shape[2]
    fields = (z0, z1, z2, z3)
    count = rest.shape[0]
    stores = [pltpu.make_async_copy(rest, o_ref.at[pl.ds(wears - SUBSTEPS - count, count)], out_sem.at[2])]
    stores[0].start()
    has = [jnp.where(at_end("age", i == 1), 0.0, 1.0).astype(f32) for i in range(2)]
    near = [jnp.where(at_end("wear", i == 1), 0.0, 1.0).astype(f32) for i in range(2)]
    for l in range(halves):
        lanes = pl.ds(l * 128, 128)
        for e, (ref, at) in enumerate(((up_ref, 0), (down_ref, HALO + wears))):
            values = ref[:, lanes].astype(f32) * near[e]
            z0[l, at : at + HALO, ROW0 : ROW0 + ages, :] = values[: HALO * ages].reshape(HALO, ages, 128)
            for s in range(sides):
                corner = values[HALO * (ages + s * HALO) : HALO * (ages + (s + 1) * HALO)]
                for i, column in ((0, ROW0 - HALO), (1, ROW0 + ages)):
                    if sides == 1 or s == i:
                        part = corner * has[i]
                        for w in range(HALO):
                            z0[l, at + w, column : column + HALO, :] = part[w * HALO : (w + 1) * HALO]

    def run(low, high, keeps):
        for k in range(1, SUBSTEPS):
            for l in range(halves):
                for e, start in enumerate((k, rows - HALO - k)):
                    beyond = (lambda w: w < HALO, lambda w: w >= HALO + wears)[e]
                    rows_step(
                        fields[k - 1], l, start, start + HALO, low, high, lane_terms(speed_ref, l),
                        put_in(
                            fields[k], l, low, high, keeps,
                            lambda w, e=e, beyond=beyond: jnp.where(beyond(w), near[e], 1.0).astype(f32),
                        ), 4,
                    )
        for e, start in enumerate((HALO, rows - 2 * HALO)):
            for l in range(halves):
                def put(w, out, l=l, e=e, start=start):
                    stage[e, w - start, :, l * 128 : (l + 1) * 128] = out

                rows_step(fields[-1], l, start, start + HALO, ROW0, ROW0 + ages, lane_terms(speed_ref, l), put, 4)
            pltpu.make_async_copy(stage.at[e], o_ref.at[pl.ds(start - HALO, HALO)], out_sem.at[e]).start()

    by_sides(sides, ages, run)
    for e, start in enumerate((HALO, rows - 2 * HALO)):
        stores.append(pltpu.make_async_copy(stage.at[e], o_ref.at[pl.ds(start - HALO, HALO)], out_sem.at[e]))
    for copy in stores:
        copy.wait()


def outer_substeps(o, fields, rest, speed, up, down, sides):
    wears, ages, size = o.shape
    return pl.pallas_call(
        functools.partial(outer_kernel, sides),
        out_shape=[jax.ShapeDtypeStruct(o.shape, f32)] + [pltpu.VMEM(z.shape, f32) for z in fields],
        in_specs=[ANY] + [VMEM] * 8,
        out_specs=[ANY] + [VMEM] * 4,
        scratch_shapes=[pltpu.VMEM((2, HALO, ages, size), f32), pltpu.SemaphoreType.DMA((3,))],
        input_output_aliases={i: i for i in range(5)},
        compiler_params=params(16),
        cost_estimate=cost(20 * SUBSTEPS * 2 * HALO * ages * size, 2**20),
        name="outer_substeps",
    )(o, *[in_vmem(x) for x in (*fields, rest)], speed, in_vmem(up), in_vmem(down))[0]


def body(adjoint_value, load_diffusion, load_drift, wear_speed, hazard):
    wears, ages, size = adjoint_value.shape
    points = load_diffusion.shape[0]
    devices = points // size
    slots, send, take_second, take_first, own_second, own_first = factors(points, devices)
    ranks = tuple(rank for _, rank in slots)
    n_wear, n_age = lax.axis_size("wear"), lax.axis_size("age")
    sides = 1 if n_age == 2 else 2
    extra = sides * wears // 2 * HALO
    u4 = adjoint_value.reshape(2, wears // 2, ages, size)
    diffusion = load_diffusion.reshape(devices, 1, size)
    drift = load_drift.reshape(devices, 1, size)
    tables = [jnp.asarray(t, f32) for t in (own_second, own_first, take_second, take_first)]

    def ring(n):
        after = [(i, (i + 1) % n) for i in range(n)]
        return after, [(j, i) for i, j in after]

    most = 2 * max(ranks) * (wears // 2 * ages) // size
    edge = edges(adjoint_value, hazard, sides, max(wears * HALO + HAZARD_ROWS, -(-most // 16) * 16))
    near = [lax.ppermute(x, "age", pairs) for x, pairs in zip(edge, ring(n_age))]
    q, send, tables = pack(u4, hazard, [jnp.asarray(send, bf16), diffusion, drift, *tables], edge, ranks)
    moves = [list(pairs) for pairs, _ in slots]
    arrived = [lax.ppermute(x, "cheb", pairs) for x, pairs in zip(q, moves)]
    arrived[0], *q_edges = pack_edges(send, near, arrived[0], ranks, sides, extra)
    arrived_edges = [lax.ppermute(x, "cheb", pairs) for x, pairs in zip(q_edges, moves)]
    z, *later, beside, ends, take = local(u4, tables, near, sides)
    top, bottom = outer_rows(ends, beside, take, arrived, arrived_edges, ranks, sides, wears, ages)
    after, before = ring(n_wear)
    up, down = lax.ppermute(bottom, "wear", after), lax.ppermute(top, "wear", before)
    z = section(z, beside, take, arrived, arrived_edges, ranks, sides, wears, ages)
    speed = wear_speed.reshape(1, size)
    o, rest, *later = inner_substeps([z, *later], speed, sides, wears, ages)
    return outer_substeps(o, [z, *later], rest, speed, up, down, sides)


def solution(mesh):
    placed = (P("wear", "age", "cheb"), P(), P(), P("cheb"), P("wear", "age"))
    return jax.shard_map(
        body, mesh=mesh, in_specs=placed, out_specs=P("wear", "age", "cheb"), check_vma=False
    )
```

```python
import functools

import jax
import jax.numpy as jnp
import numpy as np
from jax import lax
from jax.experimental import pallas as pl
from jax.experimental.pallas import tpu as pltpu
from jax.sharding import PartitionSpec as P

SUBSTEPS = 4
HALO = SUBSTEPS

age_courant = 0.4
wear_spread = 0.1
coupling = 0.05
GAIN = 1.0 / coupling
START = coupling**SUBSTEPS

NEGLIGIBLE = 2.0**-32

f32 = jnp.float32
bf16 = jnp.bfloat16


def operators(points):
    modes = np.arange(points)[:, None]
    nodes = np.arange(points)[None, :]
    angles = (modes * (2 * nodes + 1)) % (4 * points) * (np.pi / (2 * points))
    cosine, sine = np.cos(angles), np.sin(angles)
    analysis = np.where(modes == 0, 1.0, 2.0) / points * cosine
    wavenumber = modes / points
    return (-(wavenumber**2) * cosine).T @ analysis, (wavenumber * sine).T @ analysis


def arrived_rows(rank):
    return -(-rank // 16) * 16


@functools.lru_cache(maxsize=None)
def factors(points, devices):
    second, first = operators(points)
    size = points // devices
    parts = [slice(b * size, (b + 1) * size) for b in range(devices)]
    slots, found = [], {}
    for shift in range(1, devices):
        pairs, most = [], 0
        for c in range(devices):
            b = c ^ shift if devices & (devices - 1) == 0 else (c + shift) % devices
            joint = np.concatenate([second[parts[b], parts[c]], first[parts[b], parts[c]]])
            _, sizes, rows = np.linalg.svd(joint, full_matrices=False)
            rank = int((sizes > NEGLIGIBLE).sum())
            rank = -(-rank // 8) * 8
            basis = rows[:rank]
            found[c, b] = (basis, second[parts[b], parts[c]] @ basis.T, first[parts[b], parts[c]] @ basis.T)
            pairs.append((c, b))
            most = max(most, rank)
        slots.append((tuple(pairs), most))
    send = np.zeros((devices, sum(rank for _, rank in slots), size))
    wide = sum(arrived_rows(rank) for _, rank in slots)
    take_second = np.zeros((devices, 2, wide, size))
    take_first = np.zeros((devices, 2, wide, size))
    at = row = 0
    for pairs, rank in slots:
        whole = rank // 16 * 16
        for c, b in pairs:
            basis, left_second, left_first = (
                np.pad(x, ((0, rank - len(found[c, b][0])), (0, 0))) for x in (found[c, b][0], found[c, b][1].T, found[c, b][2].T)
            )
            send[c, at : at + rank] = basis
            for half in range(2):
                for take, left in ((take_second, left_second), (take_first, left_first)):
                    take[b, half, row : row + whole] = left[:whole]
                    place = row + whole + half * (rank - whole)
                    take[b, half, place : place + rank - whole] = left[whole:]
        at += rank
        row += arrived_rows(rank)
    own_second = np.stack([second[p, p].T for p in parts])
    own_first = np.stack([first[p, p].T for p in parts])
    return slots, send, take_second, take_first, own_second, own_first


ANY = pl.BlockSpec(memory_space=pl.ANY)
VMEM = pl.BlockSpec(memory_space=pltpu.VMEM)
PIN = pltpu.VMEM
ROW0 = 16
HAZARD_ROWS = 16


def at_end(axis, last):
    return lax.axis_index(axis) == (lax.axis_size(axis) - 1 if last else 0)


def in_hbm(x):
    return pltpu.with_memory_space_constraint(x, pltpu.HBM)


def in_vmem(x):
    return pltpu.with_memory_space_constraint(x, pltpu.VMEM)


def params(mebibytes):
    return pltpu.CompilerParams(vmem_limit_bytes=mebibytes * 2**20)


def cost(flops, bytes_accessed):
    return pl.CostEstimate(flops=flops, bytes_accessed=bytes_accessed, transcendentals=0)


def edge_kernel(sides, u_hbm, hazard_hbm, *refs):
    out_refs, (tiles, hazard, sem) = refs[:sides], refs[sides:]
    wears, ages, size = u_hbm.shape
    copies = [pltpu.make_async_copy(hazard_hbm, hazard, sem.at[sides])]
    for i in range(sides):
        if sides == 1:
            start = pl.multiple_of(jnp.where(at_end("age", False), ages - 8, 0), 8)
        else:
            start = (ages - 8, 0)[i]
        copies.append(pltpu.make_async_copy(u_hbm.at[:, pl.ds(start, 8)], tiles.at[i], sem.at[i]))
    for copy in copies:
        copy.start()
    for copy in copies:
        copy.wait()
    by_age = jnp.transpose(hazard[...])
    last, early = by_age[ages - HALO :], by_age[:HALO]
    for i, out_ref in enumerate(out_refs):
        for w in range(0, wears, 4):
            late = [tiles[i, w + j, 8 - HALO :] for j in range(4)]
            soon = [tiles[i, w + j, :HALO] for j in range(4)]
            late, soon = jnp.concatenate(late, axis=0), jnp.concatenate(soon, axis=0)
            if sides == 1:
                cells = jnp.where(at_end("age", False), late, soon)
            else:
                cells = (late, soon)[i]
            out_ref[w * HALO : (w + 4) * HALO] = cells.astype(bf16)
        if sides == 1:
            exact = jnp.where(at_end("age", False), last, early)
        else:
            exact = (last, early)[i]
        high = exact.astype(bf16).astype(f32)
        rows = jnp.concatenate([high, exact - high, jnp.zeros((HAZARD_ROWS - 2 * HALO, wears), f32)], axis=0)
        rows = jnp.concatenate([rows, jnp.zeros((HAZARD_ROWS, size - wears), f32)], axis=1)
        out_ref[wears * HALO : wears * HALO + HAZARD_ROWS] = rows.astype(bf16)
        used = wears * HALO + HAZARD_ROWS
        if out_ref.shape[0] > used:
            out_ref[used:] = jnp.zeros((out_ref.shape[0] - used, size), bf16)


def edges(u, hazard, sides, rows):
    wears, ages, size = u.shape
    return pl.pallas_call(
        functools.partial(edge_kernel, sides),
        in_specs=[ANY, ANY],
        out_specs=[VMEM] * sides,
        out_shape=[PIN((rows, size), bf16)] * sides,
        scratch_shapes=[
            pltpu.VMEM((sides, wears, 8, size), f32),
            pltpu.VMEM((wears, ages), f32),
            pltpu.SemaphoreType.DMA((sides + 1,)),
        ],
        compiler_params=params(16),
        cost_estimate=cost(0, 8 * wears * 8 * size),
        name="age_edges",
    )(in_hbm(u), in_hbm(hazard))


def pack_rows(ranks, halves):
    packed, row = [], 0
    for rank in ranks:
        cut = row + rank // 16 * 16
        pieces = [h[row:cut] for h in halves if cut > row]
        pieces += [h[cut : row + rank] for h in halves if cut < row + rank]
        packed.append(jnp.concatenate(pieces, axis=0).astype(bf16))
        row += rank
    return packed


def analyse(table, cells):
    return lax.dot_general(table, cells, (((1,), (1,)), ((), ())), preferred_element_type=f32)


def pack_kernel(ranks, u_ref, *refs):
    shared, refs = refs[:SHARED], refs[SHARED:]
    tables, refs = refs[:TABLES], refs[-(len(ranks) + SHARED + TABLES + 1) :]
    q_refs, send = refs[: len(ranks)], refs[len(ranks)]
    copied, sem = refs[len(ranks) + 1 : -1], refs[-1]
    _, wears, ages, size = u_ref.shape
    at = lax.axis_index("cheb")
    sources = [t.at[at] for t in tables[:1]] + list(shared) + [t.at[at] for t in tables[1:]]
    copies = [pltpu.make_async_copy(a, b, sem.at[i]) for i, (a, b) in enumerate(zip(sources, (send, *copied)))]
    for copy in copies:
        copy.start()
    copies[0].wait()
    chunk = 4
    for g in range(wears // chunk):
        halves = [
            analyse(send[...], u_ref[half, g * chunk : (g + 1) * chunk].reshape(chunk * ages, size).astype(bf16))
            for half in range(2)
        ]
        for q_ref, rows in zip(q_refs, pack_rows(ranks, halves)):
            q_ref[:, g * chunk * ages : (g + 1) * chunk * ages] = rows
    for copy in copies[1:]:
        copy.wait()


SHARED, TABLES = 1, 7


def pack(u4, hazard, tables, edge, ranks):
    _, wears, ages, size = u4.shape
    cells = wears * ages
    copied = [PIN(hazard.shape, f32)] + [PIN(t.shape[1:], f32) for t in tables[1:]]
    out = pl.pallas_call(
        functools.partial(pack_kernel, ranks),
        in_specs=[VMEM] + [ANY] * (SHARED + TABLES + len(edge)),
        out_specs=[VMEM] * (len(ranks) + SHARED + TABLES),
        out_shape=[PIN((2 * r, cells), bf16) for r in ranks] + [PIN(tables[0].shape[1:], bf16)] + copied,
        scratch_shapes=[pltpu.SemaphoreType.DMA((SHARED + TABLES,))],
        compiler_params=params(16),
        cost_estimate=cost(4 * cells * sum(ranks) * size, 8 * cells * size),
        name="pack_coefficients",
    )(in_vmem(u4), *[in_hbm(x) for x in (hazard, *tables)], *[in_vmem(x) for x in edge])
    return out[: len(ranks)], out[len(ranks)], out[len(ranks) + 1 :]


def pack_edges_kernel(ranks, sides, send_ref, *refs):
    edge_refs, q_refs = refs[:sides], refs[sides + 2 :]
    count = 2 * q_refs[0].shape[1] // sides
    halves = []
    for half in range(2):
        cells = [r[half * count // 2 : (half + 1) * count // 2] for r in edge_refs]
        halves.append(analyse(send_ref[...], jnp.concatenate(cells, axis=0)))
    for q_ref, rows in zip(q_refs, pack_rows(ranks, halves)):
        q_ref[...] = rows


def pack_edges(send, near, arrived, ranks, sides, extra):
    return pl.pallas_call(
        functools.partial(pack_edges_kernel, ranks, sides),
        in_specs=[VMEM] * (2 + sides),
        out_specs=[VMEM] * (1 + len(ranks)),
        out_shape=[PIN(arrived.shape, bf16)] + [PIN((2 * r, extra), bf16) for r in ranks],
        input_output_aliases={1 + sides: 0},
        compiler_params=params(16),
        cost_estimate=cost(0, 2**18),
        name="pack_edges",
    )(*[in_vmem(x) for x in (send, *near, arrived)])


def local_kernel(sides, u_ref, hazard, diffusion, drift, second, first, take_second, take_first, *refs):
    edge_refs, fields, (beside, ends, take, own) = refs[:sides], refs[sides : sides + SUBSTEPS], refs[sides + SUBSTEPS :]
    z = fields[0]
    halves, rows, _, _ = z.shape
    _, wears, ages, size = u_ref.shape
    for l in range(halves):
        zero = jnp.zeros((rows, 16, 128), f32)
        z[l, :, :ROW0, :] = zero
        z[l, :, ROW0 + ages :, :] = zero
        for later in fields[1:]:
            later[l, :, ROW0 - 8 : ROW0, :] = zero[:, :8]
            later[l, :, ROW0 + ages : ROW0 + ages + 8, :] = zero[:, :8]
    scaled, moved = START * diffusion[...], START * drift[...]
    own[...] = (second[...] * scaled + first[...] * moved).astype(bf16)
    take[...] = (take_second[...] * scaled + take_first[...] * moved).astype(bf16)
    keep = jnp.transpose(START - START * hazard[...])
    chunk = 4
    for w in range(0, 2 * wears, chunk):
        half, v = divmod(w, wears)
        u = u_ref[half, v : v + chunk].reshape(chunk * ages, size)
        rate = jnp.dot(u.astype(bf16), own[...], preferred_element_type=f32)
        for i in range(chunk):
            cells = slice(i * ages, (i + 1) * ages)
            value = rate[cells] + keep[:, w + i : w + i + 1] * u[cells]
            for l in range(halves):
                z[l, HALO + w + i, ROW0 : ROW0 + ages, :] = value[:, l * 128 : (l + 1) * 128]
            for e, start in enumerate((0, 2 * wears - HALO)):
                if start <= w + i < start + HALO:
                    ends[e, (w + i - start) * ages : (w + i - start + 1) * ages] = value
    for s, ref in enumerate(edge_refs):
        count = 2 * wears * HALO
        parts = ref[count : count + HAZARD_ROWS].astype(f32)
        near = START - START * (parts[:HALO, : 2 * wears] + parts[HALO : 2 * HALO, : 2 * wears])
        rate = jnp.dot(ref[:count], own[...], preferred_element_type=f32)
        for w in range(0, 2 * wears, 4):
            place = slice(w * HALO, (w + 4) * HALO)
            columns = [jnp.broadcast_to(near[:, w + j : w + j + 1], (HALO, size)) for j in range(4)]
            beside[s, place] = rate[place] + jnp.concatenate(columns, axis=0) * ref[place].astype(f32)


def local(u4, tables, near, sides):
    _, wears, ages, size = u4.shape
    cells = 2 * wears * ages
    return pl.pallas_call(
        functools.partial(local_kernel, sides),
        in_specs=[VMEM] * (1 + len(tables) + sides),
        out_specs=[VMEM] * (SUBSTEPS + 3),
        out_shape=[pltpu.VMEM((size // 128, 2 * wears + 2 * HALO, ages + 32, 128), f32)] * SUBSTEPS
        + [
            pltpu.VMEM((sides, 2 * wears * HALO, size), f32),
            pltpu.VMEM((2, HALO * ages, size), f32),
            pltpu.VMEM(tables[-1].shape, bf16),
        ],
        scratch_shapes=[pltpu.VMEM((size, size), bf16)],
        compiler_params=params(16),
        cost_estimate=cost(2 * cells * size * size, 8 * cells * size),
        name="local_rate",
    )(*[in_vmem(x) for x in (u4, *tables, *near)])


def distant(ranks, q_refs, take_ref, half, columns):
    tiles = []
    for rank, q, place in zip(ranks, q_refs, columns):
        cut = rank // 16 * 16
        if cut:
            tiles.append(q[half * cut : (half + 1) * cut, place])
        if rank > cut:
            tiles.append(q[2 * cut : 2 * rank, place])
    return lax.dot_general(
        jnp.concatenate(tiles, axis=0), take_ref[half], (((0,), (0,)), ((), ())), preferred_element_type=f32
    )


def odd_age():
    return lax.rem(lax.axis_index("age"), 2) == 1


def rows_kernel(ranks, sides, wears, ages, ends_ref, beside_ref, take_ref, *refs):
    q_refs, edge_refs, out_refs = refs[: len(ranks)], refs[len(ranks) : -2], refs[-2:]
    each, corner = wears // 2 * HALO, HALO * HALO
    odd = odd_age()
    first_rows, last_rows = [], []
    for half, (start, rows) in enumerate(((0, first_rows), (wears - HALO, last_rows))):
        v = (start - half * wears // 2) * ages
        rate = distant(ranks, q_refs, take_ref, half, [slice(v, v + HALO * ages)] * len(ranks))
        rows.append(rate + ends_ref[half])
        first = 0 if half == 0 else each - corner
        for s in range(sides):
            rate = distant(ranks, edge_refs, take_ref, half, [slice(s * each, (s + 1) * each)] * len(ranks))
            rows.append(rate[first : first + corner] + beside_ref[s, start * HALO : start * HALO + corner])
    row = 0
    for top, bottom in zip(first_rows, last_rows):
        place = slice(row, row + top.shape[0])
        out_refs[0][place] = jnp.where(odd, top, bottom).astype(bf16)
        out_refs[1][place] = jnp.where(odd, bottom, top).astype(bf16)
        row += top.shape[0]


def outer_rows(ends, beside, take, q, q_edges, ranks, sides, wears, ages):
    size = ends.shape[-1]
    message = PIN((HALO * ages + sides * HALO * HALO, size), bf16)
    return pl.pallas_call(
        functools.partial(rows_kernel, ranks, sides, wears, ages),
        in_specs=[VMEM] * (3 + 2 * len(ranks)),
        out_specs=[VMEM] * 2,
        out_shape=[message, message],
        compiler_params=params(16),
        cost_estimate=cost(2 * 8 * ages * take.shape[1] * size, 2**20),
        name="outer_rows",
    )(*[in_vmem(x) for x in (ends, beside, take, *q, *q_edges)])


def section_kernel(ranks, sides, wears, ages, z_in, beside_ref, take_ref, *refs):
    q_refs, edge_refs, z = refs[: len(ranks)], refs[len(ranks) : -1], refs[-1]
    halves = z.shape[0]
    each = wears // 2 * HALO
    chunk = 4
    for w in range(0, wears, chunk):
        half, v = divmod(w, wears // 2)
        rate = distant(ranks, q_refs, take_ref, half, [slice(v * ages, (v + chunk) * ages)] * len(ranks))
        for i in range(chunk):
            for l in range(halves):
                z[l, HALO + w + i, ROW0 : ROW0 + ages, :] = (
                    z_in[l, HALO + w + i, ROW0 : ROW0 + ages, :]
                    + rate[i * ages : (i + 1) * ages, l * 128 : (l + 1) * 128]
                )
    has = [jnp.where(at_end("age", i == 1), 0.0, 1.0).astype(f32) for i in range(2)]
    for s in range(sides):
        for half in range(2):
            place = slice(half * each, (half + 1) * each)
            cells = distant(ranks, edge_refs, take_ref, half, [slice(s * each, (s + 1) * each)] * len(ranks))
            cells += beside_ref[s, place]
            for i, column in ((0, ROW0 - HALO), (1, ROW0 + ages)):
                if sides == 1 or s == i:
                    part = cells * has[i]
                    for w in range(wears // 2):
                        for l in range(halves):
                            z[l, HALO + half * wears // 2 + w, column : column + HALO, :] = part[
                                w * HALO : (w + 1) * HALO, l * 128 : (l + 1) * 128
                            ]


def section(z, beside, take, q, q_edges, ranks, sides, wears, ages):
    size = z.shape[0] * 128
    cells = wears * ages
    return pl.pallas_call(
        functools.partial(section_kernel, ranks, sides, wears, ages),
        in_specs=[VMEM] * (3 + 2 * len(ranks)),
        out_specs=VMEM,
        out_shape=pltpu.VMEM(z.shape, f32),
        input_output_aliases={0: 0},
        compiler_params=params(16),
        cost_estimate=cost(2 * cells * take.shape[1] * size, 8 * cells * size),
        name="section",
    )(z, *[in_vmem(x) for x in (beside, take, *q, *q_edges)])


def lane_terms(speed_ref, l):
    speed = speed_ref[0:1, l * 128 : (l + 1) * 128]
    stay = GAIN * (1.0 - age_courant - 2.0 * wear_spread - speed)
    worn = GAIN * (speed + wear_spread)
    return stay, worn


def row_terms(src, l, w, lo, hi, stay, worn):
    t = src[l, w, lo:hi, :]
    older = src[l, w, lo + 1 : hi + 1, :]
    slope = older - src[l, w, lo - 1 : hi - 1, :]
    centre = stay * t + (GAIN * age_courant) * older
    less = (t - slope) + t
    return centre, worn * t + slope, less


def rows_step(src, l, start, stop, lo, hi, factors, put, unroll):
    def step(w, carry):
        partial, less = carry
        centre, more, new_less = row_terms(src, l, w + 1, lo, hi, *factors)
        put(w, partial + more)
        return centre + less, new_less

    _, _, less0 = row_terms(src, l, start - 1, lo, hi, *factors)
    centre1, _, less1 = row_terms(src, l, start, lo, hi, *factors)
    if stop - start == unroll:
        carry = (centre1 + less0, less1)
        for w in range(start, stop):
            carry = step(w, carry)
        return
    lax.fori_loop(start, stop, step, (centre1 + less0, less1), unroll=unroll)


def put_in(dst, l, lo, hi, keeps, factor=None):
    def put(w, out):
        if factor is not None:
            out = out * factor(w)
        if keeps is None:
            dst[l, w, lo:hi, :] = out
        else:
            dst[l, w, lo : lo + 8, :] = out[:8] * keeps[0]
            dst[l, w, lo + 8 : hi - 8, :] = out[8:-8]
            dst[l, w, hi - 8 : hi, :] = out[-8:] * keeps[1]

    return put


def by_sides(sides, ages, run):
    if sides == 1:
        pl.when(at_end("age", False))(lambda: run(ROW0, ROW0 + ages + 8, None))
        pl.when(at_end("age", True))(lambda: run(ROW0 - 8, ROW0 + ages, None))
    else:
        has = [jnp.where(at_end("age", i == 1), 0.0, 1.0).astype(f32) for i in range(2)]
        run(ROW0 - 8, ROW0 + ages + 8, [jnp.zeros((8, 128), f32) + h for h in has])


def inner_kernel(sides, z0, z1_in, z2_in, z3_in, speed_ref, o_ref, rest, z1, z2, z3, stage, out_sem):
    del z1_in, z2_in, z3_in
    halves, rows, _, _ = z0.shape
    done, ages = stage.shape[:2]
    fields = (z0, z1, z2, z3)

    def run(low, high, keeps):
        for k in range(1, SUBSTEPS):
            for l in range(halves):
                rows_step(
                    fields[k - 1], l, HALO + k, rows - HALO - k, low, high, lane_terms(speed_ref, l),
                    put_in(fields[k], l, low, high, keeps), 4,
                )
        stores = []
        first = HALO + SUBSTEPS
        bounds = [0, done * 3 // 5 // 8 * 8, done, done + rest.shape[0]]
        for a, b in zip(bounds, bounds[1:]):
            for l in range(halves):
                def put(w, out, l=l, a=a):
                    if a < done:
                        stage[w - first, :, l * 128 : (l + 1) * 128] = out
                    else:
                        rest[w - first - done, :, l * 128 : (l + 1) * 128] = out

                rows_step(
                    fields[-1], l, first + a, first + b, ROW0, ROW0 + ages, lane_terms(speed_ref, l), put, 4,
                )
            if a < done:
                copy = pltpu.make_async_copy(
                    stage.at[pl.ds(a, b - a)], o_ref.at[pl.ds(SUBSTEPS + a, b - a)], out_sem.at[len(stores)]
                )
                copy.start()
                stores.append(copy)
        for copy in stores:
            copy.wait()

    by_sides(sides, ages, run)


def inner_substeps(fields, speed, sides, wears, ages):
    z = fields[0]
    size = z.shape[0] * 128
    shape = (wears, ages, size)
    kept = 16
    return pl.pallas_call(
        functools.partial(inner_kernel, sides),
        out_shape=[jax.ShapeDtypeStruct(shape, f32), pltpu.VMEM((kept, ages, size), f32)] + [pltpu.VMEM(z.shape, f32)] * 3,
        in_specs=[VMEM] * 5,
        out_specs=[ANY] + [VMEM] * 4,
        scratch_shapes=[
            pltpu.VMEM((wears - 2 * SUBSTEPS - kept, ages, size), f32),
            pltpu.SemaphoreType.DMA((2,)),
        ],
        input_output_aliases={1: 2, 2: 3, 3: 4},
        compiler_params=params(16),
        cost_estimate=cost(10 * SUBSTEPS * wears * ages * size, 8 * wears * ages * size),
        name="inner_substeps",
    )(*[in_vmem(x) for x in fields], speed)


def outer_kernel(sides, o_in, z0_in, z1_in, z2_in, z3_in, rest, speed_ref, first_ref, second_ref, o_ref, z0, z1, z2, z3,
                 stage, out_sem):
    del o_in, z0_in, z1_in, z2_in, z3_in
    halves, rows, _, _ = z0.shape
    wears, ages = rows - 2 * HALO, stage.shape[2]
    fields = (z0, z1, z2, z3)
    odd = odd_age()
    count = rest.shape[0]
    stores = [pltpu.make_async_copy(rest, o_ref.at[pl.ds(wears - SUBSTEPS - count, count)], out_sem.at[2])]
    stores[0].start()
    has = [jnp.where(at_end("age", i == 1), 0.0, 1.0).astype(f32) for i in range(2)]
    near = [jnp.where(at_end("wear", i == 1), 0.0, 1.0).astype(f32) for i in range(2)]
    for l in range(halves):
        lanes = pl.ds(l * 128, 128)
        first, second = first_ref[:, lanes].astype(f32), second_ref[:, lanes].astype(f32)
        for e, at in enumerate((0, HALO + wears)):
            values = jnp.where(odd, *((second, first) if e == 0 else (first, second))) * near[e]
            z0[l, at : at + HALO, ROW0 : ROW0 + ages, :] = values[: HALO * ages].reshape(HALO, ages, 128)
            for s in range(sides):
                corner = values[HALO * (ages + s * HALO) : HALO * (ages + (s + 1) * HALO)]
                for i, column in ((0, ROW0 - HALO), (1, ROW0 + ages)):
                    if sides == 1 or s == i:
                        part = corner * has[i]
                        for w in range(HALO):
                            z0[l, at + w, column : column + HALO, :] = part[w * HALO : (w + 1) * HALO]

    def run(low, high, keeps):
        for k in range(1, SUBSTEPS):
            for l in range(halves):
                for e, start in enumerate((k, rows - HALO - k)):
                    beyond = (lambda w: w < HALO, lambda w: w >= HALO + wears)[e]
                    rows_step(
                        fields[k - 1], l, start, start + HALO, low, high, lane_terms(speed_ref, l),
                        put_in(
                            fields[k], l, low, high, keeps,
                            lambda w, e=e, beyond=beyond: jnp.where(beyond(w), near[e], 1.0).astype(f32),
                        ), 4,
                    )
        for e, start in enumerate((HALO, rows - 2 * HALO)):
            for l in range(halves):
                def put(w, out, l=l, e=e, start=start):
                    stage[e, w - start, :, l * 128 : (l + 1) * 128] = out

                rows_step(fields[-1], l, start, start + HALO, ROW0, ROW0 + ages, lane_terms(speed_ref, l), put, 4)
            pltpu.make_async_copy(stage.at[e], o_ref.at[pl.ds(start - HALO, HALO)], out_sem.at[e]).start()

    by_sides(sides, ages, run)
    for e, start in enumerate((HALO, rows - 2 * HALO)):
        stores.append(pltpu.make_async_copy(stage.at[e], o_ref.at[pl.ds(start - HALO, HALO)], out_sem.at[e]))
    for copy in stores:
        copy.wait()


def outer_substeps(o, fields, rest, speed, first, second, sides):
    wears, ages, size = o.shape
    return pl.pallas_call(
        functools.partial(outer_kernel, sides),
        out_shape=[jax.ShapeDtypeStruct(o.shape, f32)] + [pltpu.VMEM(z.shape, f32) for z in fields],
        in_specs=[ANY] + [VMEM] * 8,
        out_specs=[ANY] + [VMEM] * 4,
        scratch_shapes=[pltpu.VMEM((2, HALO, ages, size), f32), pltpu.SemaphoreType.DMA((3,))],
        input_output_aliases={i: i for i in range(5)},
        compiler_params=params(16),
        cost_estimate=cost(20 * SUBSTEPS * 2 * HALO * ages * size, 2**20),
        name="outer_substeps",
    )(o, *[in_vmem(x) for x in (*fields, rest)], speed, in_vmem(first), in_vmem(second))[0]


def body(adjoint_value, load_diffusion, load_drift, wear_speed, hazard):
    wears, ages, size = adjoint_value.shape
    points = load_diffusion.shape[0]
    devices = points // size
    slots, send, take_second, take_first, own_second, own_first = factors(points, devices)
    ranks = tuple(rank for _, rank in slots)
    n_wear, n_age = lax.axis_size("wear"), lax.axis_size("age")
    sides = 1 if n_age == 2 else 2
    extra = sides * wears // 2 * HALO
    u4 = adjoint_value.reshape(2, wears // 2, ages, size)
    diffusion = load_diffusion.reshape(devices, 1, size)
    drift = load_drift.reshape(devices, 1, size)
    tables = [jnp.asarray(t, f32) for t in (own_second, own_first, take_second, take_first)]

    def ring(n):
        after = [(i, (i + 1) % n) for i in range(n)]
        return after, [(j, i) for i, j in after]

    most = 2 * max(ranks) * (wears // 2 * ages) // size
    edge = edges(adjoint_value, hazard, sides, max(wears * HALO + HAZARD_ROWS, -(-most // 16) * 16))
    near = [lax.ppermute(x, "age", pairs) for x, pairs in zip(edge, ring(n_age))]
    q, send, tables = pack(u4, hazard, [jnp.asarray(send, bf16), diffusion, drift, *tables], edge, ranks)
    moves = [list(pairs) for pairs, _ in slots]
    arrived = [lax.ppermute(x, "cheb", pairs) for x, pairs in zip(q, moves)]
    arrived[0], *q_edges = pack_edges(send, near, arrived[0], ranks, sides, extra)
    arrived_edges = [lax.ppermute(x, "cheb", pairs) for x, pairs in zip(q_edges, moves)]
    z, *later, beside, ends, take = local(u4, tables, near, sides)
    messages = outer_rows(ends, beside, take, arrived, arrived_edges, ranks, sides, wears, ages)
    around = []
    for w in range(n_wear):
        for a in range(n_age):
            to = w + 1 if a % 2 == 0 else w - 1
            if 0 <= to < n_wear:
                around.append((w * n_age + a, to * n_age + a))
            elif n_age % 2 == 0:
                around.append((w * n_age + a, w * n_age + (a ^ 1)))
    turns = (around, [(j, i) for i, j in around])
    first, second = (lax.ppermute(x, ("wear", "age"), turn) for x, turn in zip(messages, turns))
    z = section(z, beside, take, arrived, arrived_edges, ranks, sides, wears, ages)
    speed = wear_speed.reshape(1, size)
    o, rest, *later = inner_substeps([z, *later], speed, sides, wears, ages)
    return outer_substeps(o, [z, *later], rest, speed, first, second, sides)


def solution(mesh):
    placed = (P("wear", "age", "cheb"), P(), P(), P("cheb"), P("wear", "age"))
    return jax.shard_map(
        body, mesh=mesh, in_specs=placed, out_specs=P("wear", "age", "cheb"), check_vma=False
    )
```

```python
import functools

import jax
import jax.numpy as jnp
import numpy as np
from jax import lax
from jax.experimental import pallas as pl
from jax.experimental.pallas import tpu as pltpu
from jax.sharding import PartitionSpec as P

SUBSTEPS = 4
HALO = SUBSTEPS

age_courant = 0.4
wear_spread = 0.1
coupling = 0.05
GAIN = 1.0 / coupling
START = coupling**SUBSTEPS

NEGLIGIBLE = 2.0**-32

f32 = jnp.float32
bf16 = jnp.bfloat16


def operators(points):
    modes = np.arange(points)[:, None]
    nodes = np.arange(points)[None, :]
    angles = (modes * (2 * nodes + 1)) % (4 * points) * (np.pi / (2 * points))
    cosine, sine = np.cos(angles), np.sin(angles)
    analysis = np.where(modes == 0, 1.0, 2.0) / points * cosine
    wavenumber = modes / points
    return (-(wavenumber**2) * cosine).T @ analysis, (wavenumber * sine).T @ analysis


def arrived_rows(rank):
    return -(-rank // 16) * 16


@functools.lru_cache(maxsize=None)
def factors(points, devices):
    second, first = operators(points)
    size = points // devices
    parts = [slice(b * size, (b + 1) * size) for b in range(devices)]
    slots, found = [], {}
    for shift in range(1, devices):
        pairs, most = [], 0
        for c in range(devices):
            b = c ^ shift if devices & (devices - 1) == 0 else (c + shift) % devices
            joint = np.concatenate([second[parts[b], parts[c]], first[parts[b], parts[c]]])
            _, sizes, rows = np.linalg.svd(joint, full_matrices=False)
            rank = int((sizes > NEGLIGIBLE).sum())
            rank = -(-rank // 8) * 8
            basis = rows[:rank]
            found[c, b] = (basis, second[parts[b], parts[c]] @ basis.T, first[parts[b], parts[c]] @ basis.T)
            pairs.append((c, b))
            most = max(most, rank)
        slots.append((tuple(pairs), most))
    send = np.zeros((devices, sum(rank for _, rank in slots), size))
    wide = sum(arrived_rows(rank) for _, rank in slots)
    take_second = np.zeros((devices, 2, wide, size))
    take_first = np.zeros((devices, 2, wide, size))
    at = row = 0
    for pairs, rank in slots:
        whole = rank // 16 * 16
        for c, b in pairs:
            basis, left_second, left_first = (
                np.pad(x, ((0, rank - len(found[c, b][0])), (0, 0))) for x in (found[c, b][0], found[c, b][1].T, found[c, b][2].T)
            )
            send[c, at : at + rank] = basis
            for half in range(2):
                for take, left in ((take_second, left_second), (take_first, left_first)):
                    take[b, half, row : row + whole] = left[:whole]
                    place = row + whole + half * (rank - whole)
                    take[b, half, place : place + rank - whole] = left[whole:]
        at += rank
        row += arrived_rows(rank)
    own_second = np.stack([second[p, p].T for p in parts])
    own_first = np.stack([first[p, p].T for p in parts])
    return slots, send, take_second, take_first, own_second, own_first


ANY = pl.BlockSpec(memory_space=pl.ANY)
VMEM = pl.BlockSpec(memory_space=pltpu.VMEM)
PIN = pltpu.VMEM
ROW0 = 16
HAZARD_ROWS = 16


def at_end(axis, last):
    return lax.axis_index(axis) == (lax.axis_size(axis) - 1 if last else 0)


def in_hbm(x):
    return pltpu.with_memory_space_constraint(x, pltpu.HBM)


def in_vmem(x):
    return pltpu.with_memory_space_constraint(x, pltpu.VMEM)


def params(mebibytes):
    return pltpu.CompilerParams(vmem_limit_bytes=mebibytes * 2**20)


def cost(flops, bytes_accessed):
    return pl.CostEstimate(flops=flops, bytes_accessed=bytes_accessed, transcendentals=0)


def edge_kernel(sides, u_hbm, hazard_hbm, send_hbm, *refs):
    out_refs, (send, tiles, hazard, sem) = refs[:sides], refs[sides:]
    wears, ages, size = u_hbm.shape
    copies = [
        pltpu.make_async_copy(hazard_hbm, hazard, sem.at[sides]),
        pltpu.make_async_copy(send_hbm.at[lax.axis_index("cheb")], send, sem.at[sides + 1]),
    ]
    for i in range(sides):
        if sides == 1:
            start = pl.multiple_of(jnp.where(at_end("age", False), ages - 8, 0), 8)
        else:
            start = (ages - 8, 0)[i]
        copies.append(pltpu.make_async_copy(u_hbm.at[:, pl.ds(start, 8)], tiles.at[i], sem.at[i]))
    for copy in copies:
        copy.start()
    first = at_end("age", False)
    count = wears * HALO
    copies[0].wait()
    by_age = jnp.transpose(hazard[...])
    last, early = by_age[ages - HALO :], by_age[:HALO]
    for i, out_ref in enumerate(out_refs):
        exact = jnp.where(first, last, early) if sides == 1 else (last, early)[i]
        high = exact.astype(bf16).astype(f32)
        rows = jnp.concatenate([high, exact - high, jnp.zeros((HAZARD_ROWS - 2 * HALO, wears), f32)], axis=0)
        rows = jnp.concatenate([rows, jnp.zeros((HAZARD_ROWS, size - wears), f32)], axis=1)
        out_ref[count : count + HAZARD_ROWS] = rows.astype(bf16)
        if out_ref.shape[0] > count + HAZARD_ROWS:
            out_ref[count + HAZARD_ROWS :] = jnp.zeros((out_ref.shape[0] - count - HAZARD_ROWS, size), bf16)
    for copy in copies[1:]:
        copy.wait()
    for i, out_ref in enumerate(out_refs):
        for w in range(0, wears, 4):
            late = [tiles[i, w + j, 8 - HALO :] for j in range(4)]
            soon = [tiles[i, w + j, :HALO] for j in range(4)]
            late, soon = jnp.concatenate(late, axis=0), jnp.concatenate(soon, axis=0)
            cells = jnp.where(first, late, soon) if sides == 1 else (late, soon)[i]
            out_ref[w * HALO : (w + 4) * HALO] = cells.astype(bf16)


def edges(u, hazard, send, sides, rows):
    wears, ages, size = u.shape
    return pl.pallas_call(
        functools.partial(edge_kernel, sides),
        in_specs=[ANY] * 3,
        out_specs=[VMEM] * (sides + 1),
        out_shape=[PIN((rows, size), bf16)] * sides + [PIN(send.shape[1:], bf16)],
        scratch_shapes=[
            pltpu.VMEM((sides, wears, 8, size), f32),
            pltpu.VMEM((wears, ages), f32),
            pltpu.SemaphoreType.DMA((sides + 2,)),
        ],
        compiler_params=params(8),
        cost_estimate=cost(0, 8 * wears * 8 * size),
        name="age_edges",
    )(*[in_hbm(x) for x in (u, hazard, send)])


def pack_rows(ranks, halves):
    packed, row = [], 0
    for rank in ranks:
        cut = row + rank // 16 * 16
        pieces = [h[row:cut] for h in halves if cut > row]
        pieces += [h[cut : row + rank] for h in halves if cut < row + rank]
        packed.append(jnp.concatenate(pieces, axis=0).astype(bf16))
        row += rank
    return packed


def analyse(table, cells):
    return lax.dot_general(table, cells, (((1,), (1,)), ((), ())), preferred_element_type=f32)


def pack_kernel(ranks, u_ref, send, *refs):
    q_refs = refs[-len(ranks) :]
    _, wears, ages, size = u_ref.shape
    chunk = 4
    for g in range(wears // chunk):
        halves = [
            analyse(send[...], u_ref[half, g * chunk : (g + 1) * chunk].reshape(chunk * ages, size).astype(bf16))
            for half in range(2)
        ]
        for q_ref, rows in zip(q_refs, pack_rows(ranks, halves)):
            q_ref[:, g * chunk * ages : (g + 1) * chunk * ages] = rows


def pack(u4, send, edge, ranks):
    _, wears, ages, size = u4.shape
    cells = wears * ages
    return pl.pallas_call(
        functools.partial(pack_kernel, ranks),
        in_specs=[VMEM] * 2 + [ANY] * len(edge),
        out_specs=[VMEM] * len(ranks),
        out_shape=[PIN((2 * r, cells), bf16) for r in ranks],
        compiler_params=params(8),
        cost_estimate=cost(4 * cells * sum(ranks) * size, 8 * cells * size),
        name="pack_coefficients",
    )(*[in_vmem(x) for x in (u4, send, *edge)])


def pack_edges_kernel(ranks, sides, send_ref, *refs):
    edge_refs, q_refs = refs[:sides], refs[sides + 2 :]
    count = 2 * q_refs[0].shape[1] // sides
    halves = []
    for half in range(2):
        cells = [r[half * count // 2 : (half + 1) * count // 2] for r in edge_refs]
        halves.append(analyse(send_ref[...], jnp.concatenate(cells, axis=0)))
    for q_ref, rows in zip(q_refs, pack_rows(ranks, halves)):
        q_ref[...] = rows


def pack_edges(send, near, arrived, ranks, sides, extra):
    return pl.pallas_call(
        functools.partial(pack_edges_kernel, ranks, sides),
        in_specs=[VMEM] * (2 + sides),
        out_specs=[VMEM] * (1 + len(ranks)),
        out_shape=[PIN(arrived.shape, bf16)] + [PIN((2 * r, extra), bf16) for r in ranks],
        input_output_aliases={1 + sides: 0},
        compiler_params=params(8),
        cost_estimate=cost(0, 2**18),
        name="pack_edges",
    )(*[in_vmem(x) for x in (send, *near, arrived)])


def local_kernel(sides, u_ref, tables, hazard, diffusion, drift, *refs):
    edge_refs, fields, refs = refs[:sides], refs[sides : sides + SUBSTEPS], refs[sides + SUBSTEPS :]
    beside, ends, take, own = refs
    z = fields[0]
    halves, rows, _, _ = z.shape
    _, wears, ages, size = u_ref.shape
    at = lax.axis_index("cheb")
    for l in range(halves):
        zero = jnp.zeros((rows, 16, 128), f32)
        z[l, :, :ROW0, :] = zero
        z[l, :, ROW0 + ages :, :] = zero
        for later in fields[1:]:
            later[l, :, ROW0 - 8 : ROW0, :] = zero[:, :8]
            later[l, :, ROW0 + ages : ROW0 + ages + 8, :] = zero[:, :8]
    both = tables[at, 0] * (START * diffusion[at]) + tables[at, 1] * (START * drift[at])
    own[...] = both[:size].astype(bf16)
    take[...] = both[size:].reshape(take.shape).astype(bf16)
    keep = jnp.transpose(START - START * hazard[...])
    chunk = 4
    for w in range(0, 2 * wears, chunk):
        half, v = divmod(w, wears)
        u = u_ref[half, v : v + chunk].reshape(chunk * ages, size)
        rate = jnp.dot(u.astype(bf16), own[...], preferred_element_type=f32)
        for i in range(chunk):
            cells = slice(i * ages, (i + 1) * ages)
            value = rate[cells] + keep[:, w + i : w + i + 1] * u[cells]
            for l in range(halves):
                z[l, HALO + w + i, ROW0 : ROW0 + ages, :] = value[:, l * 128 : (l + 1) * 128]
            for e, start in enumerate((0, 2 * wears - HALO)):
                if start <= w + i < start + HALO:
                    ends[e, (w + i - start) * ages : (w + i - start + 1) * ages] = value
    for s, ref in enumerate(edge_refs):
        count = 2 * wears * HALO
        parts = ref[count : count + HAZARD_ROWS].astype(f32)
        near = START - START * (parts[:HALO, : 2 * wears] + parts[HALO : 2 * HALO, : 2 * wears])
        rate = jnp.dot(ref[:count], own[...], preferred_element_type=f32)
        for w in range(0, 2 * wears, 4):
            place = slice(w * HALO, (w + 4) * HALO)
            columns = [jnp.broadcast_to(near[:, w + j : w + j + 1], (HALO, size)) for j in range(4)]
            beside[s, place] = rate[place] + jnp.concatenate(columns, axis=0) * ref[place].astype(f32)


def local(u4, tables, hazard, diffusion, drift, near, sides):
    _, wears, ages, size = u4.shape
    cells = 2 * wears * ages
    wide = (tables.shape[2] - size) // 2
    return pl.pallas_call(
        functools.partial(local_kernel, sides),
        in_specs=[VMEM] * (5 + sides),
        out_specs=[VMEM] * (SUBSTEPS + 3),
        out_shape=[pltpu.VMEM((size // 128, 2 * wears + 2 * HALO, ages + 32, 128), f32)] * SUBSTEPS
        + [
            pltpu.VMEM((sides, 2 * wears * HALO, size), f32),
            pltpu.VMEM((2, HALO * ages, size), f32),
            pltpu.VMEM((2, wide, size), bf16),
        ],
        scratch_shapes=[
            pltpu.VMEM((size, size), bf16),
        ],
        compiler_params=params(8),
        cost_estimate=cost(2 * cells * size * size, 8 * cells * size),
        name="local_rate",
    )(*[in_vmem(x) for x in (u4, tables, hazard, diffusion, drift, *near)])


def distant(ranks, q_refs, take_ref, half, columns):
    tiles = []
    for rank, q, place in zip(ranks, q_refs, columns):
        cut = rank // 16 * 16
        if cut:
            tiles.append(q[half * cut : (half + 1) * cut, place])
        if rank > cut:
            tiles.append(q[2 * cut : 2 * rank, place])
    return lax.dot_general(
        jnp.concatenate(tiles, axis=0), take_ref[half], (((0,), (0,)), ((), ())), preferred_element_type=f32
    )


def odd_age():
    return lax.rem(lax.axis_index("age"), 2) == 1


def rows_kernel(ranks, sides, wears, ages, ends_ref, beside_ref, take_ref, *refs):
    q_refs, edge_refs, out_refs = refs[: len(ranks)], refs[len(ranks) : -2], refs[-2:]
    each, corner = wears // 2 * HALO, HALO * HALO
    odd = odd_age()
    first_rows, last_rows = [], []
    for half, (start, rows) in enumerate(((0, first_rows), (wears - HALO, last_rows))):
        v = (start - half * wears // 2) * ages
        rate = distant(ranks, q_refs, take_ref, half, [slice(v, v + HALO * ages)] * len(ranks))
        rows.append(rate + ends_ref[half])
        first = 0 if half == 0 else each - corner
        for s in range(sides):
            rate = distant(ranks, edge_refs, take_ref, half, [slice(s * each, (s + 1) * each)] * len(ranks))
            rows.append(rate[first : first + corner] + beside_ref[s, start * HALO : start * HALO + corner])
    row = 0
    for top, bottom in zip(first_rows, last_rows):
        place = slice(row, row + top.shape[0])
        out_refs[0][place] = jnp.where(odd, top, bottom).astype(bf16)
        out_refs[1][place] = jnp.where(odd, bottom, top).astype(bf16)
        row += top.shape[0]


def outer_rows(ends, beside, take, q, q_edges, ranks, sides, wears, ages):
    size = ends.shape[-1]
    message = PIN((HALO * ages + sides * HALO * HALO, size), bf16)
    return pl.pallas_call(
        functools.partial(rows_kernel, ranks, sides, wears, ages),
        in_specs=[VMEM] * (3 + 2 * len(ranks)),
        out_specs=[VMEM] * 2,
        out_shape=[message, message],
        compiler_params=params(8),
        cost_estimate=cost(2 * 8 * ages * take.shape[1] * size, 2**20),
        name="outer_rows",
    )(*[in_vmem(x) for x in (ends, beside, take, *q, *q_edges)])


def section_kernel(ranks, sides, wears, ages, z_in, beside_ref, take_ref, *refs):
    q_refs, edge_refs, z = refs[: len(ranks)], refs[len(ranks) : -1], refs[-1]
    halves = z.shape[0]
    each = wears // 2 * HALO
    chunk = 4
    for w in range(0, wears, chunk):
        half, v = divmod(w, wears // 2)
        rate = distant(ranks, q_refs, take_ref, half, [slice(v * ages, (v + chunk) * ages)] * len(ranks))
        for i in range(chunk):
            for l in range(halves):
                z[l, HALO + w + i, ROW0 : ROW0 + ages, :] = (
                    z_in[l, HALO + w + i, ROW0 : ROW0 + ages, :]
                    + rate[i * ages : (i + 1) * ages, l * 128 : (l + 1) * 128]
                )
    has = [jnp.where(at_end("age", i == 1), 0.0, 1.0).astype(f32) for i in range(2)]
    for s in range(sides):
        for half in range(2):
            place = slice(half * each, (half + 1) * each)
            cells = distant(ranks, edge_refs, take_ref, half, [slice(s * each, (s + 1) * each)] * len(ranks))
            cells += beside_ref[s, place]
            for i, column in ((0, ROW0 - HALO), (1, ROW0 + ages)):
                if sides == 1 or s == i:
                    part = cells * has[i]
                    for w in range(wears // 2):
                        for l in range(halves):
                            z[l, HALO + half * wears // 2 + w, column : column + HALO, :] = part[
                                w * HALO : (w + 1) * HALO, l * 128 : (l + 1) * 128
                            ]


def section(z, beside, take, q, q_edges, ranks, sides, wears, ages):
    size = z.shape[0] * 128
    cells = wears * ages
    return pl.pallas_call(
        functools.partial(section_kernel, ranks, sides, wears, ages),
        in_specs=[VMEM] * (3 + 2 * len(ranks)),
        out_specs=VMEM,
        out_shape=pltpu.VMEM(z.shape, f32),
        input_output_aliases={0: 0},
        compiler_params=params(8),
        cost_estimate=cost(2 * cells * take.shape[1] * size, 8 * cells * size),
        name="section",
    )(z, *[in_vmem(x) for x in (beside, take, *q, *q_edges)])


def lane_terms(speed_ref, l):
    speed = speed_ref[0:1, l * 128 : (l + 1) * 128]
    stay = GAIN * (1.0 - age_courant - 2.0 * wear_spread - speed)
    worn = GAIN * (speed + wear_spread)
    return stay, worn


def row_terms(src, l, w, lo, hi, stay, worn):
    t = src[l, w, lo:hi, :]
    older = src[l, w, lo + 1 : hi + 1, :]
    slope = older - src[l, w, lo - 1 : hi - 1, :]
    centre = stay * t + (GAIN * age_courant) * older
    less = (t - slope) + t
    return centre, worn * t + slope, less


def rows_step(src, l, start, stop, lo, hi, factors, put, unroll):
    def step(w, carry):
        partial, less = carry
        centre, more, new_less = row_terms(src, l, w + 1, lo, hi, *factors)
        put(w, partial + more)
        return centre + less, new_less

    _, _, less0 = row_terms(src, l, start - 1, lo, hi, *factors)
    centre1, _, less1 = row_terms(src, l, start, lo, hi, *factors)
    if stop - start == unroll:
        carry = (centre1 + less0, less1)
        for w in range(start, stop):
            carry = step(w, carry)
        return
    lax.fori_loop(start, stop, step, (centre1 + less0, less1), unroll=unroll)


def put_in(dst, l, lo, hi, keeps, beyond=None, factor=None):
    def put(w, out):
        if factor is not None and beyond(w):
            out = out * factor
        if keeps is None:
            dst[l, w, lo:hi, :] = out
        else:
            dst[l, w, lo : lo + 8, :] = out[:8] * keeps[0]
            dst[l, w, lo + 8 : hi - 8, :] = out[8:-8]
            dst[l, w, hi - 8 : hi, :] = out[-8:] * keeps[1]

    return put


def by_sides(sides, ages, run):
    if sides == 1:
        pl.when(at_end("age", False))(lambda: run(ROW0, ROW0 + ages + 8, None))
        pl.when(at_end("age", True))(lambda: run(ROW0 - 8, ROW0 + ages, None))
    else:
        has = [jnp.where(at_end("age", i == 1), 0.0, 1.0).astype(f32) for i in range(2)]
        run(ROW0 - 8, ROW0 + ages + 8, [jnp.zeros((8, 128), f32) + h for h in has])


def inner_kernel(sides, z0, z1_in, z2_in, z3_in, speed_ref, o_ref, rest, z1, z2, z3, stage, out_sem):
    del z1_in, z2_in, z3_in
    halves, rows, _, _ = z0.shape
    done, ages = stage.shape[:2]
    fields = (z0, z1, z2, z3)

    def run(low, high, keeps):
        for k in range(1, SUBSTEPS):
            for l in range(halves):
                rows_step(
                    fields[k - 1], l, HALO + k, rows - HALO - k, low, high, lane_terms(speed_ref, l),
                    put_in(fields[k], l, low, high, keeps), 4,
                )
        stores = []
        first = HALO + SUBSTEPS
        bounds = [0, done * 3 // 5 // 8 * 8, done, done + rest.shape[0]]
        for a, b in zip(bounds, bounds[1:]):
            for l in range(halves):
                def put(w, out, l=l, a=a):
                    if a < done:
                        stage[w - first, :, l * 128 : (l + 1) * 128] = out
                    else:
                        rest[w - first - done, :, l * 128 : (l + 1) * 128] = out

                rows_step(
                    fields[-1], l, first + a, first + b, ROW0, ROW0 + ages, lane_terms(speed_ref, l), put, 4,
                )
            if a < done:
                copy = pltpu.make_async_copy(
                    stage.at[pl.ds(a, b - a)], o_ref.at[pl.ds(SUBSTEPS + a, b - a)], out_sem.at[len(stores)]
                )
                copy.start()
                stores.append(copy)
        for copy in stores:
            copy.wait()

    by_sides(sides, ages, run)


def inner_substeps(fields, speed, sides, wears, ages):
    z = fields[0]
    size = z.shape[0] * 128
    shape = (wears, ages, size)
    kept = 16
    return pl.pallas_call(
        functools.partial(inner_kernel, sides),
        out_shape=[jax.ShapeDtypeStruct(shape, f32), pltpu.VMEM((kept, ages, size), f32)] + [pltpu.VMEM(z.shape, f32)] * 3,
        in_specs=[VMEM] * 5,
        out_specs=[ANY] + [VMEM] * 4,
        scratch_shapes=[
            pltpu.VMEM((wears - 2 * SUBSTEPS - kept, ages, size), f32),
            pltpu.SemaphoreType.DMA((2,)),
        ],
        input_output_aliases={1: 2, 2: 3, 3: 4},
        compiler_params=params(8),
        cost_estimate=cost(10 * SUBSTEPS * wears * ages * size, 8 * wears * ages * size),
        name="inner_substeps",
    )(*[in_vmem(x) for x in fields], speed)


def outer_kernel(sides, o_in, z0_in, z1_in, z2_in, z3_in, rest, speed_ref, first_ref, second_ref, o_ref, z0, z1, z2, z3,
                 stage, out_sem):
    del o_in, z0_in, z1_in, z2_in, z3_in
    halves, rows, _, _ = z0.shape
    wears, ages = rows - 2 * HALO, stage.shape[2]
    fields = (z0, z1, z2, z3)
    odd = odd_age()
    count = rest.shape[0]
    stores = [pltpu.make_async_copy(rest, o_ref.at[pl.ds(wears - SUBSTEPS - count, count)], out_sem.at[2])]
    stores[0].start()
    has = [jnp.where(at_end("age", i == 1), 0.0, 1.0).astype(f32) for i in range(2)]
    near = [jnp.where(at_end("wear", i == 1), 0.0, 1.0).astype(f32) for i in range(2)]
    for l in range(halves):
        lanes = pl.ds(l * 128, 128)
        first, second = first_ref[:, lanes].astype(f32), second_ref[:, lanes].astype(f32)
        for e, at in enumerate((0, HALO + wears)):
            values = jnp.where(odd, *((second, first) if e == 0 else (first, second))) * near[e]
            z0[l, at : at + HALO, ROW0 : ROW0 + ages, :] = values[: HALO * ages].reshape(HALO, ages, 128)
            for s in range(sides):
                corner = values[HALO * (ages + s * HALO) : HALO * (ages + (s + 1) * HALO)]
                for i, column in ((0, ROW0 - HALO), (1, ROW0 + ages)):
                    if sides == 1 or s == i:
                        part = corner * has[i]
                        for w in range(HALO):
                            z0[l, at + w, column : column + HALO, :] = part[w * HALO : (w + 1) * HALO]

    def run(low, high, keeps):
        for k in range(1, SUBSTEPS):
            for l in range(halves):
                for e, start in enumerate((k, rows - HALO - k)):
                    beyond = (lambda w: w < HALO, lambda w: w >= HALO + wears)[e]
                    rows_step(
                        fields[k - 1], l, start, start + HALO, low, high, lane_terms(speed_ref, l),
                        put_in(fields[k], l, low, high, keeps, beyond, near[e]), HALO,
                    )
        for e, start in enumerate((HALO, rows - 2 * HALO)):
            for l in range(halves):
                def put(w, out, l=l, e=e, start=start):
                    stage[e, w - start, :, l * 128 : (l + 1) * 128] = out

                rows_step(fields[-1], l, start, start + HALO, ROW0, ROW0 + ages, lane_terms(speed_ref, l), put, 4)
            pltpu.make_async_copy(stage.at[e], o_ref.at[pl.ds(start - HALO, HALO)], out_sem.at[e]).start()

    by_sides(sides, ages, run)
    for e, start in enumerate((HALO, rows - 2 * HALO)):
        stores.append(pltpu.make_async_copy(stage.at[e], o_ref.at[pl.ds(start - HALO, HALO)], out_sem.at[e]))
    for copy in stores:
        copy.wait()


def outer_substeps(o, fields, rest, speed, first, second, sides):
    wears, ages, size = o.shape
    return pl.pallas_call(
        functools.partial(outer_kernel, sides),
        out_shape=[jax.ShapeDtypeStruct(o.shape, f32)] + [pltpu.VMEM(z.shape, f32) for z in fields],
        in_specs=[ANY] + [VMEM] * 8,
        out_specs=[ANY] + [VMEM] * 4,
        scratch_shapes=[pltpu.VMEM((2, HALO, ages, size), f32), pltpu.SemaphoreType.DMA((3,))],
        input_output_aliases={i: i for i in range(5)},
        compiler_params=params(8),
        cost_estimate=cost(20 * SUBSTEPS * 2 * HALO * ages * size, 2**20),
        name="outer_substeps",
    )(o, *[in_vmem(x) for x in (*fields, rest)], speed, in_vmem(first), in_vmem(second))[0]


def body(adjoint_value, load_diffusion, load_drift, wear_speed, hazard):
    wears, ages, size = adjoint_value.shape
    points = load_diffusion.shape[0]
    devices = points // size
    slots, send, take_second, take_first, own_second, own_first = factors(points, devices)
    ranks = tuple(rank for _, rank in slots)
    n_wear, n_age = lax.axis_size("wear"), lax.axis_size("age")
    sides = 1 if n_age == 2 else 2
    extra = sides * wears // 2 * HALO
    u4 = adjoint_value.reshape(2, wears // 2, ages, size)
    sides = 1 if n_age == 2 else 2
    extra = sides * wears // 2 * HALO
    u4 = adjoint_value.reshape(2, wears // 2, ages, size)
    diffusion = load_diffusion.reshape(devices, 1, size)
    drift = load_drift.reshape(devices, 1, size)
    tables = np.stack(
        [
            np.concatenate([own, take.reshape(devices, -1, size)], axis=1)
            for own, take in ((own_second, take_second), (own_first, take_first))
        ],
        axis=1,
    )
    diffusion = load_diffusion.reshape(devices, 1, size)
    drift = load_drift.reshape(devices, 1, size)

    def ring(n):
        after = [(i, (i + 1) % n) for i in range(n)]
        return after, [(j, i) for i, j in after]

    most = 2 * max(ranks) * (wears // 2 * ages) // size
    *edge, send = edges(adjoint_value, hazard, jnp.asarray(send, bf16), sides, max(wears * HALO + HAZARD_ROWS, -(-most // 16) * 16))
    near = [lax.ppermute(x, "age", pairs) for x, pairs in zip(edge, ring(n_age))]
    q = pack(u4, send, edge, ranks)
    moves = [list(pairs) for pairs, _ in slots]
    arrived = [lax.ppermute(x, "cheb", pairs) for x, pairs in zip(q, moves)]
    arrived[0], *q_edges = pack_edges(send, near, arrived[0], ranks, sides, extra)
    arrived_edges = [lax.ppermute(x, "cheb", pairs) for x, pairs in zip(q_edges, moves)]
    z, *later, beside, ends, take = local(u4, jnp.asarray(tables, f32), hazard, diffusion, drift, near, sides)
    messages = outer_rows(ends, beside, take, arrived, arrived_edges, ranks, sides, wears, ages)
    around = []
    for w in range(n_wear):
        for a in range(n_age):
            to = w + 1 if a % 2 == 0 else w - 1
            if 0 <= to < n_wear:
                around.append((w * n_age + a, to * n_age + a))
            elif n_age % 2 == 0:
                around.append((w * n_age + a, w * n_age + (a ^ 1)))
    turns = (around, [(j, i) for i, j in around])
    first, second = (lax.ppermute(x, ("wear", "age"), turn) for x, turn in zip(messages, turns))
    z = section(z, beside, take, arrived, arrived_edges, ranks, sides, wears, ages)
    speed = wear_speed.reshape(1, size)
    o, rest, *later = inner_substeps([z, *later], speed, sides, wears, ages)
    return outer_substeps(o, [z, *later], rest, speed, first, second, sides)


def solution(mesh):
    placed = (P("wear", "age", "cheb"), P(), P(), P("cheb"), P("wear", "age"))
    return jax.shard_map(
        body, mesh=mesh, in_specs=placed, out_specs=P("wear", "age", "cheb"), check_vma=False
    )
```

```python
import functools

import jax
import jax.numpy as jnp
import numpy as np
from jax import lax
from jax.experimental import pallas as pl
from jax.experimental.pallas import tpu as pltpu
from jax.sharding import PartitionSpec as P

SUBSTEPS = 4
HALO = SUBSTEPS

age_courant = 0.4
wear_spread = 0.1
coupling = 0.05
GAIN = 1.0 / coupling
START = coupling**SUBSTEPS

NEGLIGIBLE = 2.0**-32

f32 = jnp.float32
bf16 = jnp.bfloat16


def operators(points):
    modes = np.arange(points)[:, None]
    nodes = np.arange(points)[None, :]
    angles = (modes * (2 * nodes + 1)) % (4 * points) * (np.pi / (2 * points))
    cosine, sine = np.cos(angles), np.sin(angles)
    analysis = np.where(modes == 0, 1.0, 2.0) / points * cosine
    wavenumber = modes / points
    return (-(wavenumber**2) * cosine).T @ analysis, (wavenumber * sine).T @ analysis


def arrived_rows(rank):
    return -(-rank // 16) * 16


@functools.lru_cache(maxsize=None)
def factors(points, devices):
    second, first = operators(points)
    size = points // devices
    parts = [slice(b * size, (b + 1) * size) for b in range(devices)]
    slots, found = [], {}
    for shift in range(1, devices):
        pairs, most = [], 0
        for c in range(devices):
            b = c ^ shift if devices & (devices - 1) == 0 else (c + shift) % devices
            joint = np.concatenate([second[parts[b], parts[c]], first[parts[b], parts[c]]])
            _, sizes, rows = np.linalg.svd(joint, full_matrices=False)
            rank = int((sizes > NEGLIGIBLE).sum())
            rank = -(-rank // 8) * 8
            basis = rows[:rank]
            found[c, b] = (basis, second[parts[b], parts[c]] @ basis.T, first[parts[b], parts[c]] @ basis.T)
            pairs.append((c, b))
            most = max(most, rank)
        slots.append((tuple(pairs), most))
    send = np.zeros((devices, sum(rank for _, rank in slots), size))
    wide = sum(arrived_rows(rank) for _, rank in slots)
    take_second = np.zeros((devices, 2, wide, size))
    take_first = np.zeros((devices, 2, wide, size))
    at = row = 0
    for pairs, rank in slots:
        whole = rank // 16 * 16
        for c, b in pairs:
            basis, left_second, left_first = (
                np.pad(x, ((0, rank - len(found[c, b][0])), (0, 0))) for x in (found[c, b][0], found[c, b][1].T, found[c, b][2].T)
            )
            send[c, at : at + rank] = basis
            for half in range(2):
                for take, left in ((take_second, left_second), (take_first, left_first)):
                    take[b, half, row : row + whole] = left[:whole]
                    place = row + whole + half * (rank - whole)
                    take[b, half, place : place + rank - whole] = left[whole:]
        at += rank
        row += arrived_rows(rank)
    own_second = np.stack([second[p, p].T for p in parts])
    own_first = np.stack([first[p, p].T for p in parts])
    return slots, send, take_second, take_first, own_second, own_first


ANY = pl.BlockSpec(memory_space=pl.ANY)
VMEM = pl.BlockSpec(memory_space=pltpu.VMEM)
PIN = pltpu.VMEM
ROW0 = 16
HAZARD_ROWS = 16


def at_end(axis, last):
    return lax.axis_index(axis) == (lax.axis_size(axis) - 1 if last else 0)


def in_hbm(x):
    return pltpu.with_memory_space_constraint(x, pltpu.HBM)


def in_vmem(x):
    return pltpu.with_memory_space_constraint(x, pltpu.VMEM)


def params(mebibytes):
    return pltpu.CompilerParams(vmem_limit_bytes=mebibytes * 2**20)


def cost(flops, bytes_accessed):
    return pl.CostEstimate(flops=flops, bytes_accessed=bytes_accessed, transcendentals=0)


def edge_kernel(sides, u_hbm, hazard_hbm, send_hbm, *refs):
    out_refs, (send, tiles, hazard, sem) = refs[:sides], refs[sides:]
    wears, ages, size = u_hbm.shape
    copies = [
        pltpu.make_async_copy(hazard_hbm, hazard, sem.at[sides]),
        pltpu.make_async_copy(send_hbm.at[lax.axis_index("cheb")], send, sem.at[sides + 1]),
    ]
    for i in range(sides):
        if sides == 1:
            start = pl.multiple_of(jnp.where(at_end("age", False), ages - 8, 0), 8)
        else:
            start = (ages - 8, 0)[i]
        copies.append(pltpu.make_async_copy(u_hbm.at[:, pl.ds(start, 8)], tiles.at[i], sem.at[i]))
    for copy in copies:
        copy.start()
    first = at_end("age", False)
    count = wears * HALO
    copies[0].wait()
    by_age = jnp.transpose(hazard[...])
    last, early = by_age[ages - HALO :], by_age[:HALO]
    for i, out_ref in enumerate(out_refs):
        exact = jnp.where(first, last, early) if sides == 1 else (last, early)[i]
        high = exact.astype(bf16).astype(f32)
        rows = jnp.concatenate([high, exact - high, jnp.zeros((HAZARD_ROWS - 2 * HALO, wears), f32)], axis=0)
        rows = jnp.concatenate([rows, jnp.zeros((HAZARD_ROWS, size - wears), f32)], axis=1)
        out_ref[count : count + HAZARD_ROWS] = rows.astype(bf16)
        if out_ref.shape[0] > count + HAZARD_ROWS:
            out_ref[count + HAZARD_ROWS :] = jnp.zeros((out_ref.shape[0] - count - HAZARD_ROWS, size), bf16)
    for copy in copies[1:]:
        copy.wait()
    for i, out_ref in enumerate(out_refs):
        for w in range(0, wears, 4):
            late = [tiles[i, w + j, 8 - HALO :] for j in range(4)]
            soon = [tiles[i, w + j, :HALO] for j in range(4)]
            late, soon = jnp.concatenate(late, axis=0), jnp.concatenate(soon, axis=0)
            cells = jnp.where(first, late, soon) if sides == 1 else (late, soon)[i]
            out_ref[w * HALO : (w + 4) * HALO] = cells.astype(bf16)


def edges(u, hazard, send, sides, rows):
    wears, ages, size = u.shape
    return pl.pallas_call(
        functools.partial(edge_kernel, sides),
        in_specs=[ANY] * 3,
        out_specs=[VMEM] * (sides + 1),
        out_shape=[PIN((rows, size), bf16)] * sides + [PIN(send.shape[1:], bf16)],
        scratch_shapes=[
            pltpu.VMEM((sides, wears, 8, size), f32),
            pltpu.VMEM((wears, ages), f32),
            pltpu.SemaphoreType.DMA((sides + 2,)),
        ],
        compiler_params=params(8),
        cost_estimate=cost(0, 8 * wears * 8 * size),
        name="age_edges",
    )(*[in_hbm(x) for x in (u, hazard, send)])


def pack_rows(ranks, halves):
    packed, row = [], 0
    for rank in ranks:
        cut = row + rank // 16 * 16
        pieces = [h[row:cut] for h in halves if cut > row]
        pieces += [h[cut : row + rank] for h in halves if cut < row + rank]
        packed.append(jnp.concatenate(pieces, axis=0).astype(bf16))
        row += rank
    return packed


def analyse(table, cells):
    return lax.dot_general(table, cells, (((1,), (1,)), ((), ())), preferred_element_type=f32)


def pack_kernel(ranks, u_ref, send, *refs):
    q_refs = refs[-len(ranks) :]
    _, wears, ages, size = u_ref.shape
    chunk = 4
    for g in range(wears // chunk):
        halves = [
            analyse(send[...], u_ref[half, g * chunk : (g + 1) * chunk].reshape(chunk * ages, size).astype(bf16))
            for half in range(2)
        ]
        for q_ref, rows in zip(q_refs, pack_rows(ranks, halves)):
            q_ref[:, g * chunk * ages : (g + 1) * chunk * ages] = rows


def pack(u4, send, edge, ranks):
    _, wears, ages, size = u4.shape
    cells = wears * ages
    return pl.pallas_call(
        functools.partial(pack_kernel, ranks),
        in_specs=[VMEM] * 2 + [ANY] * len(edge),
        out_specs=[VMEM] * len(ranks),
        out_shape=[PIN((2 * r, cells), bf16) for r in ranks],
        compiler_params=params(8),
        cost_estimate=cost(4 * cells * sum(ranks) * size, 8 * cells * size),
        name="pack_coefficients",
    )(*[in_vmem(x) for x in (u4, send, *edge)])


def pack_edges_kernel(ranks, sides, send_ref, *refs):
    edge_refs, q_refs = refs[:sides], refs[sides + 2 :]
    count = 2 * q_refs[0].shape[1] // sides
    halves = []
    for half in range(2):
        cells = [r[half * count // 2 : (half + 1) * count // 2] for r in edge_refs]
        halves.append(analyse(send_ref[...], jnp.concatenate(cells, axis=0)))
    for q_ref, rows in zip(q_refs, pack_rows(ranks, halves)):
        q_ref[...] = rows


def pack_edges(send, near, arrived, ranks, sides, extra):
    return pl.pallas_call(
        functools.partial(pack_edges_kernel, ranks, sides),
        in_specs=[VMEM] * (2 + sides),
        out_specs=[VMEM] * (1 + len(ranks)),
        out_shape=[PIN(arrived.shape, bf16)] + [PIN((2 * r, extra), bf16) for r in ranks],
        input_output_aliases={1 + sides: 0},
        compiler_params=params(8),
        cost_estimate=cost(0, 2**18),
        name="pack_edges",
    )(*[in_vmem(x) for x in (send, *near, arrived)])


def own_rate(u, own):
    return jnp.dot(jnp.concatenate([u, u], axis=1), own[...], preferred_element_type=f32)


def local_kernel(sides, u_ref, tables, hazard, diffusion, drift, *refs):
    edge_refs, fields, refs = refs[:sides], refs[sides : sides + SUBSTEPS], refs[sides + SUBSTEPS :]
    beside, ends, take, own = refs
    z = fields[0]
    halves, rows, _, _ = z.shape
    _, wears, ages, size = u_ref.shape
    at = lax.axis_index("cheb")
    for l in range(halves):
        zero = jnp.zeros((rows, 16, 128), f32)
        z[l, :, :ROW0, :] = zero
        z[l, :, ROW0 + ages :, :] = zero
        for later in fields[1:]:
            later[l, :, ROW0 - 8 : ROW0, :] = zero[:, :8]
            later[l, :, ROW0 + ages : ROW0 + ages + 8, :] = zero[:, :8]
    both = tables[at, 0] * (START * diffusion[at]) + tables[at, 1] * (START * drift[at])
    high = both[:size].astype(bf16)
    own[:size] = high
    own[size:] = (both[:size] - high.astype(f32)).astype(bf16)
    take[...] = both[size:].reshape(take.shape).astype(bf16)
    keep = jnp.transpose(START - START * hazard[...])
    chunk = 4
    for w in range(0, 2 * wears, chunk):
        half, v = divmod(w, wears)
        u = u_ref[half, v : v + chunk].reshape(chunk * ages, size)
        rate = own_rate(u.astype(bf16), own)
        for i in range(chunk):
            cells = slice(i * ages, (i + 1) * ages)
            value = rate[cells] + keep[:, w + i : w + i + 1] * u[cells]
            for l in range(halves):
                z[l, HALO + w + i, ROW0 : ROW0 + ages, :] = value[:, l * 128 : (l + 1) * 128]
            for e, start in enumerate((0, 2 * wears - HALO)):
                if start <= w + i < start + HALO:
                    ends[e, (w + i - start) * ages : (w + i - start + 1) * ages] = value
    for s, ref in enumerate(edge_refs):
        count = 2 * wears * HALO
        parts = ref[count : count + HAZARD_ROWS].astype(f32)
        near = START - START * (parts[:HALO, : 2 * wears] + parts[HALO : 2 * HALO, : 2 * wears])
        rate = own_rate(ref[:count], own)
        for w in range(0, 2 * wears, 4):
            place = slice(w * HALO, (w + 4) * HALO)
            columns = [jnp.broadcast_to(near[:, w + j : w + j + 1], (HALO, size)) for j in range(4)]
            beside[s, place] = rate[place] + jnp.concatenate(columns, axis=0) * ref[place].astype(f32)


def local(u4, tables, hazard, diffusion, drift, near, sides):
    _, wears, ages, size = u4.shape
    cells = 2 * wears * ages
    wide = (tables.shape[2] - size) // 2
    return pl.pallas_call(
        functools.partial(local_kernel, sides),
        in_specs=[VMEM] * (5 + sides),
        out_specs=[VMEM] * (SUBSTEPS + 3),
        out_shape=[pltpu.VMEM((size // 128, 2 * wears + 2 * HALO, ages + 32, 128), f32)] * SUBSTEPS
        + [
            pltpu.VMEM((sides, 2 * wears * HALO, size), f32),
            pltpu.VMEM((2, HALO * ages, size), f32),
            pltpu.VMEM((2, wide, size), bf16),
        ],
        scratch_shapes=[pltpu.VMEM((2 * size, size), bf16)],
        compiler_params=params(8),
        cost_estimate=cost(4 * cells * size * size, 8 * cells * size),
        name="local_rate",
    )(*[in_vmem(x) for x in (u4, tables, hazard, diffusion, drift, *near)])


def distant(ranks, q_refs, take_ref, half, columns):
    tiles = []
    for rank, q, place in zip(ranks, q_refs, columns):
        cut = rank // 16 * 16
        if cut:
            tiles.append(q[half * cut : (half + 1) * cut, place])
        if rank > cut:
            tiles.append(q[2 * cut : 2 * rank, place])
    return lax.dot_general(
        jnp.concatenate(tiles, axis=0), take_ref[half], (((0,), (0,)), ((), ())), preferred_element_type=f32
    )


def odd_age():
    return lax.rem(lax.axis_index("age"), 2) == 1


def rows_kernel(ranks, sides, wears, ages, ends_ref, beside_ref, take_ref, *refs):
    q_refs, edge_refs, out_refs = refs[: len(ranks)], refs[len(ranks) : -2], refs[-2:]
    each, corner = wears // 2 * HALO, HALO * HALO
    odd = odd_age()
    first_rows, last_rows = [], []
    for half, (start, rows) in enumerate(((0, first_rows), (wears - HALO, last_rows))):
        v = (start - half * wears // 2) * ages
        rate = distant(ranks, q_refs, take_ref, half, [slice(v, v + HALO * ages)] * len(ranks))
        rows.append(rate + ends_ref[half])
        first = 0 if half == 0 else each - corner
        for s in range(sides):
            rate = distant(ranks, edge_refs, take_ref, half, [slice(s * each, (s + 1) * each)] * len(ranks))
            rows.append(rate[first : first + corner] + beside_ref[s, start * HALO : start * HALO + corner])
    row = 0
    for top, bottom in zip(first_rows, last_rows):
        place = slice(row, row + top.shape[0])
        out_refs[0][place] = jnp.where(odd, top, bottom).astype(bf16)
        out_refs[1][place] = jnp.where(odd, bottom, top).astype(bf16)
        row += top.shape[0]


def outer_rows(ends, beside, take, q, q_edges, ranks, sides, wears, ages):
    size = ends.shape[-1]
    message = PIN((HALO * ages + sides * HALO * HALO, size), bf16)
    return pl.pallas_call(
        functools.partial(rows_kernel, ranks, sides, wears, ages),
        in_specs=[VMEM] * (3 + 2 * len(ranks)),
        out_specs=[VMEM] * 2,
        out_shape=[message, message],
        compiler_params=params(8),
        cost_estimate=cost(2 * 8 * ages * take.shape[1] * size, 2**20),
        name="outer_rows",
    )(*[in_vmem(x) for x in (ends, beside, take, *q, *q_edges)])


def section_kernel(ranks, sides, wears, ages, z_in, beside_ref, take_ref, *refs):
    q_refs, edge_refs, z = refs[: len(ranks)], refs[len(ranks) : -1], refs[-1]
    halves = z.shape[0]
    each = wears // 2 * HALO
    chunk = 4
    for w in range(0, wears, chunk):
        half, v = divmod(w, wears // 2)
        rate = distant(ranks, q_refs, take_ref, half, [slice(v * ages, (v + chunk) * ages)] * len(ranks))
        for i in range(chunk):
            for l in range(halves):
                z[l, HALO + w + i, ROW0 : ROW0 + ages, :] = (
                    z_in[l, HALO + w + i, ROW0 : ROW0 + ages, :]
                    + rate[i * ages : (i + 1) * ages, l * 128 : (l + 1) * 128]
                )
    has = [jnp.where(at_end("age", i == 1), 0.0, 1.0).astype(f32) for i in range(2)]
    for s in range(sides):
        for half in range(2):
            place = slice(half * each, (half + 1) * each)
            cells = distant(ranks, edge_refs, take_ref, half, [slice(s * each, (s + 1) * each)] * len(ranks))
            cells += beside_ref[s, place]
            for i, column in ((0, ROW0 - HALO), (1, ROW0 + ages)):
                if sides == 1 or s == i:
                    part = cells * has[i]
                    for w in range(wears // 2):
                        for l in range(halves):
                            z[l, HALO + half * wears // 2 + w, column : column + HALO, :] = part[
                                w * HALO : (w + 1) * HALO, l * 128 : (l + 1) * 128
                            ]


def section(z, beside, take, q, q_edges, ranks, sides, wears, ages):
    size = z.shape[0] * 128
    cells = wears * ages
    return pl.pallas_call(
        functools.partial(section_kernel, ranks, sides, wears, ages),
        in_specs=[VMEM] * (3 + 2 * len(ranks)),
        out_specs=VMEM,
        out_shape=pltpu.VMEM(z.shape, f32),
        input_output_aliases={0: 0},
        compiler_params=params(8),
        cost_estimate=cost(2 * cells * take.shape[1] * size, 8 * cells * size),
        name="section",
    )(z, *[in_vmem(x) for x in (beside, take, *q, *q_edges)])


def lane_terms(speed_ref, l):
    speed = speed_ref[0:1, l * 128 : (l + 1) * 128]
    stay = GAIN * (1.0 - age_courant - 2.0 * wear_spread - speed)
    worn = GAIN * (speed + wear_spread)
    return stay, worn


def row_terms(src, l, w, lo, hi, stay, worn):
    t = src[l, w, lo:hi, :]
    older = src[l, w, lo + 1 : hi + 1, :]
    slope = older - src[l, w, lo - 1 : hi - 1, :]
    centre = stay * t + (GAIN * age_courant) * older
    less = (t - slope) + t
    return centre, worn * t + slope, less


def rows_step(src, l, start, stop, lo, hi, factors, put, unroll):
    def step(w, carry):
        partial, less = carry
        centre, more, new_less = row_terms(src, l, w + 1, lo, hi, *factors)
        put(w, partial + more)
        return centre + less, new_less

    _, _, less0 = row_terms(src, l, start - 1, lo, hi, *factors)
    centre1, _, less1 = row_terms(src, l, start, lo, hi, *factors)
    if stop - start == unroll:
        carry = (centre1 + less0, less1)
        for w in range(start, stop):
            carry = step(w, carry)
        return
    lax.fori_loop(start, stop, step, (centre1 + less0, less1), unroll=unroll)


def put_in(dst, l, lo, hi, keeps, beyond=None, factor=None):
    def put(w, out):
        if factor is not None and beyond(w):
            out = out * factor
        if keeps is None:
            dst[l, w, lo:hi, :] = out
        else:
            dst[l, w, lo : lo + 8, :] = out[:8] * keeps[0]
            dst[l, w, lo + 8 : hi - 8, :] = out[8:-8]
            dst[l, w, hi - 8 : hi, :] = out[-8:] * keeps[1]

    return put


def by_sides(sides, ages, run):
    if sides == 1:
        pl.when(at_end("age", False))(lambda: run(ROW0, ROW0 + ages + 8, None))
        pl.when(at_end("age", True))(lambda: run(ROW0 - 8, ROW0 + ages, None))
    else:
        has = [jnp.where(at_end("age", i == 1), 0.0, 1.0).astype(f32) for i in range(2)]
        run(ROW0 - 8, ROW0 + ages + 8, [jnp.zeros((8, 128), f32) + h for h in has])


def inner_kernel(sides, z0, z1_in, z2_in, z3_in, speed_ref, o_ref, rest, z1, z2, z3, stage, out_sem):
    del z1_in, z2_in, z3_in
    halves, rows, _, _ = z0.shape
    done, ages = stage.shape[:2]
    fields = (z0, z1, z2, z3)

    def run(low, high, keeps):
        for k in range(1, SUBSTEPS):
            for l in range(halves):
                rows_step(
                    fields[k - 1], l, HALO + k, rows - HALO - k, low, high, lane_terms(speed_ref, l),
                    put_in(fields[k], l, low, high, keeps), 4,
                )
        stores = []
        first = HALO + SUBSTEPS
        bounds = [0, done * 3 // 5 // 8 * 8, done, done + rest.shape[0]]
        for a, b in zip(bounds, bounds[1:]):
            for l in range(halves):
                def put(w, out, l=l, a=a):
                    if a < done:
                        stage[w - first, :, l * 128 : (l + 1) * 128] = out
                    else:
                        rest[w - first - done, :, l * 128 : (l + 1) * 128] = out

                rows_step(
                    fields[-1], l, first + a, first + b, ROW0, ROW0 + ages, lane_terms(speed_ref, l), put, 4,
                )
            if a < done:
                copy = pltpu.make_async_copy(
                    stage.at[pl.ds(a, b - a)], o_ref.at[pl.ds(SUBSTEPS + a, b - a)], out_sem.at[len(stores)]
                )
                copy.start()
                stores.append(copy)
        for copy in stores:
            copy.wait()

    by_sides(sides, ages, run)


def inner_substeps(fields, speed, sides, wears, ages):
    z = fields[0]
    size = z.shape[0] * 128
    shape = (wears, ages, size)
    kept = 16
    return pl.pallas_call(
        functools.partial(inner_kernel, sides),
        out_shape=[jax.ShapeDtypeStruct(shape, f32), pltpu.VMEM((kept, ages, size), f32)] + [pltpu.VMEM(z.shape, f32)] * 3,
        in_specs=[VMEM] * 5,
        out_specs=[ANY] + [VMEM] * 4,
        scratch_shapes=[
            pltpu.VMEM((wears - 2 * SUBSTEPS - kept, ages, size), f32),
            pltpu.SemaphoreType.DMA((2,)),
        ],
        input_output_aliases={1: 2, 2: 3, 3: 4},
        compiler_params=params(8),
        cost_estimate=cost(10 * SUBSTEPS * wears * ages * size, 8 * wears * ages * size),
        name="inner_substeps",
    )(*[in_vmem(x) for x in fields], speed)


def outer_kernel(sides, o_in, z0_in, z1_in, z2_in, z3_in, rest, speed_ref, first_ref, second_ref, o_ref, z0, z1, z2, z3,
                 stage, out_sem):
    del o_in, z0_in, z1_in, z2_in, z3_in
    halves, rows, _, _ = z0.shape
    wears, ages = rows - 2 * HALO, stage.shape[2]
    fields = (z0, z1, z2, z3)
    odd = odd_age()
    count = rest.shape[0]
    stores = [pltpu.make_async_copy(rest, o_ref.at[pl.ds(wears - SUBSTEPS - count, count)], out_sem.at[2])]
    stores[0].start()
    has = [jnp.where(at_end("age", i == 1), 0.0, 1.0).astype(f32) for i in range(2)]
    near = [jnp.where(at_end("wear", i == 1), 0.0, 1.0).astype(f32) for i in range(2)]
    for l in range(halves):
        lanes = pl.ds(l * 128, 128)
        first, second = first_ref[:, lanes].astype(f32), second_ref[:, lanes].astype(f32)
        for e, at in enumerate((0, HALO + wears)):
            values = jnp.where(odd, *((second, first) if e == 0 else (first, second))) * near[e]
            z0[l, at : at + HALO, ROW0 : ROW0 + ages, :] = values[: HALO * ages].reshape(HALO, ages, 128)
            for s in range(sides):
                corner = values[HALO * (ages + s * HALO) : HALO * (ages + (s + 1) * HALO)]
                for i, column in ((0, ROW0 - HALO), (1, ROW0 + ages)):
                    if sides == 1 or s == i:
                        part = corner * has[i]
                        for w in range(HALO):
                            z0[l, at + w, column : column + HALO, :] = part[w * HALO : (w + 1) * HALO]

    def run(low, high, keeps):
        for k in range(1, SUBSTEPS):
            for l in range(halves):
                for e, start in enumerate((k, rows - HALO - k)):
                    beyond = (lambda w: w < HALO, lambda w: w >= HALO + wears)[e]
                    rows_step(
                        fields[k - 1], l, start, start + HALO, low, high, lane_terms(speed_ref, l),
                        put_in(fields[k], l, low, high, keeps, beyond, near[e]), HALO,
                    )
        for e, start in enumerate((HALO, rows - 2 * HALO)):
            for l in range(halves):
                def put(w, out, l=l, e=e, start=start):
                    stage[e, w - start, :, l * 128 : (l + 1) * 128] = out

                rows_step(fields[-1], l, start, start + HALO, ROW0, ROW0 + ages, lane_terms(speed_ref, l), put, 4)
            pltpu.make_async_copy(stage.at[e], o_ref.at[pl.ds(start - HALO, HALO)], out_sem.at[e]).start()

    by_sides(sides, ages, run)
    for e, start in enumerate((HALO, rows - 2 * HALO)):
        stores.append(pltpu.make_async_copy(stage.at[e], o_ref.at[pl.ds(start - HALO, HALO)], out_sem.at[e]))
    for copy in stores:
        copy.wait()


def outer_substeps(o, fields, rest, speed, first, second, sides):
    wears, ages, size = o.shape
    return pl.pallas_call(
        functools.partial(outer_kernel, sides),
        out_shape=[jax.ShapeDtypeStruct(o.shape, f32)] + [pltpu.VMEM(z.shape, f32) for z in fields],
        in_specs=[ANY] + [VMEM] * 8,
        out_specs=[ANY] + [VMEM] * 4,
        scratch_shapes=[pltpu.VMEM((2, HALO, ages, size), f32), pltpu.SemaphoreType.DMA((3,))],
        input_output_aliases={i: i for i in range(5)},
        compiler_params=params(8),
        cost_estimate=cost(20 * SUBSTEPS * 2 * HALO * ages * size, 2**20),
        name="outer_substeps",
    )(o, *[in_vmem(x) for x in (*fields, rest)], speed, in_vmem(first), in_vmem(second))[0]


def body(adjoint_value, load_diffusion, load_drift, wear_speed, hazard):
    wears, ages, size = adjoint_value.shape
    points = load_diffusion.shape[0]
    devices = points // size
    slots, send, take_second, take_first, own_second, own_first = factors(points, devices)
    ranks = tuple(rank for _, rank in slots)
    n_wear, n_age = lax.axis_size("wear"), lax.axis_size("age")
    sides = 1 if n_age == 2 else 2
    extra = sides * wears // 2 * HALO
    u4 = adjoint_value.reshape(2, wears // 2, ages, size)
    sides = 1 if n_age == 2 else 2
    extra = sides * wears // 2 * HALO
    u4 = adjoint_value.reshape(2, wears // 2, ages, size)
    diffusion = load_diffusion.reshape(devices, 1, size)
    drift = load_drift.reshape(devices, 1, size)
    tables = np.stack(
        [
            np.concatenate([own, take.reshape(devices, -1, size)], axis=1)
            for own, take in ((own_second, take_second), (own_first, take_first))
        ],
        axis=1,
    )
    diffusion = load_diffusion.reshape(devices, 1, size)
    drift = load_drift.reshape(devices, 1, size)

    def ring(n):
        after = [(i, (i + 1) % n) for i in range(n)]
        return after, [(j, i) for i, j in after]

    most = 2 * max(ranks) * (wears // 2 * ages) // size
    *edge, send = edges(adjoint_value, hazard, jnp.asarray(send, bf16), sides, max(wears * HALO + HAZARD_ROWS, -(-most // 16) * 16))
    near = [lax.ppermute(x, "age", pairs) for x, pairs in zip(edge, ring(n_age))]
    q = pack(u4, send, edge, ranks)
    moves = [list(pairs) for pairs, _ in slots]
    arrived = [lax.ppermute(x, "cheb", pairs) for x, pairs in zip(q, moves)]
    arrived[0], *q_edges = pack_edges(send, near, arrived[0], ranks, sides, extra)
    arrived_edges = [lax.ppermute(x, "cheb", pairs) for x, pairs in zip(q_edges, moves)]
    z, *later, beside, ends, take = local(u4, jnp.asarray(tables, f32), hazard, diffusion, drift, near, sides)
    messages = outer_rows(ends, beside, take, arrived, arrived_edges, ranks, sides, wears, ages)
    around = []
    for w in range(n_wear):
        for a in range(n_age):
            to = w + 1 if a % 2 == 0 else w - 1
            if 0 <= to < n_wear:
                around.append((w * n_age + a, to * n_age + a))
            elif n_age % 2 == 0:
                around.append((w * n_age + a, w * n_age + (a ^ 1)))
    turns = (around, [(j, i) for i, j in around])
    first, second = (lax.ppermute(x, ("wear", "age"), turn) for x, turn in zip(messages, turns))
    z = section(z, beside, take, arrived, arrived_edges, ranks, sides, wears, ages)
    speed = wear_speed.reshape(1, size)
    o, rest, *later = inner_substeps([z, *later], speed, sides, wears, ages)
    return outer_substeps(o, [z, *later], rest, speed, first, second, sides)


def solution(mesh):
    placed = (P("wear", "age", "cheb"), P(), P(), P("cheb"), P("wear", "age"))
    return jax.shard_map(
        body, mesh=mesh, in_specs=placed, out_specs=P("wear", "age", "cheb"), check_vma=False
    )
```

```python
import functools

import jax
import jax.numpy as jnp
import numpy as np
from jax import lax
from jax.experimental import pallas as pl
from jax.experimental.pallas import tpu as pltpu
from jax.sharding import PartitionSpec as P

SUBSTEPS = 4
HALO = SUBSTEPS

age_courant = 0.4
wear_spread = 0.1
coupling = 0.05
GAIN = 1.0 / coupling
START = coupling**SUBSTEPS

NEGLIGIBLE = 2.0**-32

f32 = jnp.float32
bf16 = jnp.bfloat16


def operators(points):
    modes = np.arange(points)[:, None]
    nodes = np.arange(points)[None, :]
    angles = (modes * (2 * nodes + 1)) % (4 * points) * (np.pi / (2 * points))
    cosine, sine = np.cos(angles), np.sin(angles)
    analysis = np.where(modes == 0, 1.0, 2.0) / points * cosine
    wavenumber = modes / points
    return (-(wavenumber**2) * cosine).T @ analysis, (wavenumber * sine).T @ analysis


def arrived_rows(rank):
    return -(-rank // 16) * 16


@functools.lru_cache(maxsize=None)
def factors(points, devices):
    second, first = operators(points)
    size = points // devices
    parts = [slice(b * size, (b + 1) * size) for b in range(devices)]
    slots, found = [], {}
    for shift in range(1, devices):
        pairs, most = [], 0
        for c in range(devices):
            b = c ^ shift if devices & (devices - 1) == 0 else (c + shift) % devices
            joint = np.concatenate([second[parts[b], parts[c]], first[parts[b], parts[c]]])
            _, sizes, rows = np.linalg.svd(joint, full_matrices=False)
            rank = int((sizes > NEGLIGIBLE).sum())
            rank = -(-rank // 8) * 8
            basis = rows[:rank]
            found[c, b] = (basis, second[parts[b], parts[c]] @ basis.T, first[parts[b], parts[c]] @ basis.T)
            pairs.append((c, b))
            most = max(most, rank)
        slots.append((tuple(pairs), most))
    send = np.zeros((devices, sum(rank for _, rank in slots), size))
    wide = sum(arrived_rows(rank) for _, rank in slots)
    take_second = np.zeros((devices, 2, wide, size))
    take_first = np.zeros((devices, 2, wide, size))
    at = row = 0
    for pairs, rank in slots:
        whole = rank // 16 * 16
        for c, b in pairs:
            basis, left_second, left_first = (
                np.pad(x, ((0, rank - len(found[c, b][0])), (0, 0))) for x in (found[c, b][0], found[c, b][1].T, found[c, b][2].T)
            )
            send[c, at : at + rank] = basis
            for half in range(2):
                for take, left in ((take_second, left_second), (take_first, left_first)):
                    take[b, half, row : row + whole] = left[:whole]
                    place = row + whole + half * (rank - whole)
                    take[b, half, place : place + rank - whole] = left[whole:]
        at += rank
        row += arrived_rows(rank)
    own_second = np.stack([second[p, p].T for p in parts])
    own_first = np.stack([first[p, p].T for p in parts])
    return slots, send, take_second, take_first, own_second, own_first


ANY = pl.BlockSpec(memory_space=pl.ANY)
VMEM = pl.BlockSpec(memory_space=pltpu.VMEM)
PIN = pltpu.VMEM
ROW0 = 16
HAZARD_ROWS = 16


def at_end(axis, last):
    return lax.axis_index(axis) == (lax.axis_size(axis) - 1 if last else 0)


def in_hbm(x):
    return pltpu.with_memory_space_constraint(x, pltpu.HBM)


def in_vmem(x):
    return pltpu.with_memory_space_constraint(x, pltpu.VMEM)


def params(mebibytes):
    return pltpu.CompilerParams(vmem_limit_bytes=mebibytes * 2**20)


def cost(flops, bytes_accessed):
    return pl.CostEstimate(flops=flops, bytes_accessed=bytes_accessed, transcendentals=0)


def edge_kernel(sides, u_hbm, hazard_hbm, send_hbm, *refs):
    out_refs, (send, tiles, hazard, sem) = refs[:sides], refs[sides:]
    wears, ages, size = u_hbm.shape
    copies = [
        pltpu.make_async_copy(hazard_hbm, hazard, sem.at[sides]),
        pltpu.make_async_copy(send_hbm.at[lax.axis_index("cheb")], send, sem.at[sides + 1]),
    ]
    for i in range(sides):
        if sides == 1:
            start = pl.multiple_of(jnp.where(at_end("age", False), ages - 8, 0), 8)
        else:
            start = (ages - 8, 0)[i]
        copies.append(pltpu.make_async_copy(u_hbm.at[:, pl.ds(start, 8)], tiles.at[i], sem.at[i]))
    for copy in copies:
        copy.start()
    first = at_end("age", False)
    count = wears * HALO
    copies[0].wait()
    by_age = jnp.transpose(hazard[...])
    last, early = by_age[ages - HALO :], by_age[:HALO]
    for i, out_ref in enumerate(out_refs):
        exact = jnp.where(first, last, early) if sides == 1 else (last, early)[i]
        high = exact.astype(bf16).astype(f32)
        rows = jnp.concatenate([high, exact - high, jnp.zeros((HAZARD_ROWS - 2 * HALO, wears), f32)], axis=0)
        rows = jnp.concatenate([rows, jnp.zeros((HAZARD_ROWS, size - wears), f32)], axis=1)
        out_ref[count : count + HAZARD_ROWS] = rows.astype(bf16)
        if out_ref.shape[0] > count + HAZARD_ROWS:
            out_ref[count + HAZARD_ROWS :] = jnp.zeros((out_ref.shape[0] - count - HAZARD_ROWS, size), bf16)
    for copy in copies[1:]:
        copy.wait()
    for i, out_ref in enumerate(out_refs):
        for w in range(0, wears, 4):
            late = [tiles[i, w + j, 8 - HALO :] for j in range(4)]
            soon = [tiles[i, w + j, :HALO] for j in range(4)]
            late, soon = jnp.concatenate(late, axis=0), jnp.concatenate(soon, axis=0)
            cells = jnp.where(first, late, soon) if sides == 1 else (late, soon)[i]
            out_ref[w * HALO : (w + 4) * HALO] = cells.astype(bf16)


def edges(u, hazard, send, sides, rows):
    wears, ages, size = u.shape
    return pl.pallas_call(
        functools.partial(edge_kernel, sides),
        in_specs=[ANY] * 3,
        out_specs=[VMEM] * (sides + 1),
        out_shape=[PIN((rows, size), bf16)] * sides + [PIN(send.shape[1:], bf16)],
        scratch_shapes=[
            pltpu.VMEM((sides, wears, 8, size), f32),
            pltpu.VMEM((wears, ages), f32),
            pltpu.SemaphoreType.DMA((sides + 2,)),
        ],
        compiler_params=params(8),
        cost_estimate=cost(0, 8 * wears * 8 * size),
        name="age_edges",
    )(*[in_hbm(x) for x in (u, hazard, send)])


def pack_rows(ranks, halves):
    packed, row = [], 0
    for rank in ranks:
        cut = row + rank // 16 * 16
        pieces = [h[row:cut] for h in halves if cut > row]
        pieces += [h[cut : row + rank] for h in halves if cut < row + rank]
        packed.append(jnp.concatenate(pieces, axis=0).astype(bf16))
        row += rank
    return packed


def analyse(table, cells):
    return lax.dot_general(table, cells, (((1,), (1,)), ((), ())), preferred_element_type=f32)


def pack_kernel(ranks, u_ref, send, *refs):
    q_refs = refs[-len(ranks) :]
    _, wears, ages, size = u_ref.shape
    chunk = 4
    for g in range(wears // chunk):
        halves = [
            analyse(send[...], u_ref[half, g * chunk : (g + 1) * chunk].reshape(chunk * ages, size).astype(bf16))
            for half in range(2)
        ]
        for q_ref, rows in zip(q_refs, pack_rows(ranks, halves)):
            q_ref[:, g * chunk * ages : (g + 1) * chunk * ages] = rows


def pack(u4, send, edge, ranks):
    _, wears, ages, size = u4.shape
    cells = wears * ages
    return pl.pallas_call(
        functools.partial(pack_kernel, ranks),
        in_specs=[VMEM] * 2 + [ANY] * len(edge),
        out_specs=[VMEM] * len(ranks),
        out_shape=[PIN((2 * r, cells), bf16) for r in ranks],
        compiler_params=params(8),
        cost_estimate=cost(4 * cells * sum(ranks) * size, 8 * cells * size),
        name="pack_coefficients",
    )(*[in_vmem(x) for x in (u4, send, *edge)])


def pack_edges_kernel(ranks, sides, send_ref, *refs):
    edge_refs, q_refs = refs[:sides], refs[sides + 2 :]
    count = 2 * q_refs[0].shape[1] // sides
    halves = []
    for half in range(2):
        cells = [r[half * count // 2 : (half + 1) * count // 2] for r in edge_refs]
        halves.append(analyse(send_ref[...], jnp.concatenate(cells, axis=0)))
    for q_ref, rows in zip(q_refs, pack_rows(ranks, halves)):
        q_ref[...] = rows


def pack_edges(send, near, arrived, ranks, sides, extra):
    return pl.pallas_call(
        functools.partial(pack_edges_kernel, ranks, sides),
        in_specs=[VMEM] * (2 + sides),
        out_specs=[VMEM] * (1 + len(ranks)),
        out_shape=[PIN(arrived.shape, bf16)] + [PIN((2 * r, extra), bf16) for r in ranks],
        input_output_aliases={1 + sides: 0},
        compiler_params=params(8),
        cost_estimate=cost(0, 2**18),
        name="pack_edges",
    )(*[in_vmem(x) for x in (send, *near, arrived)])


def own_rate(u, own):
    return jnp.dot(jnp.concatenate([u, u], axis=1), own[...], preferred_element_type=f32)


def local_kernel(sides, u_ref, tables, hazard, diffusion, drift, *refs):
    edge_refs, fields, refs = refs[:sides], refs[sides : sides + SUBSTEPS], refs[sides + SUBSTEPS :]
    beside, ends, take, own = refs
    z = fields[0]
    halves, rows, _, _ = z.shape
    _, wears, ages, size = u_ref.shape
    at = lax.axis_index("cheb")
    for l in range(halves):
        zero = jnp.zeros((rows, 16, 128), f32)
        z[l, :, :ROW0, :] = zero
        z[l, :, ROW0 + ages :, :] = zero
        for later in fields[1:]:
            later[l, :, ROW0 - 8 : ROW0, :] = zero[:, :8]
            later[l, :, ROW0 + ages : ROW0 + ages + 8, :] = zero[:, :8]
    both = tables[at, 0] * (START * diffusion[at]) + tables[at, 1] * (START * drift[at])
    high = both[:size].astype(bf16)
    own[:size] = high
    own[size:] = (both[:size] - high.astype(f32)).astype(bf16)
    take[...] = both[size:].reshape(take.shape).astype(bf16)
    keep = jnp.transpose(START - START * hazard[...])
    chunk = 4
    for w in range(0, 2 * wears, chunk):
        half, v = divmod(w, wears)
        u = u_ref[half, v : v + chunk].reshape(chunk * ages, size)
        rate = own_rate(u.astype(bf16), own)
        for i in range(chunk):
            cells = slice(i * ages, (i + 1) * ages)
            value = rate[cells] + keep[:, w + i : w + i + 1] * u[cells]
            for l in range(halves):
                z[l, HALO + w + i, ROW0 : ROW0 + ages, :] = value[:, l * 128 : (l + 1) * 128]
            for e, start in enumerate((0, 2 * wears - HALO)):
                if start <= w + i < start + HALO:
                    ends[e, (w + i - start) * ages : (w + i - start + 1) * ages] = value
    for s, ref in enumerate(edge_refs):
        count = 2 * wears * HALO
        parts = ref[count : count + HAZARD_ROWS].astype(f32)
        near = START - START * (parts[:HALO, : 2 * wears] + parts[HALO : 2 * HALO, : 2 * wears])
        rate = own_rate(ref[:count], own)
        for w in range(0, 2 * wears, 4):
            place = slice(w * HALO, (w + 4) * HALO)
            columns = [jnp.broadcast_to(near[:, w + j : w + j + 1], (HALO, size)) for j in range(4)]
            beside[s, place] = rate[place] + jnp.concatenate(columns, axis=0) * ref[place].astype(f32)


def local(u4, tables, hazard, diffusion, drift, near, sides):
    _, wears, ages, size = u4.shape
    cells = 2 * wears * ages
    wide = (tables.shape[2] - size) // 2
    return pl.pallas_call(
        functools.partial(local_kernel, sides),
        in_specs=[VMEM] * (5 + sides),
        out_specs=[VMEM] * (SUBSTEPS + 3),
        out_shape=[pltpu.VMEM((size // 128, 2 * wears + 2 * HALO, ages + 32, 128), f32)] * SUBSTEPS
        + [
            pltpu.VMEM((sides, 2 * wears * HALO, size), f32),
            pltpu.VMEM((2, HALO * ages, size), f32),
            pltpu.VMEM((2, wide, size), bf16),
        ],
        scratch_shapes=[pltpu.VMEM((2 * size, size), bf16)],
        compiler_params=params(8),
        cost_estimate=cost(4 * cells * size * size, 8 * cells * size),
        name="local_rate",
    )(*[in_vmem(x) for x in (u4, tables, hazard, diffusion, drift, *near)])


def distant(ranks, q_refs, take_ref, half, columns):
    tiles = []
    for rank, q, place in zip(ranks, q_refs, columns):
        cut = rank // 16 * 16
        if cut:
            tiles.append(q[half * cut : (half + 1) * cut, place])
        if rank > cut:
            tiles.append(q[2 * cut : 2 * rank, place])
    return lax.dot_general(
        jnp.concatenate(tiles, axis=0), take_ref[half], (((0,), (0,)), ((), ())), preferred_element_type=f32
    )


def odd_age():
    return lax.rem(lax.axis_index("age"), 2) == 1


def rows_kernel(ranks, sides, wears, ages, ends_ref, beside_ref, take_ref, *refs):
    q_refs, edge_refs, out_refs = refs[: len(ranks)], refs[len(ranks) : -2], refs[-2:]
    each, corner = wears // 2 * HALO, HALO * HALO
    odd = odd_age()
    first_rows, last_rows = [], []
    for half, (start, rows) in enumerate(((0, first_rows), (wears - HALO, last_rows))):
        v = (start - half * wears // 2) * ages
        rate = distant(ranks, q_refs, take_ref, half, [slice(v, v + HALO * ages)] * len(ranks))
        rows.append(rate + ends_ref[half])
        first = 0 if half == 0 else each - corner
        for s in range(sides):
            rate = distant(ranks, edge_refs, take_ref, half, [slice(s * each, (s + 1) * each)] * len(ranks))
            rows.append(rate[first : first + corner] + beside_ref[s, start * HALO : start * HALO + corner])
    row = 0
    for top, bottom in zip(first_rows, last_rows):
        place = slice(row, row + top.shape[0])
        out_refs[0][place] = jnp.where(odd, top, bottom).astype(bf16)
        out_refs[1][place] = jnp.where(odd, bottom, top).astype(bf16)
        row += top.shape[0]


def outer_rows(ends, beside, take, q, q_edges, ranks, sides, wears, ages):
    size = ends.shape[-1]
    message = PIN((HALO * ages + sides * HALO * HALO, size), bf16)
    return pl.pallas_call(
        functools.partial(rows_kernel, ranks, sides, wears, ages),
        in_specs=[VMEM] * (3 + 2 * len(ranks)),
        out_specs=[VMEM] * 2,
        out_shape=[message, message],
        compiler_params=params(8),
        cost_estimate=cost(2 * 8 * ages * take.shape[1] * size, 2**20),
        name="outer_rows",
    )(*[in_vmem(x) for x in (ends, beside, take, *q, *q_edges)])


def section_kernel(ranks, sides, wears, ages, z_in, beside_ref, take_ref, *refs):
    q_refs, edge_refs, z = refs[: len(ranks)], refs[len(ranks) : -1], refs[-1]
    halves = z.shape[0]
    each = wears // 2 * HALO
    chunk = 4
    for w in range(0, wears, chunk):
        half, v = divmod(w, wears // 2)
        rate = distant(ranks, q_refs, take_ref, half, [slice(v * ages, (v + chunk) * ages)] * len(ranks))
        for i in range(chunk):
            for l in range(halves):
                z[l, HALO + w + i, ROW0 : ROW0 + ages, :] = (
                    z_in[l, HALO + w + i, ROW0 : ROW0 + ages, :]
                    + rate[i * ages : (i + 1) * ages, l * 128 : (l + 1) * 128]
                )
    has = [jnp.where(at_end("age", i == 1), 0.0, 1.0).astype(f32) for i in range(2)]
    for s in range(sides):
        for half in range(2):
            place = slice(half * each, (half + 1) * each)
            cells = distant(ranks, edge_refs, take_ref, half, [slice(s * each, (s + 1) * each)] * len(ranks))
            cells += beside_ref[s, place]
            for i, column in ((0, ROW0 - HALO), (1, ROW0 + ages)):
                if sides == 1 or s == i:
                    part = cells * has[i]
                    for w in range(wears // 2):
                        for l in range(halves):
                            z[l, HALO + half * wears // 2 + w, column : column + HALO, :] = part[
                                w * HALO : (w + 1) * HALO, l * 128 : (l + 1) * 128
                            ]


def section(z, beside, take, q, q_edges, ranks, sides, wears, ages):
    size = z.shape[0] * 128
    cells = wears * ages
    return pl.pallas_call(
        functools.partial(section_kernel, ranks, sides, wears, ages),
        in_specs=[VMEM] * (3 + 2 * len(ranks)),
        out_specs=VMEM,
        out_shape=pltpu.VMEM(z.shape, f32),
        input_output_aliases={0: 0},
        compiler_params=params(8),
        cost_estimate=cost(2 * cells * take.shape[1] * size, 8 * cells * size),
        name="section",
    )(z, *[in_vmem(x) for x in (beside, take, *q, *q_edges)])


def lane_terms(speed_ref, l):
    speed = speed_ref[0:1, l * 128 : (l + 1) * 128]
    stay = GAIN * (1.0 - age_courant - 2.0 * wear_spread - speed)
    worn = GAIN * (speed + wear_spread)
    return stay, worn


def row_terms(src, l, w, lo, hi, stay, worn):
    t = src[l, w, lo:hi, :]
    older = src[l, w, lo + 1 : hi + 1, :]
    slope = older - src[l, w, lo - 1 : hi - 1, :]
    centre = stay * t + (GAIN * age_courant) * older
    less = (t - slope) + t
    return centre, worn * t + slope, less


def rows_step(src, l, start, stop, lo, hi, factors, put, unroll):
    def step(w, carry):
        partial, less = carry
        centre, more, new_less = row_terms(src, l, w + 1, lo, hi, *factors)
        put(w, partial + more)
        return centre + less, new_less

    _, _, less0 = row_terms(src, l, start - 1, lo, hi, *factors)
    centre1, _, less1 = row_terms(src, l, start, lo, hi, *factors)
    if stop - start == unroll:
        carry = (centre1 + less0, less1)
        for w in range(start, stop):
            carry = step(w, carry)
        return
    lax.fori_loop(start, stop, step, (centre1 + less0, less1), unroll=unroll)


def put_in(dst, l, lo, hi, keeps, beyond=None, factor=None):
    def put(w, out):
        if factor is not None and beyond(w):
            out = out * factor
        if keeps is None:
            dst[l, w, lo:hi, :] = out
        else:
            dst[l, w, lo : lo + 8, :] = out[:8] * keeps[0]
            dst[l, w, lo + 8 : hi - 8, :] = out[8:-8]
            dst[l, w, hi - 8 : hi, :] = out[-8:] * keeps[1]

    return put


def by_sides(sides, ages, run):
    if sides == 1:
        pl.when(at_end("age", False))(lambda: run(ROW0, ROW0 + ages + 8, None))
        pl.when(at_end("age", True))(lambda: run(ROW0 - 8, ROW0 + ages, None))
    else:
        has = [jnp.where(at_end("age", i == 1), 0.0, 1.0).astype(f32) for i in range(2)]
        run(ROW0 - 8, ROW0 + ages + 8, [jnp.zeros((8, 128), f32) + h for h in has])


def inner_kernel(sides, z0, z1_in, z2_in, z3_in, speed_ref, o_ref, rest, z1, z2, z3, stage, out_sem):
    del z1_in, z2_in, z3_in
    halves, rows, _, _ = z0.shape
    done, ages = stage.shape[:2]
    fields = (z0, z1, z2, z3)

    def run(low, high, keeps):
        for k in range(1, SUBSTEPS):
            for l in range(halves):
                rows_step(
                    fields[k - 1], l, HALO + k, rows - HALO - k, low, high, lane_terms(speed_ref, l),
                    put_in(fields[k], l, low, high, keeps), 10,
                )
        stores = []
        first = HALO + SUBSTEPS
        bounds = [0, done * 3 // 5 // 8 * 8, done, done + rest.shape[0]]
        for a, b in zip(bounds, bounds[1:]):
            for l in range(halves):
                def put(w, out, l=l, a=a):
                    if a < done:
                        stage[w - first, :, l * 128 : (l + 1) * 128] = out
                    else:
                        rest[w - first - done, :, l * 128 : (l + 1) * 128] = out

                rows_step(
                    fields[-1], l, first + a, first + b, ROW0, ROW0 + ages, lane_terms(speed_ref, l), put, 8,
                )
            if a < done:
                copy = pltpu.make_async_copy(
                    stage.at[pl.ds(a, b - a)], o_ref.at[pl.ds(SUBSTEPS + a, b - a)], out_sem.at[len(stores)]
                )
                copy.start()
                stores.append(copy)
        for copy in stores:
            copy.wait()

    by_sides(sides, ages, run)


def inner_substeps(fields, speed, sides, wears, ages):
    z = fields[0]
    size = z.shape[0] * 128
    shape = (wears, ages, size)
    kept = 16
    return pl.pallas_call(
        functools.partial(inner_kernel, sides),
        out_shape=[jax.ShapeDtypeStruct(shape, f32), pltpu.VMEM((kept, ages, size), f32)] + [pltpu.VMEM(z.shape, f32)] * 3,
        in_specs=[VMEM] * 5,
        out_specs=[ANY] + [VMEM] * 4,
        scratch_shapes=[
            pltpu.VMEM((wears - 2 * SUBSTEPS - kept, ages, size), f32),
            pltpu.SemaphoreType.DMA((2,)),
        ],
        input_output_aliases={1: 2, 2: 3, 3: 4},
        compiler_params=params(8),
        cost_estimate=cost(10 * SUBSTEPS * wears * ages * size, 8 * wears * ages * size),
        name="inner_substeps",
    )(*[in_vmem(x) for x in fields], speed)


def outer_kernel(sides, o_in, z0_in, z1_in, z2_in, z3_in, rest, speed_ref, first_ref, second_ref, o_ref, z0, z1, z2, z3,
                 stage, out_sem):
    del o_in, z0_in, z1_in, z2_in, z3_in
    halves, rows, _, _ = z0.shape
    wears, ages = rows - 2 * HALO, stage.shape[2]
    fields = (z0, z1, z2, z3)
    odd = odd_age()
    count = rest.shape[0]
    stores = [pltpu.make_async_copy(rest, o_ref.at[pl.ds(wears - SUBSTEPS - count, count)], out_sem.at[2])]
    stores[0].start()
    has = [jnp.where(at_end("age", i == 1), 0.0, 1.0).astype(f32) for i in range(2)]
    near = [jnp.where(at_end("wear", i == 1), 0.0, 1.0).astype(f32) for i in range(2)]
    for l in range(halves):
        lanes = pl.ds(l * 128, 128)
        first, second = first_ref[:, lanes].astype(f32), second_ref[:, lanes].astype(f32)
        for e, at in enumerate((0, HALO + wears)):
            values = jnp.where(odd, *((second, first) if e == 0 else (first, second))) * near[e]
            z0[l, at : at + HALO, ROW0 : ROW0 + ages, :] = values[: HALO * ages].reshape(HALO, ages, 128)
            for s in range(sides):
                corner = values[HALO * (ages + s * HALO) : HALO * (ages + (s + 1) * HALO)]
                for i, column in ((0, ROW0 - HALO), (1, ROW0 + ages)):
                    if sides == 1 or s == i:
                        part = corner * has[i]
                        for w in range(HALO):
                            z0[l, at + w, column : column + HALO, :] = part[w * HALO : (w + 1) * HALO]

    def run(low, high, keeps):
        for k in range(1, SUBSTEPS):
            for l in range(halves):
                for e, start in enumerate((k, rows - HALO - k)):
                    beyond = (lambda w: w < HALO, lambda w: w >= HALO + wears)[e]
                    rows_step(
                        fields[k - 1], l, start, start + HALO, low, high, lane_terms(speed_ref, l),
                        put_in(fields[k], l, low, high, keeps, beyond, near[e]), HALO,
                    )
        for e, start in enumerate((HALO, rows - 2 * HALO)):
            for l in range(halves):
                def put(w, out, l=l, e=e, start=start):
                    stage[e, w - start, :, l * 128 : (l + 1) * 128] = out

                rows_step(fields[-1], l, start, start + HALO, ROW0, ROW0 + ages, lane_terms(speed_ref, l), put, 4)
            pltpu.make_async_copy(stage.at[e], o_ref.at[pl.ds(start - HALO, HALO)], out_sem.at[e]).start()

    by_sides(sides, ages, run)
    for e, start in enumerate((HALO, rows - 2 * HALO)):
        stores.append(pltpu.make_async_copy(stage.at[e], o_ref.at[pl.ds(start - HALO, HALO)], out_sem.at[e]))
    for copy in stores:
        copy.wait()


def outer_substeps(o, fields, rest, speed, first, second, sides):
    wears, ages, size = o.shape
    return pl.pallas_call(
        functools.partial(outer_kernel, sides),
        out_shape=[jax.ShapeDtypeStruct(o.shape, f32)] + [pltpu.VMEM(z.shape, f32) for z in fields],
        in_specs=[ANY] + [VMEM] * 8,
        out_specs=[ANY] + [VMEM] * 4,
        scratch_shapes=[pltpu.VMEM((2, HALO, ages, size), f32), pltpu.SemaphoreType.DMA((3,))],
        input_output_aliases={i: i for i in range(5)},
        compiler_params=params(8),
        cost_estimate=cost(20 * SUBSTEPS * 2 * HALO * ages * size, 2**20),
        name="outer_substeps",
    )(o, *[in_vmem(x) for x in (*fields, rest)], speed, in_vmem(first), in_vmem(second))[0]


def body(adjoint_value, load_diffusion, load_drift, wear_speed, hazard):
    wears, ages, size = adjoint_value.shape
    points = load_diffusion.shape[0]
    devices = points // size
    slots, send, take_second, take_first, own_second, own_first = factors(points, devices)
    ranks = tuple(rank for _, rank in slots)
    n_wear, n_age = lax.axis_size("wear"), lax.axis_size("age")
    sides = 1 if n_age == 2 else 2
    extra = sides * wears // 2 * HALO
    u4 = adjoint_value.reshape(2, wears // 2, ages, size)
    sides = 1 if n_age == 2 else 2
    extra = sides * wears // 2 * HALO
    u4 = adjoint_value.reshape(2, wears // 2, ages, size)
    diffusion = load_diffusion.reshape(devices, 1, size)
    drift = load_drift.reshape(devices, 1, size)
    tables = np.stack(
        [
            np.concatenate([own, take.reshape(devices, -1, size)], axis=1)
            for own, take in ((own_second, take_second), (own_first, take_first))
        ],
        axis=1,
    )
    diffusion = load_diffusion.reshape(devices, 1, size)
    drift = load_drift.reshape(devices, 1, size)

    def ring(n):
        after = [(i, (i + 1) % n) for i in range(n)]
        return after, [(j, i) for i, j in after]

    most = 2 * max(ranks) * (wears // 2 * ages) // size
    *edge, send = edges(adjoint_value, hazard, jnp.asarray(send, bf16), sides, max(wears * HALO + HAZARD_ROWS, -(-most // 16) * 16))
    near = [lax.ppermute(x, "age", pairs) for x, pairs in zip(edge, ring(n_age))]
    q = pack(u4, send, edge, ranks)
    moves = [list(pairs) for pairs, _ in slots]
    arrived = [lax.ppermute(x, "cheb", pairs) for x, pairs in zip(q, moves)]
    arrived[0], *q_edges = pack_edges(send, near, arrived[0], ranks, sides, extra)
    arrived_edges = [lax.ppermute(x, "cheb", pairs) for x, pairs in zip(q_edges, moves)]
    z, *later, beside, ends, take = local(u4, jnp.asarray(tables, f32), hazard, diffusion, drift, near, sides)
    messages = outer_rows(ends, beside, take, arrived, arrived_edges, ranks, sides, wears, ages)
    around = []
    for w in range(n_wear):
        for a in range(n_age):
            to = w + 1 if a % 2 == 0 else w - 1
            if 0 <= to < n_wear:
                around.append((w * n_age + a, to * n_age + a))
            elif n_age % 2 == 0:
                around.append((w * n_age + a, w * n_age + (a ^ 1)))
    turns = (around, [(j, i) for i, j in around])
    first, second = (lax.ppermute(x, ("wear", "age"), turn) for x, turn in zip(messages, turns))
    z = section(z, beside, take, arrived, arrived_edges, ranks, sides, wears, ages)
    speed = wear_speed.reshape(1, size)
    o, rest, *later = inner_substeps([z, *later], speed, sides, wears, ages)
    return outer_substeps(o, [z, *later], rest, speed, first, second, sides)


def solution(mesh):
    placed = (P("wear", "age", "cheb"), P(), P(), P("cheb"), P("wear", "age"))
    return jax.shard_map(
        body, mesh=mesh, in_specs=placed, out_specs=P("wear", "age", "cheb"), check_vma=False
    )
```
